32 devices in a mesh: dp: 8 (over z, y), patch: 4 (over x, core).
Axes of the slice: x: 2, y: 2, z: 4, core: 2. Of those that a mesh axis runs over, the one named last changes fastest.
Arguments:
- description_vocabulary_ids: int32 [128, 32], P('dp'), may hold values from 0 to 15359
- description_place_indicator: int32 [128, 32], P('dp'), may hold values from 0 to 1, as said below
- paired_description_ids: int32 [128], P('dp'), may hold values from 0 to 127, each once
- picture_patch_encodings: bfloat16 [128, 128, 1408], P('dp', 'patch'), may hold values from -6 to 6
- incoming_adjoint_signal: bfloat16 [128, 64, 768], P('dp'), may hold values from -6 to 6
- trainable_probe_vectors: bfloat16 [32, 768], replicated, may hold values from -6 to 6
- vocabulary_vector_lookup: bfloat16 [15360, 768], P('patch'), may hold values from -6 to 6
- placement_vector_lookup: bfloat16 [32, 768], replicated, may hold values from -3 to 3
- lexicon_layernorm_stretch: float32 [768], replicated, may hold values from 0.5 to 1.5
- lexicon_layernorm_shift: float32 [768], replicated, may hold values from -1.5 to 1.5
- inward_attn_triple_proj: bfloat16 [768, 2304], replicated, may hold values from -0.21875 to 0.21875
- inward_attn_result_proj: bfloat16 [768, 768], replicated, may hold values from -0.625 to 0.625
- inward_layernorm_stretch: float32 [768], replicated, may hold values from 0.5 to 1.5
- inward_layernorm_shift: float32 [768], replicated, may hold values from -1.5 to 1.5
- between_attn_question_proj: bfloat16 [768, 768], replicated, may hold values from -0.21875 to 0.21875
- between_attn_lookup_proj: bfloat16 [1408, 768], P('patch'), may hold values from -0.15625 to 0.15625
- between_attn_content_proj: bfloat16 [1408, 768], P('patch'), may hold values from -0.15625 to 0.15625
- between_attn_result_proj: bfloat16 [768, 768], replicated, may hold values from -0.875 to 0.875
- between_layernorm_stretch: float32 [768], replicated, may hold values from 0.5 to 1.5
- between_layernorm_shift: float32 [768], replicated, may hold values from -1.5 to 1.5
- probe_mlp_first_proj: bfloat16 [768, 3072], replicated, may hold values from -0.21875 to 0.21875
- probe_mlp_second_proj: bfloat16 [3072, 768], replicated, may hold values from -0.15625 to 0.15625
- probe_mlp_layernorm_stretch: float32 [768], replicated, may hold values from 0.5 to 1.5
- probe_mlp_layernorm_shift: float32 [768], replicated, may hold values from -1.5 to 1.5
- sentence_mlp_first_proj: bfloat16 [768, 3072], replicated, may hold values from -0.21875 to 0.21875
- sentence_mlp_second_proj: bfloat16 [3072, 768], replicated, may hold values from -0.15625 to 0.15625
- sentence_mlp_layernorm_stretch: float32 [768], replicated, may hold values from 0.5 to 1.5
- sentence_mlp_layernorm_shift: float32 [768], replicated, may hold values from -1.5 to 1.5
- picture_alignment_proj: bfloat16 [768, 256], replicated, may hold values from -0.21875 to 0.21875
- sentence_alignment_proj: bfloat16 [768, 256], replicated, may hold values from -0.21875 to 0.21875
- sharpness_unbounded: float32 [], replicated, may hold values from 0.03 to 0.08
Outputs:
- hidden_out: bfloat16 [128, 64, 768], P('dp')
- loss: float32 [128], P('dp')
- features_grad: float32 [128, 128, 1408], P('dp', 'patch')
- query_tokens_grad: float32 [32, 768], P(None, 'dp')
- word_table_grad: float32 [15360, 768], P('patch')
- position_grad: float32 [32, 768], P(None, 'dp')
- emb_gain_grad: float32 [768], P('dp')
- emb_bias_grad: float32 [768], P('dp')
- qkv_weight_grad: float32 [768, 2304], P('dp')
- out_weight_grad: float32 [768, 768], P('dp')
- self_gain_grad: float32 [768], P('dp')
- self_bias_grad: float32 [768], P('dp')
- cross_query_grad: float32 [768, 768], P('dp')
- cross_key_grad: float32 [1408, 768], P('patch')
- cross_value_grad: float32 [1408, 768], P('patch')
- cross_out_grad: float32 [768, 768], P('dp')
- cross_gain_grad: float32 [768], P('dp')
- cross_bias_grad: float32 [768], P('dp')
- query_up_grad: float32 [768, 3072], P('dp')
- query_down_grad: float32 [3072, 768], P('dp')
- query_gain_grad: float32 [768], P('dp')
- query_bias_grad: float32 [768], P('dp')
- text_up_grad: float32 [768, 3072], P('dp')
- text_down_grad: float32 [3072, 768], P('dp')
- text_gain_grad: float32 [768], P('dp')
- text_bias_grad: float32 [768], P('dp')
- image_proj_grad: float32 [768, 256], P('dp')
- text_proj_grad: float32 [768, 256], P('dp')
- sharpness_derivative: float32 [], replicated
The draws below stay inside these ranges and needn't reach their ends.
Inputs may be any that keep to these rules, and one draw needn't show every extreme that they name: `description_place_indicator`: each row is some ones followed by zeros, with 5 to 32 ones; some row has 32.
All inputs are finite; a program needn't handle non-finite values.
Results may differ from the reference program's by a relative error of at most 0.038.
Values may be sent and summed in bfloat16 or wider, within the bound.
No kernel may reach another device: no remote copies, remote signals or barrier semaphores. Data moves between devices by JAX's collectives and lax.ppermute only.
A program may use at most 256 MiB of HBM per device.

```python
import math
import jax
import jax.numpy as jnp
import numpy as np
from jax import lax

D = 768
HEADS = 12
FF = 3072
VIS = 1408
EMB = 256
QN = 32
VOCAB = 15360
CAP = 32
FEAT = 128
ITEMS = 128


def draw_description_place_indicator(key, part):
    key = jax.random.fold_in(key, 7)
    length_key, longest_key = jax.random.split(key)
    lengths = jax.random.randint(length_key, (ITEMS,), 5, CAP + 1)
    longest = jax.random.randint(longest_key, (), 0, ITEMS)
    lengths = jnp.where(jnp.arange(ITEMS) == longest, CAP, lengths)
    return (jnp.arange(CAP)[None, :] < lengths[:, None]).astype(jnp.int32)


def with_ends(array, rng, smallest, high):
    dims = array.shape
    place = [jax.random.randint(jax.random.fold_in(rng, axis), (), 0, dims[axis]) for axis in range(len(dims))]
    array = array.at[tuple(place)].set(smallest)
    longest = dims.index(max(dims))
    place[longest] = (place[longest] + 1) % dims[longest]
    return array.at[tuple(place)].set(high)


def shard_levels(own_key, dims, cuts, low, largest):
    def one(dim, parts):
        steps = jax.random.uniform(jax.random.fold_in(jax.random.fold_in(own_key, 6), dim), (parts,), jnp.float32, low / len(cuts), largest / len(cuts))
        return jnp.repeat(jnp.exp(steps), dims[dim] // parts).reshape((-1,) + (1,) * (len(dims) - dim - 1))

    loudness = one(*cuts[0])
    for cut in cuts[1:]:
        loudness = loudness * one(*cut)
    return loudness


def rank_table(count, slope):
    portions = [(1 << 20) // math.isqrt(grade ** slope) + 1 for grade in range(1, count + 1)]
    scale = 1 + sum(portions) // (1 << 30)
    return np.cumsum(np.array([max(1, weight // scale) for weight in portions]))


def skewed_ids(stream_key, extent, number_of, slope):
    listing = rank_table(number_of, slope)
    pick = jax.random.randint(jax.random.fold_in(stream_key, 1), extent, 0, int(listing[number_of - 1]))
    rank = jnp.searchsorted(jnp.asarray(listing, jnp.int32), pick, side="right")
    return jax.random.permutation(jax.random.fold_in(stream_key, 2), number_of)[rank].astype(jnp.int32)


def gaussian(own_key, extent, width, bound, pieces=(), dtype=jnp.bfloat16):
    factor_of = shard_levels(own_key, extent, pieces, -0.22, 0.18) if pieces else 1.0
    result = jax.random.normal(own_key, extent, jnp.float32) * width * factor_of
    return jnp.minimum(jnp.maximum(result, -bound), bound).astype(dtype)


def setup_inputs(seed: int = 0) -> dict:
    splits = jax.random.split(jax.random.key(seed), 32)
    return {
        "description_vocabulary_ids": with_ends(skewed_ids(splits[0], (ITEMS, CAP), VOCAB, 2), jax.random.fold_in(splits[0], 3), 0, VOCAB - 1).astype(jnp.int32),
        "description_place_indicator": draw_description_place_indicator(jax.random.fold_in(splits[31], 71), 0),
        "paired_description_ids": jax.random.permutation(splits[2], ITEMS).astype(jnp.int32),
        "picture_patch_encodings": gaussian(splits[3], (ITEMS, FEAT, VIS), 1.0, 6.0, ((0, 8), (1, 4))),
        "incoming_adjoint_signal": gaussian(splits[4], (ITEMS, QN + CAP, D), 1.0, 6.0, ((0, 8),)),
        "trainable_probe_vectors": gaussian(splits[5], (QN, D), 1.0, 6.0),
        "vocabulary_vector_lookup": gaussian(splits[6], (VOCAB, D), 1.0, 6.0, ((0, 4),)),
        "placement_vector_lookup": gaussian(splits[7], (CAP, D), 0.5, 3.0),
        "lexicon_layernorm_stretch": jnp.clip(1.0 + 0.1 * jax.random.normal(splits[8], (D,), jnp.float32), 0.5, 1.5),
        "lexicon_layernorm_shift": gaussian(splits[9], (D,), 0.3, 1.5, (), jnp.float32),
        "inward_attn_triple_proj": gaussian(splits[10], (D, 3 * D), D ** -0.5, 0.21875),
        "inward_attn_result_proj": gaussian(splits[11], (D, D), (D // 8) ** -0.5, 0.625),
        "inward_layernorm_stretch": jnp.clip(1.0 + 0.1 * jax.random.normal(splits[12], (D,), jnp.float32), 0.5, 1.5),
        "inward_layernorm_shift": gaussian(splits[13], (D,), 0.3, 1.5, (), jnp.float32),
        "between_attn_question_proj": gaussian(splits[14], (D, D), D ** -0.5, 0.21875),
        "between_attn_lookup_proj": gaussian(splits[15], (VIS, D), VIS ** -0.5, 0.15625, ((0, 4),)),
        "between_attn_content_proj": gaussian(splits[16], (VIS, D), VIS ** -0.5, 0.15625, ((0, 4),)),
        "between_attn_result_proj": gaussian(splits[17], (D, D), (D // 16) ** -0.5, 0.875),
        "between_layernorm_stretch": jnp.clip(1.0 + 0.1 * jax.random.normal(splits[18], (D,), jnp.float32), 0.5, 1.5),
        "between_layernorm_shift": gaussian(splits[19], (D,), 0.3, 1.5, (), jnp.float32),
        "probe_mlp_first_proj": gaussian(splits[20], (D, FF), D ** -0.5, 0.21875),
        "probe_mlp_second_proj": gaussian(splits[21], (FF, D), (FF // 2) ** -0.5, 0.15625),
        "probe_mlp_layernorm_stretch": jnp.clip(1.0 + 0.1 * jax.random.normal(splits[22], (D,), jnp.float32), 0.5, 1.5),
        "probe_mlp_layernorm_shift": gaussian(splits[23], (D,), 0.3, 1.5, (), jnp.float32),
        "sentence_mlp_first_proj": gaussian(splits[24], (D, FF), D ** -0.5, 0.21875),
        "sentence_mlp_second_proj": gaussian(splits[25], (FF, D), (FF // 2) ** -0.5, 0.15625),
        "sentence_mlp_layernorm_stretch": jnp.clip(1.0 + 0.1 * jax.random.normal(splits[26], (D,), jnp.float32), 0.5, 1.5),
        "sentence_mlp_layernorm_shift": gaussian(splits[27], (D,), 0.3, 1.5, (), jnp.float32),
        "picture_alignment_proj": gaussian(splits[28], (D, EMB), D ** -0.5, 0.21875),
        "sentence_alignment_proj": gaussian(splits[29], (D, EMB), D ** -0.5, 0.21875),
        "sharpness_unbounded": jnp.clip(jax.random.uniform(splits[30], (), jnp.float32, 0.03, 0.08), 0.03, 0.08),
    }


@jax.custom_vjp
def low(v):
    return lax.optimization_barrier(v.astype(jnp.bfloat16)).astype(jnp.float32)

@jax.custom_vjp
def low_back(v):
    return v

def low_keep(v):
    return (low(v), None)

def low_pass(kept, grad):
    return (grad,)

def back_keep(v):
    return (v, None)

def back_low(kept, grad):
    return (low(grad),)
low.defvjp(low_keep, low_pass)
low_back.defvjp(back_keep, back_low)

def rounded(argument_number):
    return low(low_back(argument_number))

def product(argument_number, weight):
    return jnp.einsum('...i,ij->...j', argument_number, weight, precision=lax.Precision.HIGHEST)

def layer_norm(values, gain, offset):
    centred = values - lax.optimization_barrier(jnp.mean(values, axis=-1, keepdims=True))
    spread = lax.optimization_barrier(jnp.mean(centred * centred, axis=-1, keepdims=True))
    return centred * lax.rsqrt(spread + 1e-06) * gain + offset

def unit_rows(values):
    return values * lax.rsqrt(lax.optimization_barrier(jnp.sum(values * values, axis=-1, keepdims=True)) + 1e-06)

def split_heads(values):
    return values.reshape(values.shape[0], values.shape[1], HEADS, values.shape[2] // HEADS)

def feed_forward(rows, up_weight, down_weight, gain, offset):
    inner = low_back(product(low(rows), up_weight))
    active = jax.nn.gelu(inner, approximate=False)
    outer = low_back(product(low(active), down_weight))
    return layer_norm(rows + outer, gain, offset)

def compute_layer_result(description_vocabulary_ids, description_place_indicator, paired_description_ids, picture_patch_encodings, trainable_probe_vectors, vocabulary_vector_lookup, placement_vector_lookup, lexicon_layernorm_stretch, lexicon_layernorm_shift, inward_attn_triple_proj, inward_attn_result_proj, inward_layernorm_stretch, inward_layernorm_shift, between_attn_question_proj, between_attn_lookup_proj, between_attn_content_proj, between_attn_result_proj, between_layernorm_stretch, between_layernorm_shift, probe_mlp_first_proj, probe_mlp_second_proj, probe_mlp_layernorm_stretch, probe_mlp_layernorm_shift, sentence_mlp_first_proj, sentence_mlp_second_proj, sentence_mlp_layernorm_stretch, sentence_mlp_layernorm_shift, picture_alignment_proj, sentence_alignment_proj, sharpness_unbounded):
    item_count = description_vocabulary_ids.shape[0]
    model_width = trainable_probe_vectors.shape[1]
    scaling = 1.0 / math.sqrt(model_width // HEADS)
    highest = lax.Precision.HIGHEST
    words = jnp.take(vocabulary_vector_lookup, description_vocabulary_ids, axis=0) + placement_vector_lookup[None]
    joined = jnp.concatenate([jnp.broadcast_to(trainable_probe_vectors[None], (item_count, QN, model_width)), words], axis=1)
    start = layer_norm(joined, lexicon_layernorm_stretch, lexicon_layernorm_shift)
    packed = rounded(product(low(start), inward_attn_triple_proj))
    queries = split_heads(packed[..., :model_width])
    keys = split_heads(packed[..., model_width:2 * model_width])
    values = split_heads(packed[..., 2 * model_width:])
    scores = low_back(jnp.einsum('nqhd,nkhd->nhqk', queries, keys, precision=highest) * scaling)
    valid = jnp.concatenate([jnp.ones((item_count, QN), jnp.int32), description_place_indicator], axis=1) > 0
    weights = jax.nn.softmax(jnp.where(valid[:, None, None, :], scores, -1e+30), axis=-1)
    mixed = jnp.einsum('nhqk,nkhd->nqhd', low(weights), values, precision=highest)
    mixed = rounded(mixed.reshape(item_count, QN + CAP, model_width))
    first = layer_norm(start + low_back(product(mixed, inward_attn_result_proj)), inward_layernorm_stretch, inward_layernorm_shift)
    query_rows = first[:, :QN]
    text_rows = first[:, QN:]
    cross_q = split_heads(rounded(product(low(query_rows), between_attn_question_proj)))
    cross_k = split_heads(rounded(product(picture_patch_encodings, between_attn_lookup_proj)))
    cross_v = split_heads(rounded(product(picture_patch_encodings, between_attn_content_proj)))
    cross_scores = low_back(jnp.einsum('nqhd,nkhd->nhqk', cross_q, cross_k, precision=highest) * scaling)
    cross_weights = jax.nn.softmax(cross_scores, axis=-1)
    cross_mixed = jnp.einsum('nhqk,nkhd->nqhd', cross_weights, cross_v, precision=highest)
    cross_mixed = rounded(cross_mixed.reshape(item_count, QN, model_width))
    second = layer_norm(query_rows + low_back(product(cross_mixed, between_attn_result_proj)), between_layernorm_stretch, between_layernorm_shift)
    query_final = feed_forward(second, probe_mlp_first_proj, probe_mlp_second_proj, probe_mlp_layernorm_stretch, probe_mlp_layernorm_shift)
    text_final = feed_forward(text_rows, sentence_mlp_first_proj, sentence_mlp_second_proj, sentence_mlp_layernorm_stretch, sentence_mlp_layernorm_shift)
    image_raw = low_back(product(low(query_final), picture_alignment_proj))
    image_embed = unit_rows(lax.optimization_barrier(jnp.mean(image_raw, axis=1)))
    text_embed = unit_rows(low_back(product(low(text_final[:, 0]), sentence_alignment_proj)))
    multiplier_coefficient = 1.0 / jnp.clip(sharpness_unbounded, 0.04, 0.5)
    logits = jnp.dot(image_embed, text_embed.T, precision=highest) * multiplier_coefficient
    matches = lax.broadcasted_iota(jnp.int32, logits.shape, 1) == paired_description_ids[:, None]
    row_part = jax.nn.logsumexp(logits, axis=1)
    column_part = jax.nn.logsumexp(logits, axis=0)
    item_losses = 0.5 * (row_part + column_part) - lax.optimization_barrier(jnp.sum(jnp.where(matches, logits, 0.0), axis=1))
    hidden = jnp.concatenate([query_final, text_final], axis=1)
    return (hidden, item_losses)

def reference(description_vocabulary_ids, description_place_indicator, paired_description_ids, picture_patch_encodings, incoming_adjoint_signal, trainable_probe_vectors, vocabulary_vector_lookup, placement_vector_lookup, lexicon_layernorm_stretch, lexicon_layernorm_shift, inward_attn_triple_proj, inward_attn_result_proj, inward_layernorm_stretch, inward_layernorm_shift, between_attn_question_proj, between_attn_lookup_proj, between_attn_content_proj, between_attn_result_proj, between_layernorm_stretch, between_layernorm_shift, probe_mlp_first_proj, probe_mlp_second_proj, probe_mlp_layernorm_stretch, probe_mlp_layernorm_shift, sentence_mlp_first_proj, sentence_mlp_second_proj, sentence_mlp_layernorm_stretch, sentence_mlp_layernorm_shift, picture_alignment_proj, sentence_alignment_proj, sharpness_unbounded):
    real_numbers = [argument_number.astype(jnp.float32) for argument_number in (picture_patch_encodings, trainable_probe_vectors, vocabulary_vector_lookup, placement_vector_lookup, lexicon_layernorm_stretch, lexicon_layernorm_shift, inward_attn_triple_proj, inward_attn_result_proj, inward_layernorm_stretch, inward_layernorm_shift, between_attn_question_proj, between_attn_lookup_proj, between_attn_content_proj, between_attn_result_proj, between_layernorm_stretch, between_layernorm_shift, probe_mlp_first_proj, probe_mlp_second_proj, probe_mlp_layernorm_stretch, probe_mlp_layernorm_shift, sentence_mlp_first_proj, sentence_mlp_second_proj, sentence_mlp_layernorm_stretch, sentence_mlp_layernorm_shift, picture_alignment_proj, sentence_alignment_proj, sharpness_unbounded)]

    def objective(*inputs):
        return compute_layer_result(description_vocabulary_ids, description_place_indicator, paired_description_ids, *inputs)
    (hidden, item_losses), pullback = jax.vjp(objective, *real_numbers)
    gradients = pullback((incoming_adjoint_signal.astype(jnp.float32), jnp.ones(item_losses.shape, jnp.float32)))
    return (hidden.astype(jnp.bfloat16), item_losses, gradients[0], gradients[1], gradients[2], gradients[3], gradients[4], gradients[5], gradients[6], gradients[7], gradients[8], gradients[9], gradients[10], gradients[11], gradients[12], gradients[13], gradients[14], gradients[15], gradients[16], gradients[17], gradients[18], gradients[19], gradients[20], gradients[21], gradients[22], gradients[23], gradients[24], gradients[25], gradients[26])
```

```python
import functools
import math

import jax
import jax.numpy as jnp
from jax import lax
from jax.experimental import pallas as pl
from jax.experimental.pallas import tpu as pltpu
from jax.sharding import Mesh, PartitionSpec as P

HEADS = 12
GROUP = 4
SLOTS = 128
CORES = 2
BF = jnp.bfloat16
F32 = jnp.float32
HIGHEST = lax.Precision.HIGHEST
VMEM_BYTES = 60 * 1024 * 1024
VMEM_SPARE = 10 * 1024 * 1024
SLAB = 32
DP, SHARE, PARTNER, CORE, MEMBER, OTHER = range(6)


def nn(a, b):
    return lax.dot_general(a, b, (((1,), (0,)), ((), ())), preferred_element_type=F32)


def nt(a, b):
    return lax.dot_general(a, b, (((1,), (1,)), ((), ())), preferred_element_type=F32)


def tn(a, b):
    return lax.dot_general(a, b, (((0,), (0,)), ((), ())), preferred_element_type=F32)


def exact(a, b, dims):
    return lax.dot_general(a, b, ((dims[0], dims[1]), ((), ())), precision=HIGHEST)


def normalise(values):
    centred = values - jnp.mean(values, axis=-1, keepdims=True)
    spread = jnp.mean(centred * centred, axis=-1, keepdims=True)
    scale = lax.rsqrt(spread + 1e-06)
    return centred * scale, scale


def slabs(rows):
    step = math.gcd(rows, SLAB)
    return [slice(r, r + step) for r in range(0, rows, step)]


def fold(values):
    return jnp.sum(values.reshape(-1, 8, values.shape[-1]), axis=0)


def norm_back(grad, normal, scale, gain):
    inner = grad * gain
    first = jnp.mean(inner, axis=-1, keepdims=True)
    second = jnp.mean(inner * normal, axis=-1, keepdims=True)
    return scale * (inner - first - normal * second), fold(grad * normal), fold(grad)


def norm_back_rows(grad_of, normal, scale, gain, put):
    gains = biases = None
    for at in slabs(normal.shape[0]):
        grad_in, part_gain, part_bias = norm_back(grad_of(at), normal[at], scale[at], gain[...])
        put(at, grad_in)
        gains = part_gain if gains is None else gains + part_gain
        biases = part_bias if biases is None else biases + part_bias
    return jnp.sum(gains, axis=0, keepdims=True), jnp.sum(biases, axis=0, keepdims=True)


def gelu_both(values):
    size = jnp.abs(values)
    t = 1.0 / (1.0 + (0.3275911 * math.sqrt(0.5)) * size)
    bell = jnp.exp(-0.5 * values * values)
    poly = t * (
        0.254829592
        + t * (-0.284496736 + t * (1.421413741 + t * (-1.453152027 + t * 1.061405429)))
    )
    tail = 0.5 * poly * bell
    cdf = jnp.where(values < 0, tail, 1.0 - tail)
    return values * cdf, cdf + values * bell * (1.0 / math.sqrt(2.0 * math.pi))


def order_weights(z_size, y_size, order):
    y_weights = [1 << k for k in range(y_size.bit_length() - 1)]
    z_weights = [y_size << k for k in range(z_size.bit_length() - 1)]
    return y_weights + z_weights if order == "y" else z_weights + y_weights


def relative_of(position, weights):
    last = len(weights) - 1
    return sum(w for k, w in enumerate(weights) if (position >> (last - k)) & 1)


def position_of(relative, weights):
    last = len(weights) - 1
    place = jnp.int32(0)
    for k, w in enumerate(weights):
        place = place + jnp.where((relative & w) != 0, 1 << (last - k), 0)
    return place


def choose_rows(info, share, weights, rows, size, width):
    blocks = []
    row = lax.broadcasted_iota(jnp.int32, (rows, width), 0)
    column = lax.broadcasted_iota(jnp.int32, (rows, width), 1)
    for position in range(1 << len(weights)):
        block = info[DP] ^ relative_of(position, weights)
        start = block * size + info[share] * rows
        blocks.append(jnp.where(column == row + start, 1.0, 0.0))
    return jnp.concatenate(blocks, axis=0).astype(BF)


def head_masks(lanes, head):
    lane = lax.broadcasted_iota(jnp.int32, (1, lanes), 1)
    return [(lane >= h * head) & (lane < (h + 1) * head) for h in range(lanes // head)]


def stack_heads(values, masks):
    zero = jnp.zeros_like(values)
    return jnp.concatenate([jnp.where(m, values, zero) for m in masks], axis=0)


def merge_heads(stacked, masks):
    rows = stacked.shape[0] // len(masks)
    total = None
    for h, m in enumerate(masks):
        piece = jnp.where(m, stacked[h * rows : (h + 1) * rows], 0.0)
        total = piece if total is None else total + piece
    return total


def softmax_into(out, scores, tile, scaling, closed=None):
    for r in range(0, scores.shape[0], tile):
        part = scores[r : r + tile] * scaling
        if closed is not None:
            part = part + closed
        top = jnp.max(part, axis=-1, keepdims=True)
        powers = jnp.exp(part - top)
        out[r : r + tile] = (powers / jnp.sum(powers, axis=-1, keepdims=True)).astype(BF)


def softmax_back(probs, grads, tile):
    parts = []
    for r in range(0, grads.shape[0], tile):
        p, dp = probs[r : r + tile].astype(F32), grads[r : r + tile]
        parts.append((p * (dp - jnp.sum(p * dp, axis=-1, keepdims=True))).astype(BF))
    return jnp.concatenate(parts, axis=0)


def whole(shape):
    zeros = (0,) * len(shape)
    return pl.BlockSpec(tuple(shape), lambda *_: zeros)


SCALARS = pl.BlockSpec(memory_space=pltpu.SMEM)


class Row:
    def __init__(self, stack, k):
        self.stack, self.k = stack, k
        self.size, self.dtype = stack.shape[2], stack.dtype

    def spec(self):
        return whole(self.stack.shape)


def call(kernel, ins, outs, *, grid=(), in_specs=None, out_specs=None, scratch=(), flops=0, name, after=()):
    if in_specs is None:
        in_specs = [None] * len(ins)
    in_specs = [
        spec or (SCALARS if k == 0 else v.spec() if isinstance(v, Row) else whole(v.shape))
        for k, (spec, v) in enumerate(zip(in_specs, ins))
    ]
    out_shape = [jax.ShapeDtypeStruct(shape, dtype) for shape, dtype in outs]
    if out_specs is None:
        out_specs = [None] * len(outs)
    out_specs = [spec or whole(o.shape) for spec, o in zip(out_specs, out_shape)]
    moved = sum(v.size * v.dtype.itemsize for v in list(ins) + out_shape)
    limit = VMEM_BYTES
    if not grid:
        held = sum(math.prod(v.shape) * jnp.dtype(v.dtype).itemsize for v in scratch)
        limit = min(VMEM_BYTES, moved + held + VMEM_SPARE)
    count = len(ins)
    rows = [v.k if isinstance(v, Row) else None for v in ins]
    ins = [v.stack if isinstance(v, Row) else v for v in ins]

    def body(*refs):
        given = [ref if k is None else ref.at[k] for ref, k in zip(refs, rows)]
        kernel(*given, *refs[count + len(after) :])

    return pl.pallas_call(
        body,
        grid=grid,
        in_specs=in_specs + [pl.BlockSpec(memory_space=pl.ANY)] * len(after),
        out_specs=out_specs,
        out_shape=out_shape,
        scratch_shapes=list(scratch),
        compiler_params=pltpu.CompilerParams(vmem_limit_bytes=limit),
        cost_estimate=pl.CostEstimate(
            flops=1, bytes_accessed=1, transcendentals=0
        ),
        name=name,
    )(*ins, *after)


def words_kernel(info, ids, table, mine, give, total):
    step = pl.program_id(0)
    chunk = table.shape[0]

    @pl.when(step == 0)
    def _():
        total[...] = jnp.zeros_like(total)

    column = lax.broadcasted_iota(jnp.int32, (ids.shape[0], chunk), 1) + step * chunk
    hot = jnp.where(ids[...] == column, 1.0, 0.0).astype(BF)
    total[...] += nn(hot, table[...])

    @pl.when(step == pl.num_programs(0) - 1)
    def _():
        half = total.shape[0] // 2
        mine[...] = total[:half].astype(BF)
        give[...] = total[half:].astype(BF)


def look_up(info, ids, table, chunk=640):
    rows, width = table.shape
    count = ids.shape[0]
    return call(
        words_kernel,
        [info, ids, table],
        [((count // 2, width), BF)] * 2,
        grid=(rows // chunk,),
        in_specs=[None, None, pl.BlockSpec((chunk, width), lambda k: (k, 0))],
        scratch=[pltpu.VMEM((count, width), F32)],
        flops=2 * count * rows * width,
        name="words",
    )


def embed_slab(words, positions, at):
    slots, width = positions.shape
    total = words[0][at].astype(F32)
    for other in words[1:]:
        total = total + other[at].astype(F32)
    start = at.start % slots
    if start + total.shape[0] <= slots:
        return total + positions[start : start + total.shape[0]].astype(F32)
    return (total.reshape(-1, slots, width) + positions[...].astype(F32)[None]).reshape(-1, width)


def self_forward_kernel(
    x_size, weights, share_rows, info, positions, query_tokens, emb_gain, emb_bias, qkv,
    used, out_weight, gain, bias, cross_weight, *rest,
):
    words = rest[:x_size]
    (
        packed, probs, normal_q, normal_t, scale_q, scale_t, cross_q, keep, give, chosen_q, mixed,
        start_rows, query_rows, attended,
    ) = rest[x_size:]
    slots, width = positions.shape
    queries = query_tokens.shape[0]
    rows = queries + slots
    head = width // HEADS
    lanes = GROUP * head
    start_q = normalise(query_tokens[...].astype(F32))[0] * emb_gain[...] + emb_bias[...]
    count = words[0].shape[0]
    items = count // slots
    for at in slabs(count):
        normal, _ = normalise(embed_slab(words, positions, at))
        start_rows[at] = normal * emb_gain[...] + emb_bias[...]
    start_q_low, start_w_low = start_q.astype(BF), start_rows[...].astype(BF)
    both = jnp.concatenate([start_q_low, start_w_low], axis=0)
    for c in range(3):
        span = slice(c * width, (c + 1) * width)
        product = nn(both, qkv[:, span]).astype(BF)
        for i in range(items):
            packed[i * rows : i * rows + queries, span] = product[:queries]
            packed[i * rows + queries : (i + 1) * rows, span] = product[
                queries + i * slots : queries + (i + 1) * slots
            ]
    masks = head_masks(lanes, head)
    pair = 2 * rows
    row_item = lax.broadcasted_iota(jnp.int32, (pair, pair), 0) // rows
    column_item = lax.broadcasted_iota(jnp.int32, (pair, pair), 1) // rows
    for j in range(items // 2):
        closed = jnp.where((row_item == column_item) & (used[j : j + 1] > 0), 0.0, -1e30)
        at = slice(j * pair, (j + 1) * pair)
        for g in range(HEADS // GROUP):
            base = g * lanes
            q = stack_heads(packed[at, base : base + lanes], masks)
            k = packed[at, width + base : width + base + lanes]
            v = packed[at, 2 * width + base : 2 * width + base + lanes]
            p = probs.at[j * (HEADS // GROUP) + g]
            softmax_into(p, nt(q, k), pair, 1.0 / math.sqrt(head), closed)
            mixed[at, base : base + lanes] = merge_heads(nn(p[...], v), masks).astype(BF)
    attended[...] = nn(mixed[...], out_weight[...])
    for i in range(items):
        base = i * rows
        for at in slabs(queries):
            into = slice(i * queries + at.start, i * queries + at.stop)
            normal, scale = normalise(attended[base + at.start : base + at.stop] + start_q[at])
            normal_q[into] = normal
            scale_q[into] = scale
            query_rows[into] = (normal * gain[...] + bias[...]).astype(BF)
        for at in slabs(slots):
            into = slice(i * slots + at.start, i * slots + at.stop)
            start = base + queries + at.start
            normal, scale = normalise(
                attended[start : start + at.stop - at.start] + start_rows[into]
            )
            normal_t[into] = normal
            scale_t[into] = scale
    query_low = query_rows[...]
    cross_q[...] = nn(query_low, cross_weight[...]).astype(BF)
    size = width >> len(weights)
    for share, out in ((SHARE, keep), (PARTNER, give)):
        select = choose_rows(info, share, weights, share_rows, size, width)
        out[:, : items * slots] = nt(select, start_w_low).astype(BF)
        out[:, items * slots : items * (slots + rows)] = nt(select, mixed[...]).astype(BF)
        if share == SHARE:
            chosen_q[...] = nt(select, start_q_low).astype(BF)
        out[:, items * (slots + rows) :] = nt(select, query_low).astype(BF)


def self_forward(info, words, used, p, orders, share_rows):
    slots, width = p["positions"].shape
    queries = p["query_tokens"].shape[0]
    items = words[0].shape[0] // slots
    rows = queries + slots
    blocks = 1 << len(orders["y"])
    units = (items // 2) * (HEADS // GROUP)
    ins = [
        info, p["positions"], p["query_tokens"], p["emb_gain"], p["emb_bias"], p["qkv"], used,
        p["out"], p["self_gain"], p["self_bias"], p["cross_query"], *words,
    ]
    lhs = (blocks * share_rows, items * (slots + rows + queries))
    outs = [
        ((items * rows, 3 * width), BF),
        ((units, GROUP * 2 * rows, 2 * rows), BF),
        ((items * queries, width), F32),
        ((items * slots, width), F32),
        ((items * queries, 1), F32),
        ((items * slots, 1), F32),
        ((items * queries, width), BF),
        (lhs, BF),
        (lhs, BF),
        ((blocks * share_rows, queries), BF),
    ]
    return call(
        functools.partial(self_forward_kernel, len(words), orders["y"], share_rows),
        ins,
        outs,
        scratch=[
            pltpu.VMEM((items * rows, width), BF),
            pltpu.VMEM((items * slots, width), F32),
            pltpu.VMEM((items * queries, width), BF),
            pltpu.VMEM((items * rows, width), F32),
        ],
        flops=2 * items * rows * width * width * 6,
        name="self_forward",
    )


def fill_weights(places, shards, key_full, value_full):
    half = len(shards) // 2
    size = shards[0].shape[0]
    for k in range(half):
        at = pl.ds(pl.multiple_of(places[k] * size, 16), size)
        key_full[at, :] = shards[k][...]
        value_full[at, :] = shards[half + k][...]


def key_value_kernel(pieces, info, places, *rest):
    feats, shards = rest[:pieces], rest[pieces : 3 * pieces]
    keys, values, key_full, value_full = rest[3 * pieces :]
    fill_weights(places, shards, key_full, value_full)
    items, rows, width = feats[0].shape
    for k, piece in enumerate(feats):
        flat = piece[...].reshape(items * rows, width)
        at = slice(k * rows, (k + 1) * rows)
        keys[:, at] = nn(flat, key_full[...]).astype(BF).reshape(items, rows, -1)
        values[:, at] = nn(flat, value_full[...]).astype(BF).reshape(items, rows, -1)


def key_value(info, places, feats, shards):
    items, rows, deep = feats[0].shape
    width = shards[0].shape[1]
    pieces = len(feats)
    return call(
        functools.partial(key_value_kernel, pieces),
        [info, places, *feats, *shards],
        [((items, pieces * rows, width), BF)] * 2,
        in_specs=[SCALARS, SCALARS] + [None] * (3 * pieces),
        scratch=[pltpu.VMEM((deep, width), BF)] * 2,
        flops=4 * items * rows * pieces * deep * width,
        name="key_value",
    )


def cross_forward_kernel(
    weights, share_rows, info, cross_q, keys, values, normal_q, self_gain, self_bias,
    out_weight, probs, normal, scale, keep, give, mixed, added,
):
    items, _, width = keys.shape
    queries = cross_q.shape[0] // items
    head = width // HEADS
    lanes = GROUP * head
    masks = head_masks(lanes, head)
    groups = HEADS // GROUP
    for i in range(items):
        at = slice(i * queries, (i + 1) * queries)
        for g in range(groups):
            span = slice(g * lanes, (g + 1) * lanes)
            q = stack_heads(cross_q[at, span], masks)
            p = probs.at[i * groups + g]
            softmax_into(p, nt(q, keys[i, :, span]), 2 * queries, 1.0 / math.sqrt(head))
            mixed[at, span] = merge_heads(nn(p[...], values[i, :, span]), masks).astype(BF)
    added[...] = nn(mixed[...], out_weight[...])
    for at in slabs(added.shape[0]):
        n, s = normalise(added[at] + (normal_q[at] * self_gain[...] + self_bias[...]))
        normal[at] = n
        scale[at] = s
    for share, out in ((SHARE, keep), (PARTNER, give)):
        select = choose_rows(info, share, weights, share_rows, width >> len(weights), width)
        out[...] = nt(select, mixed[...]).astype(BF)


def cross_forward(info, cross_q, keys, values, normal_q, p, orders, share_rows):
    items, all_rows, width = keys.shape
    count = cross_q.shape[0]
    blocks = 1 << len(orders["z"])
    ins = [
        info, cross_q, keys, values, normal_q, p["self_gain"], p["self_bias"], p["cross_out"],
    ]
    outs = [
        ((items * HEADS // GROUP, GROUP * count // items, all_rows), BF),
        ((count, width), F32),
        ((count, 1), F32),
        ((blocks * share_rows, count), BF),
        ((blocks * share_rows, count), BF),
    ]
    return call(
        functools.partial(cross_forward_kernel, orders["y"], share_rows),
        ins,
        outs,
        scratch=[pltpu.VMEM((count, width), BF), pltpu.VMEM((count, width), F32)],
        flops=2 * count * width * width + 4 * count * all_rows * width,
        name="cross_forward",
    )


def ff_forward_kernel(
    weights, share_rows, averaged, info, normal_in, gain_in, bias_in, up, down, gain, bias, proj,
    slope, keep, give, normal, scale, final, raw, rows_low, total, inner, active_low,
):
    step = pl.program_id(0)
    blocks = 1 << len(weights)
    count, width = normal_in.shape
    chunk = up.shape[1]
    deep = 4 * share_rows
    size = 4 * width // blocks

    @pl.when(step == 0)
    def _():
        for at in slabs(count):
            rows = normal_in[at] * gain_in[...] + bias_in[...]
            rows_low[at] = rows.astype(BF)
            total[at] = rows
        for share, out in ((SHARE, keep), (PARTNER, give)):
            select = choose_rows(info, share, weights, share_rows, width // blocks, width)
            out[: blocks * share_rows] = nt(select, rows_low[...]).astype(BF)

    inner[...] = nn(rows_low[...], up[...])
    for at in slabs(count):
        for c in range(0, chunk, 256):
            value, slant = gelu_both(inner[at, c : c + 256])
            active_low[at, c : c + 256] = value.astype(BF)
            slope[at, c : c + 256] = slant.astype(BF)
    active = active_low[...]
    total[...] += nn(active, down[...])
    each = chunk // size
    row = lax.broadcasted_iota(jnp.int32, (deep, chunk), 0)
    column = lax.broadcasted_iota(jnp.int32, (deep, chunk), 1)
    for share, out in ((SHARE, keep), (PARTNER, give)):
        select = [
            jnp.where(column == row + (j * size + info[share] * deep), 1.0, 0.0)
            for j in range(each)
        ]
        picked = nt(jnp.concatenate(select, axis=0).astype(BF), active).astype(BF)
        for j in range(each):
            block = step * each + j
            place = position_of(block ^ info[DP], weights)
            at = pl.multiple_of(blocks * share_rows + place * deep, 16)
            out[pl.ds(at, deep), :] = picked[j * deep : (j + 1) * deep]

    @pl.when(step == pl.num_programs(0) - 1)
    def _():
        for at in slabs(count):
            n, s = normalise(total[at])
            normal[at] = n
            scale[at] = s
            final[at] = (n * gain[...] + bias[...]).astype(BF)
        low = final[...]
        items = raw.shape[0]
        if averaged:
            image = nn(low, proj[...]).reshape(items, count // items, -1)
            raw[...] = jnp.mean(image, axis=1)
        else:
            heads = jnp.concatenate(
                [low[i * (count // items) : i * (count // items) + 16] for i in range(items)], axis=0
            )
            text = nn(heads, proj[...]).reshape(items, 16, -1)
            raw[...] = text[:, 0]


def ff_forward(info, normal_in, gain_in, bias_in, names, p, weights, share_rows, items, averaged):
    up, down, gain, bias, proj = (p[k] for k in names)
    count, width = normal_in.shape
    inner = up.shape[1]
    chunk = width
    blocks = 1 << len(weights)
    lhs = (blocks * share_rows * 5, count)
    return call(
        functools.partial(ff_forward_kernel, weights, share_rows, averaged),
        [info, normal_in, gain_in, bias_in, up, down, gain, bias, proj],
        [
            ((count, inner), BF),
            (lhs, BF),
            (lhs, BF),
            ((count, width), F32),
            ((count, 1), F32),
            ((count, width), BF),
            ((items, proj.shape[1]), F32),
        ],
        grid=(inner // chunk,),
        in_specs=[None] * 4
        + [
            pl.BlockSpec((width, chunk), lambda k: (0, k)),
            pl.BlockSpec((chunk, width), lambda k: (k, 0)),
        ]
        + [None] * 3,
        out_specs=[pl.BlockSpec((count, chunk), lambda k: (0, k))] + [None] * 6,
        scratch=[
            pltpu.VMEM((count, width), BF),
            pltpu.VMEM((count, width), F32),
            pltpu.VMEM((count, chunk), F32),
            pltpu.VMEM((count, chunk), BF),
        ],
        flops=4 * count * width * inner,
        name="ff_forward",
    )


def ff_backward_kernel(
    averaged, info, incoming, extra, proj, normal, scale, gain, slope, up, down,
    rhs, grad_rows, vectors, added, outer, total,
):
    step = pl.program_id(0)
    count, width = normal.shape
    chunk = slope.shape[1]

    @pl.when(step == 0)
    def _():
        items = extra.shape[0] // 2
        each = count // items
        added[...] = nt(extra[...], proj[...])

        def grad_of(at):
            grad = incoming[at.start // each, at.start % each : at.start % each + SLAB].astype(F32)
            more = added[at.start // each : at.start // each + 1]
            if averaged:
                return grad + more
            row = lax.broadcasted_iota(jnp.int32, (SLAB, 1), 0) + at.start % each
            return grad + jnp.where(row == 0, more, 0.0)

        def put(at, grad_in):
            total[at] = grad_in
            outer[at] = grad_in.astype(BF)
            rhs[at, pl.num_programs(0) * chunk :] = grad_in.astype(BF)

        grads = norm_back_rows(grad_of, normal, scale, gain, put)
        vectors[...] = jnp.concatenate(grads, axis=0)

    inner = (nt(outer[...], down[...]) * slope[...].astype(F32)).astype(BF)
    rhs[:, pl.ds(pl.multiple_of(step * chunk, 128), chunk)] = inner
    total[...] += nt(inner, up[...])

    @pl.when(step == pl.num_programs(0) - 1)
    def _():
        grad_rows[...] = total[...]


def ff_backward(info, incoming, part_of, extra, state, names, p, averaged, after=()):
    up, down, gain, proj = (p[k] for k in names)
    slope, normal, scale = state
    count, width = normal.shape
    items = extra.shape[0] // 2
    inner = up.shape[1]
    chunk = width
    each = count // items
    gs = pltpu.PrefetchScalarGridSpec(
        num_scalar_prefetch=1,
        grid=(inner // chunk,),
        in_specs=[
            pl.BlockSpec((items, each, width), lambda k, info: (info[CORE], part_of, 0)),
            whole(extra.shape),
            whole(proj.shape),
            whole(normal.shape),
            whole(scale.shape),
            gain.spec(),
            pl.BlockSpec((count, chunk), lambda k, info: (0, k)),
            pl.BlockSpec((width, chunk), lambda k, info: (0, k)),
            pl.BlockSpec((chunk, width), lambda k, info: (k, 0)),
        ]
        + [pl.BlockSpec(memory_space=pl.ANY)] * len(after),
        out_specs=[whole((count, inner + width)), whole((count, width)), whole((2, width))],
        scratch_shapes=[
            pltpu.VMEM((2 * items, width), F32),
            pltpu.VMEM((count, width), BF),
            pltpu.VMEM((count, width), F32),
        ],
    )

    def body(*refs):
        given = [ref.at[gain.k] if k == 6 else ref for k, ref in enumerate(refs[:10])]
        ff_backward_kernel(averaged, *given, *refs[10 + len(after) :])

    return pl.pallas_call(
        body,
        grid_spec=gs,
        out_shape=[
            jax.ShapeDtypeStruct((count, inner + width), BF),
            jax.ShapeDtypeStruct((count, width), F32),
            jax.ShapeDtypeStruct((2, width), F32),
        ],
        compiler_params=pltpu.CompilerParams(vmem_limit_bytes=VMEM_BYTES),
        cost_estimate=pl.CostEstimate(
            flops=1, bytes_accessed=1, transcendentals=0
        ),
        name="ff_backward",
    )(info, incoming, extra, proj, normal, scale, gain.stack, slope, up, down, *after)


def ff_weights_kernel(share_rows, blocks, info, lhs_a, lhs_b, rhs_a, rhs_b, keep, give, total):
    width = keep.shape[2]
    inner = rhs_a.shape[1] - width
    first = blocks * share_rows
    for c in range(inner // width):
        span = slice(c * width, (c + 1) * width)
        part = nn(lhs_a[:first], rhs_a[:, span]) + nn(lhs_b[:first], rhs_b[:, span])
        for b in range(blocks):
            total[b, c * share_rows : (c + 1) * share_rows] = part[
                b * share_rows : (b + 1) * share_rows
            ]
    deep = 4 * share_rows
    down = nn(lhs_a[first:], rhs_a[:, inner:]) + nn(lhs_b[first:], rhs_b[:, inner:])
    for b in range(blocks):
        out, at = (keep, b) if b < blocks // 2 else (give, b - blocks // 2)
        out[at, :deep] = total[b].astype(BF)
        out[at, deep:] = down[b * deep : (b + 1) * deep].astype(BF)


def ff_weights(info, lhs_a, lhs_b, rhs_a, rhs_b, share_rows, blocks, width, after):
    deep = 4 * share_rows
    out = ((blocks // 2, 2 * deep, width), BF)
    return call(
        functools.partial(ff_weights_kernel, share_rows, blocks),
        [info, lhs_a, lhs_b, rhs_a, rhs_b],
        [out, out],
        scratch=[pltpu.VMEM((blocks, deep, width), F32)],
        flops=4 * lhs_a.size * 4 * width,
        name="ff_weights",
        after=after,
    )


def log_sum(values, axis):
    top = jnp.max(values, axis=axis, keepdims=True)
    return top + jnp.log(jnp.sum(jnp.exp(values - top), axis=axis, keepdims=True))


def contrast_kernel(
    queries, info, gathered, pairs, pairs_row, sharpness, loss, grad_image, grad_text, grad_sharp,
    all_loss, all_image, all_text,
):
    count = gathered.shape[0]
    emb = grad_image.shape[1]
    image_raw, text_raw = gathered[:, :emb], gathered[:, emb:]
    image_scale = lax.rsqrt(jnp.sum(image_raw * image_raw, axis=1, keepdims=True) + 1e-06)
    text_scale = lax.rsqrt(jnp.sum(text_raw * text_raw, axis=1, keepdims=True) + 1e-06)
    image, text = image_raw * image_scale, text_raw * text_scale
    sharp = sharpness[...]
    factor = 1.0 / jnp.clip(sharp, 0.04, 0.5)
    inside = jnp.where((sharp >= 0.04) & (sharp <= 0.5), 1.0, 0.0)
    by_image = exact(image, text, ((1,), (1,))) * factor
    by_text = exact(text, image, ((1,), (1,))) * factor
    row, row_flat = log_sum(by_image, 1), log_sum(by_text, 0)
    column, column_flat = log_sum(by_text, 1), log_sum(by_image, 0)
    down = lax.broadcasted_iota(jnp.int32, (count, count), 0)
    across = lax.broadcasted_iota(jnp.int32, (count, count), 1)
    match = jnp.where(across == pairs[...], 1.0, 0.0)
    match_text = jnp.where(down == pairs_row[...], 1.0, 0.0)
    pull = 0.5 * (jnp.exp(by_image - row) + jnp.exp(by_image - column_flat)) - match
    pull_text = 0.5 * (jnp.exp(by_text - column) + jnp.exp(by_text - row_flat)) - match_text
    positive = jnp.sum(match * by_image, axis=1, keepdims=True)
    all_loss[...] = 0.5 * (row + column) - positive
    share = jnp.sum(jnp.sum(pull * by_image, axis=1, keepdims=True), axis=0, keepdims=True)
    grad_sharp[...] = -factor * inside * share
    toward_image = exact(pull, text, ((1,), (0,))) * factor
    toward_text = exact(pull_text, image, ((1,), (0,))) * factor
    all_image[...] = (
        image_scale
        * (toward_image - image * jnp.sum(image * toward_image, axis=1, keepdims=True))
        * (1.0 / queries)
    )
    all_text[...] = text_scale * (
        toward_text - text * jnp.sum(text * toward_text, axis=1, keepdims=True)
    )
    group = loss.shape[0]
    items = group // CORES
    base = info[DP] * group
    loss[...] = all_loss[pl.ds(pl.multiple_of(base, 8), group), :]
    mine = pl.ds(pl.multiple_of(base + info[CORE] * items, 8), items)
    theirs = pl.ds(pl.multiple_of(base + (1 - info[CORE]) * items, 8), items)
    grad_image[...] = jnp.concatenate([all_image[mine, :], all_image[theirs, :]], axis=0).astype(BF)
    grad_text[...] = jnp.concatenate([all_text[mine, :], all_text[theirs, :]], axis=0).astype(BF)


def contrast(info, gathered, pairs, pairs_row, sharpness, queries, group, emb, after):
    count = gathered.shape[0]
    return call(
        functools.partial(contrast_kernel, queries),
        [info, gathered, pairs, pairs_row, sharpness],
        [((group, 1), F32), ((group, emb), BF), ((group, emb), BF), ((1, 1), F32)],
        scratch=[
            pltpu.VMEM((count, 1), F32),
            pltpu.VMEM((count, emb), F32),
            pltpu.VMEM((count, emb), F32),
        ],
        flops=50 * count * count * emb,
        name="contrast",
        after=after,
    )


def cross_backward_kernel(
    info, grad_second, normal, scale, gain, out_weight, keys, values, probs, cross_q, cross_weight,
    rhs, grad_keys, grad_values, grad_query, vectors, grad_heads,
):
    items, _, width = keys.shape
    queries = cross_q.shape[0] // items
    head = width // HEADS
    lanes = GROUP * head
    scaling = 1.0 / math.sqrt(head)
    masks = head_masks(lanes, head)
    groups = HEADS // GROUP

    def put(at, grad_in):
        grad_query[at] = grad_in
        rhs[at, width:] = grad_in.astype(BF)

    grads = norm_back_rows(lambda at: grad_second[at], normal, scale, gain, put)
    vectors[...] = jnp.concatenate(grads, axis=0)
    grad_heads[...] = nt(rhs[:, width:], out_weight[...]).astype(BF)
    for i in range(items):
        at = slice(i * queries, (i + 1) * queries)
        for g in range(groups):
            span = slice(g * lanes, (g + 1) * lanes)
            dm = stack_heads(grad_heads[at, span], masks)
            q = stack_heads(cross_q[at, span], masks)
            p_low = probs[i * groups + g]
            ds = softmax_back(p_low, nt(dm, values[i, :, span]), 2 * queries)
            rhs[at, span] = (merge_heads(nn(ds, keys[i, :, span]), masks) * scaling).astype(BF)
            grad_keys[i, :, span] = (tn(ds, q) * scaling).astype(BF)
            grad_values[i, :, span] = tn(p_low, dm).astype(BF)
    grad_query[...] += nt(rhs[:, :width], cross_weight[...])


def cross_backward(info, grad_second, normal, scale, keys, values, probs, cross_q, p, after):
    items, all_rows, width = keys.shape
    count = cross_q.shape[0]
    return call(
        cross_backward_kernel,
        [
            info, grad_second, normal, scale, p["cross_gain"], p["cross_out"], keys, values, probs,
            cross_q, p["cross_query"],
        ],
        [
            ((count, 2 * width), BF),
            (keys.shape, BF),
            (keys.shape, BF),
            ((count, width), F32),
            ((2, width), F32),
        ],
        scratch=[pltpu.VMEM((count, width), BF)],
        flops=4 * count * width * width + 8 * count * all_rows * width,
        name="cross_backward",
        after=after,
    )


def features_kernel(pieces, info, places, grad_keys, grad_values, *rest):
    shards = rest[: 2 * pieces]
    mine, give, key_full, value_full = rest[2 * pieces :]
    fill_weights(places, shards, key_full, value_full)
    items, rows, deep = mine.shape
    for k, out in enumerate((mine, give)):
        at = slice(k * rows, (k + 1) * rows)
        grad = nt(grad_keys[:, at].reshape(items * rows, -1), key_full[...])
        grad = grad + nt(grad_values[:, at].reshape(items * rows, -1), value_full[...])
        out[...] = grad.reshape(items, rows, deep).astype(out.dtype)


def features_back(info, places, grad_keys, grad_values, shards, rows, after):
    items, _, width = grad_keys.shape
    pieces = len(shards) // 2
    deep = shards[0].shape[0] * pieces
    return call(
        functools.partial(features_kernel, pieces),
        [info, places, grad_keys, grad_values, *shards],
        [((items, rows, deep), F32), ((items, rows, deep), BF)],
        in_specs=[SCALARS, SCALARS] + [None] * (2 + len(shards)),
        scratch=[pltpu.VMEM((deep, width), BF)] * 2,
        flops=8 * items * rows * deep * width,
        name="features_back",
        after=after,
    )


def kv_weights_kernel(pieces, weights, cuts, info, grad_keys, grad_values, *rest):
    feats = rest[:pieces]
    keep, give, total, blocks = rest[pieces:]
    items, rows, deep = feats[0].shape
    width = grad_keys.shape[2]
    size = total.shape[0]
    row = lax.broadcasted_iota(jnp.int32, (size, deep), 0)
    column = lax.broadcasted_iota(jnp.int32, (size, deep), 1)
    for which, out in ((MEMBER, keep), (OTHER, give)):
        select = jnp.where(column == row + info[which] * size, 1.0, 0.0).astype(BF)
        for k, piece in enumerate(feats):
            at = slice(k * rows, (k + 1) * rows)
            picked = nt(select, piece[...].reshape(items * rows, deep)).astype(BF)
            part_k = nn(picked, grad_keys[:, at].reshape(items * rows, width))
            part_v = nn(picked, grad_values[:, at].reshape(items * rows, width))
            if k == 0:
                total[:, :width] = part_k
                total[:, width:] = part_v
            else:
                total[:, :width] += part_k
                total[:, width:] += part_v
        height, span = size // cuts[0], 2 * width // cuts[1]
        for a in range(cuts[0]):
            for b in range(cuts[1]):
                blocks[a * cuts[1] + b] = total[
                    a * height : (a + 1) * height, b * span : (b + 1) * span
                ].astype(BF)
        for position in range(cuts[0] * cuts[1]):
            if cuts[0] * cuts[1] == 1:
                out[0] = blocks[0]
            else:
                out[position] = blocks[info[DP] ^ relative_of(position, weights)]


def kv_weights(info, grad_keys, grad_values, feats, weights, size, cuts, after):
    width = grad_keys.shape[2]
    items, rows, deep = feats[0].shape
    blocks = (cuts[0] * cuts[1], size // cuts[0], 2 * width // cuts[1])
    return call(
        functools.partial(kv_weights_kernel, len(feats), weights, cuts),
        [info, grad_keys, grad_values, *feats],
        [(blocks, BF), (blocks, BF)],
        scratch=[pltpu.VMEM((size, 2 * width), F32), pltpu.VMEM(blocks, BF)],
        flops=4 * size * items * rows * len(feats) * (deep + 2 * width),
        name="kv_weights",
        after=after,
    )


def self_backward_kernel(
    x_size, info, grad_query, grad_text, normal_q, normal_t, scale_q, scale_t, gain, out_weight,
    packed, probs, positions, query_tokens, emb_gain, qkv, more, *rest,
):
    words = rest[:x_size]
    rhs, words_low, grad_mixed, attended, grad_packed, in_q, in_t = rest[x_size:]
    slots, width = positions.shape
    queries = query_tokens.shape[0]
    rows = queries + slots
    items = grad_text.shape[0] // slots
    count = items * slots
    head = width // HEADS
    lanes = GROUP * head
    scaling = 1.0 / math.sqrt(head)
    masks = head_masks(lanes, head)
    groups = HEADS // GROUP

    def put_rows(into, each, offset):
        def put(at, grad_in):
            into[at] = grad_in
            start = at.start // each * rows + offset + at.start % each
            attended[start : start + SLAB] = grad_in.astype(BF)

        return put

    gain_q, bias_q = norm_back_rows(
        lambda at: grad_query[at], normal_q, scale_q, gain, put_rows(in_q, queries, 0)
    )
    gain_t, bias_t = norm_back_rows(
        lambda at: grad_text[at], normal_t, scale_t, gain, put_rows(in_t, slots, queries)
    )
    half = items * rows // 2
    rhs[:half, 3 * width : 4 * width] = attended[:half]
    rhs[:half, 4 * width :] = attended[half:]
    grad_mixed[...] = nt(attended[...], out_weight[...]).astype(BF)
    pair = 2 * rows
    for j in range(items // 2):
        at = slice(j * pair, (j + 1) * pair)
        for g in range(groups):
            base = g * lanes
            q = stack_heads(packed[at, base : base + lanes], masks)
            k = packed[at, width + base : width + base + lanes]
            v = packed[at, 2 * width + base : 2 * width + base + lanes]
            dm = stack_heads(grad_mixed[at, base : base + lanes], masks)
            p_low = probs[j * groups + g]
            ds = softmax_back(p_low, nt(dm, v), pair)
            grad_packed[at, base : base + lanes] = (
                merge_heads(nn(ds, k), masks) * scaling
            ).astype(BF)
            grad_packed[at, width + base : width + base + lanes] = (tn(ds, q) * scaling).astype(BF)
            grad_packed[at, 2 * width + base : 2 * width + base + lanes] = tn(p_low, dm).astype(BF)
    total_q = None
    for i in range(items):
        piece = grad_packed[i * rows : i * rows + queries].astype(F32)
        total_q = piece if total_q is None else total_q + piece
        rhs[i * slots : (i + 1) * slots, : 3 * width] = grad_packed[
            i * rows + queries : (i + 1) * rows
        ]
    total_q = total_q.astype(BF)
    rhs[count : count + queries, : 3 * width] = total_q
    in_t[...] += nt(rhs[:count, : 3 * width], qkv[...])
    start_q = jnp.sum(in_q[...].reshape(items, queries, width), axis=0) + nt(total_q, qkv[...])
    normal_e, scale_e = normalise(query_tokens[...].astype(F32))
    grad_tokens, gain_e, bias_e = norm_back(start_q, normal_e, scale_e, emb_gain[...])
    gain_w, bias_w = gain_e, bias_e
    position_grad = None
    for at in slabs(count):
        normal_w, scale_w = normalise(embed_slab(words, positions, at))
        grad_words, part_gain, part_bias = norm_back(in_t[at], normal_w, scale_w, emb_gain[...])
        gain_w, bias_w = gain_w + part_gain, bias_w + part_bias
        words_low[at] = grad_words.astype(BF)
        position_grad = grad_words if position_grad is None else position_grad + grad_words
    rhs[count : count + queries, 3 * width : 4 * width] = grad_tokens.astype(BF)
    rhs[count : count + slots, 4 * width :] = position_grad.astype(BF)
    gain_w = jnp.sum(gain_w, axis=0, keepdims=True)
    bias_w = jnp.sum(bias_w, axis=0, keepdims=True)
    vectors = jnp.concatenate(
        [gain_w, bias_w, gain_q + gain_t, bias_q + bias_t]
        + [more[...], jnp.zeros((6, width), F32)],
        axis=0,
    )
    rhs[count + queries :, :width] = vectors.astype(BF)
    rhs[count + queries :, width:] = jnp.zeros((16, 4 * width), BF)


def self_backward(info, grad_query, grad_text, state, packed, probs, words, more, p, after):
    normal_q, normal_t, scale_q, scale_t = state
    slots, width = p["positions"].shape
    queries = p["query_tokens"].shape[0]
    items = words[0].shape[0] // slots
    rows = queries + slots
    count = items * slots
    ins = [
        info, grad_query, grad_text, normal_q, normal_t, scale_q, scale_t, p["self_gain"],
        p["out"], packed, probs, p["positions"], p["query_tokens"], p["emb_gain"], p["qkv"], more,
        *words,
    ]
    return call(
        functools.partial(self_backward_kernel, len(words)),
        ins,
        [((count + queries + 16, 5 * width), BF), ((count, width), BF)],
        scratch=[
            pltpu.VMEM((items * rows, width), BF),
            pltpu.VMEM((items * rows, width), BF),
            pltpu.VMEM((items * rows, 3 * width), BF),
            pltpu.VMEM((items * queries, width), F32),
            pltpu.VMEM((count, width), F32),
        ],
        flops=2 * items * rows * width * width * 7,
        name="self_backward",
        after=after,
    )


def spread_rows(grads, each, first_only):
    items, emb = grads.shape
    wide = jnp.broadcast_to(grads[:, None, :], (items, each, emb))
    if first_only:
        row = lax.broadcasted_iota(jnp.int32, (items, each, emb), 1)
        wide = jnp.where(row == 0, wide, 0.0)
    return wide.reshape(items * each, emb).astype(BF)


def mid_weights_kernel(
    weights, share_rows, info, query_a, query_b, mixed_a, mixed_b, rhs_a, rhs_b, final_a, final_b,
    text_a, text_b, grad_image, grad_text, keep, give,
):
    count, width = final_a.shape
    items = grad_image.shape[0] // 2
    each = count // items
    blocks = 1 << len(weights)
    cross_q = nn(query_a[...], rhs_a[:, :width]) + nn(query_b[...], rhs_b[:, :width])
    cross_out = nn(mixed_a[...], rhs_a[:, width:]) + nn(mixed_b[...], rhs_b[:, width:])
    select = choose_rows(info, SHARE, weights, share_rows, width // blocks, width)
    image, text = grad_image[...].astype(F32), grad_text[...].astype(F32)
    proj_i = proj_t = None
    for k, (final, first) in enumerate(((final_a, text_a), (final_b, text_b))):
        at = slice(k * items, (k + 1) * items)
        part_i = nn(nt(select, final[...]).astype(BF), spread_rows(image[at], each, False))
        part_t = nn(nt(select, first[...]).astype(BF), spread_rows(text[at], each, True))
        proj_i = part_i if proj_i is None else proj_i + part_i
        proj_t = part_t if proj_t is None else proj_t + part_t
    top = jnp.concatenate([cross_q, proj_i], axis=1)
    low = jnp.concatenate([cross_out, proj_t], axis=1)
    for b in range(blocks):
        out, at = (keep, b) if b < blocks // 2 else (give, b - blocks // 2)
        rows = slice(b * share_rows, (b + 1) * share_rows)
        out[at] = jnp.concatenate([top[rows], low[rows]], axis=0).astype(BF)


def mid_weights(
    info, query, mixed, rhs, final, text, grad_image, grad_text, weights, share_rows, after
):
    width = final[0].shape[1]
    emb = grad_image.shape[1]
    blocks = 1 << len(weights)
    out = ((blocks // 2, 2 * share_rows, width + emb), BF)
    at = query[0].shape[1] - final[0].shape[0]
    lhs_spec = pl.BlockSpec(
        (query[0].shape[0], final[0].shape[0]), lambda *_: (0, at // final[0].shape[0])
    )
    return call(
        functools.partial(mid_weights_kernel, weights, share_rows),
        [info, *query, *mixed, *rhs, *final, *text, grad_image, grad_text],
        [out, out],
        grid=(1,),
        in_specs=[None, lhs_spec, lhs_spec] + [None] * 10,
        flops=4 * query[0].shape[0] * final[0].shape[0] * 4 * width,
        name="mid_weights",
        after=after,
    )


def last_weights_kernel(
    weights, share_rows, info, chosen_q, lhs_a, lhs_b, rhs_a, rhs_b, keep, give
):
    width = rhs_a.shape[1] // 5
    blocks = 1 << len(weights)
    queries = chosen_q.shape[1]
    count = rhs_a.shape[0] - queries - 16
    select = choose_rows(info, SHARE, weights, share_rows, width // blocks, width)
    summed_q = (
        rhs_a[count : count + queries, : 3 * width].astype(F32)
        + rhs_b[count : count + queries, : 3 * width].astype(F32)
    ).astype(BF)
    qkv = nn(chosen_q[...], summed_q)
    out_grad = vector_grad = None
    for lhs, rhs in ((lhs_a, rhs_a), (lhs_b, rhs_b)):
        qkv = qkv + nn(lhs[:, :count], rhs[:count, : 3 * width])
        part = nn(lhs[:, count : 2 * count], rhs[:count, 3 * width : 4 * width])
        part = part + nn(lhs[:, 2 * count : 3 * count], rhs[:count, 4 * width :])
        out_grad = part if out_grad is None else out_grad + part
        rows = jnp.concatenate(
            [
                rhs[count : count + queries, 3 * width : 4 * width],
                rhs[count : count + queries, 4 * width :],
                rhs[count + queries :, :width],
                jnp.zeros((128 - 2 * queries - 16, width), BF),
            ],
            axis=0,
        )
        part = nt(select, rows)
        vector_grad = part if vector_grad is None else vector_grad + part
    split = 2 * width
    top = jnp.concatenate([qkv[:, :split], vector_grad], axis=1)
    low = jnp.concatenate([qkv[:, split:], out_grad, jnp.zeros_like(vector_grad)], axis=1)
    for b in range(blocks):
        out, at = (keep, b) if b < blocks // 2 else (give, b - blocks // 2)
        rows = slice(b * share_rows, (b + 1) * share_rows)
        out[at] = jnp.concatenate([top[rows], low[rows]], axis=0).astype(BF)


def last_weights(info, chosen_q, lhs, rhs, weights, share_rows, after):
    width = rhs[0].shape[1] // 5
    blocks = 1 << len(weights)
    out = ((blocks // 2, 2 * share_rows, 2 * width + 128), BF)
    return call(
        functools.partial(last_weights_kernel, weights, share_rows),
        [info, chosen_q, *lhs, *rhs],
        [out, out],
        flops=4 * chosen_q.shape[0] * 256 * 6 * width,
        name="last_weights",
        after=after,
    )


def ff_assemble_kernel(pieces, share_rows, info, places, *rest):
    parts = rest[:pieces]
    outs = rest[pieces:]
    width = parts[0].shape[1]
    deep = 4 * share_rows
    for k, piece in enumerate(parts):
        for f in range(2):
            up, down = outs[2 * f : 2 * f + 2]
            base = f * 2 * deep
            grad = piece[base : base + deep].astype(F32)
            at = pl.ds(pl.multiple_of(places[k] * share_rows, 8), share_rows)
            for c in range(4):
                up[at, c * width : (c + 1) * width] = grad[c * share_rows : (c + 1) * share_rows]
            at = pl.ds(pl.multiple_of(places[k] * deep, 8), deep)
            down[at, :] = piece[base + deep : base + 2 * deep].astype(F32)


def ff_assemble(info, places, parts, share_rows):
    width = parts[0].shape[1]
    rows = share_rows * len(parts)
    shapes = [((rows, 4 * width), F32), ((4 * rows, width), F32)] * 2
    return call(
        functools.partial(ff_assemble_kernel, len(parts), share_rows),
        [info, places, *parts],
        shapes,
        in_specs=[SCALARS, SCALARS] + [None] * len(parts),
        name="ff_assemble",
    )


def tail_assemble_kernel(pieces, share_rows, queries, info, places, *rest):
    parts = rest[:pieces]
    qkv, out, cross_q, cross_out, image, text, tokens, slots, vectors, spread = rest[pieces:]
    width = out.shape[1]
    emb = image.shape[1]
    spread[...] = jnp.zeros_like(spread)
    for k, piece in enumerate(parts):
        at = pl.ds(pl.multiple_of(places[k] * share_rows, 8), share_rows)
        grad = piece[...].astype(F32)
        top, low = grad[:share_rows], grad[share_rows:]
        cross_q[at, :] = top[:, :width]
        image[at, :] = top[:, width : width + emb]
        cross_out[at, :] = low[:, :width]
        text[at, :] = low[:, width : width + emb]
        base = width + emb
        qkv[at, : 2 * width] = top[:, base : base + 2 * width]
        spread[at, :] = top[:, base + 2 * width :]
        qkv[at, 2 * width :] = low[:, base : base + width]
        out[at, :] = low[:, base + width : base + 2 * width]
    flipped = spread[...].T
    rows = out.shape[0]
    tokens[...] = flipped[:queries, :rows]
    slots[...] = flipped[queries : 2 * queries, :rows]
    vectors[...] = flipped[2 * queries : 2 * queries + 16, :rows]


def tail_assemble(info, places, parts, share_rows, width, emb, queries):
    rows = share_rows * len(parts)
    shapes = [
        ((rows, 3 * width), F32),
        ((rows, width), F32),
        ((rows, width), F32),
        ((rows, width), F32),
        ((rows, emb), F32),
        ((rows, emb), F32),
        ((queries, rows), F32),
        ((queries, rows), F32),
        ((16, rows), F32),
    ]
    return call(
        functools.partial(tail_assemble_kernel, len(parts), share_rows, queries),
        [info, places, *parts],
        shapes,
        in_specs=[SCALARS, SCALARS] + [None] * len(parts),
        scratch=[pltpu.VMEM((128, 128), F32)],
        name="tail_assemble",
    )


def kv_assemble_kernel(count, weights, cuts, info, *rest):
    parts = rest[:count]
    key, value, blocks = rest[count:]
    at = 0
    for piece in parts:
        for b in range(piece.shape[0]):
            blocks[info[DP] ^ relative_of(at, weights)] = piece[b].astype(F32)
            at += 1
    height, span = blocks.shape[1:]
    width = key.shape[1]
    for a in range(cuts[0]):
        for b in range(cuts[1]):
            out = key if b * span < width else value
            base = b * span % width
            out[a * height : (a + 1) * height, base : base + span] = blocks[a * cuts[1] + b]


def kv_assemble(info, parts, weights, cuts, width):
    height, span = parts[0].shape[1:]
    shape = ((height * cuts[0], width), F32)
    return call(
        functools.partial(kv_assemble_kernel, len(parts), weights, cuts),
        [info, *parts],
        [shape, shape],
        scratch=[pltpu.VMEM((cuts[0] * cuts[1], height, span), F32)],
        name="kv_assemble",
    )


def features_assemble_kernel(info, mine, theirs, out):
    @pl.when(pl.program_id(0) == info[CORE])
    def _():
        out[...] = mine[...]

    @pl.when(pl.program_id(0) != info[CORE])
    def _():
        out[...] = theirs[...].astype(F32)


def features_assemble(info, mine, theirs):
    items, rows, deep = mine.shape
    return call(
        features_assemble_kernel,
        [info, mine, theirs],
        [((CORES * items, rows, deep), F32)],
        grid=(CORES,),
        out_specs=[pl.BlockSpec((items, rows, deep), lambda k: (k, 0, 0))],
        name="features_assemble",
    )[0]


def hidden_assemble_kernel(info, query_a, text_a, query_b, text_b, out):
    items = out.shape[0]
    queries = query_a.shape[0] // items
    mine = pl.program_id(0) == info[CORE]

    def put(query, text):
        out[:, :queries] = query[...].reshape(items, queries, -1)
        out[:, queries:] = text[...].reshape(items, -1, out.shape[2])

    @pl.when(mine)
    def _():
        put(query_a, text_a)

    @pl.when(jnp.logical_not(mine))
    def _():
        put(query_b, text_b)


def hidden_assemble(info, query_a, text_a, query_b, text_b, items):
    width = query_a.shape[1]
    rows = (query_a.shape[0] + text_a.shape[0]) // items
    return call(
        hidden_assemble_kernel,
        [info, query_a, text_a, query_b, text_b],
        [((CORES * items, rows, width), BF)],
        grid=(CORES,),
        out_specs=[pl.BlockSpec((items, rows, width), lambda k: (k, 0, 0))],
        name="hidden_assemble",
    )[0]


def slots_kernel(
    table_rows, patch_size, info, tokens, slot_of, rows_of, most
):
    groups, count = tokens.shape
    here_from = info[MEMBER] * table_rows
    flipped = tokens[...].T
    down = lax.broadcasted_iota(jnp.int32, (count, count), 0)
    across = lax.broadcasted_iota(jnp.int32, (count, count), 1)
    place = lax.broadcasted_iota(jnp.int32, (1, count), 1)
    place_down = lax.broadcasted_iota(jnp.int32, (count, 1), 0)
    slot_iota = lax.broadcasted_iota(jnp.int32, (count, SLOTS), 1)
    top = jnp.zeros((1, 1), jnp.int32)
    for d in range(groups):
        row, column = tokens[d : d + 1, :], flipped[:, d : d + 1]
        same = row == column
        first = jnp.min(jnp.where(same, down, count), axis=0, keepdims=True)
        first_down = jnp.min(jnp.where(same, across, count), axis=1, keepdims=True)
        lead, lead_down = first == place, first_down == place_down
        here = (row >= here_from) & (row < here_from + table_rows)
        here_down = (column >= here_from) & (column < here_from + table_rows)
        ahead = jnp.where((lead_down & here_down) & (down < first), 1, 0)
        slot_of[d : d + 1, :] = jnp.where(here, jnp.sum(ahead, axis=0, keepdims=True), -1)
        ahead = jnp.where((lead & here) & (across < first_down), 1, 0)
        slot = jnp.where(here_down, jnp.sum(ahead, axis=1, keepdims=True), -1)
        rows_of[:, d * SLOTS : (d + 1) * SLOTS] = jnp.max(
            jnp.where(slot == slot_iota, column - here_from, -1), axis=0, keepdims=True
        )
        for q in range(patch_size):
            within = lead & (row >= q * table_rows) & (row < (q + 1) * table_rows)
            top = jnp.maximum(
                top, jnp.sum(jnp.where(within, 1, 0), axis=1, keepdims=True)
            )
    most[...] = top


def slots_of(info, tokens, table_rows, patch_size):
    groups, count = tokens.shape
    return call(
        functools.partial(slots_kernel, table_rows, patch_size),
        [info, tokens],
        [
            ((groups, count), jnp.int32),
            ((1, groups * SLOTS), jnp.int32),
            ((1, 1), jnp.int32),
        ],
        flops=groups * count * count * 8,
        name="slots",
    )


def collect_kernel(info, slot_of, mine, theirs, out):
    count = mine.shape[0]
    slot = lax.broadcasted_iota(jnp.int32, (SLOTS, count), 0)
    total = None
    for rows, core in ((mine, info[CORE]), (theirs, 1 - info[CORE])):
        at = pl.ds(pl.multiple_of(core * count, 128), count)
        hot = jnp.where(slot_of[pl.ds(info[DP], 1), at] == slot, 1.0, 0.0).astype(BF)
        part = nn(hot, rows[...])
        total = part if total is None else total + part
    out[...] = total.astype(BF)


def collect(info, slot_of, mine, theirs):
    return call(
        collect_kernel,
        [info, slot_of, mine, theirs],
        [((SLOTS, mine.shape[1]), BF)],
        flops=4 * SLOTS * mine.size,
        name="collect",
    )[0]


def table_kernel(z_size, y_size, info, rows_of, own, *rest):
    rising, falling = rest[: z_size - 1], rest[z_size - 1 : 2 * (z_size - 1)]
    out, ordered = rest[2 * (z_size - 1) :]
    chunk = out.shape[0]

    @pl.when(pl.program_id(0) == 0)
    def _():
        z, y = info[DP] // y_size, info[DP] % y_size

        def put(piece, at_z):
            for j in range(y_size):
                at = pl.multiple_of((at_z * y_size + (y ^ j)) * SLOTS, SLOTS)
                ordered[pl.ds(at, SLOTS), :] = piece[j * SLOTS : (j + 1) * SLOTS]

        put(own, z)
        for k in range(1, z_size):

            @pl.when(z - k >= 0)
            def _():
                put(rising[k - 1], z - k)

            @pl.when(z + k < z_size)
            def _():
                put(falling[k - 1], z + k)

    row = lax.broadcasted_iota(jnp.int32, (chunk, rows_of.shape[1]), 0)
    row = row + pl.program_id(0) * chunk
    hot = jnp.where(row == rows_of[...], 1.0, 0.0).astype(BF)
    out[...] = nn(hot, ordered[...])


def table_back(info, rows_of, own, rising, falling, z_size, y_size, table_rows, chunk=640):
    width = own.shape[1]
    count = rows_of.shape[1]
    return call(
        functools.partial(table_kernel, z_size, y_size),
        [info, rows_of, own, *rising, *falling],
        [((table_rows, width), F32)],
        grid=(table_rows // chunk,),
        out_specs=[pl.BlockSpec((chunk, width), lambda k: (k, 0))],
        scratch=[pltpu.VMEM((count, width), BF)],
        flops=2 * table_rows * count * width,
        name="table",
    )[0]


def swap_core(values):
    return lax.ppermute(values, "core", [(0, 1), (1, 0)])


def from_x(values, size, step):
    return lax.ppermute(values, "x", [(s, (s - step) % size) for s in range(size)])


def part(values, index, size, axis):
    return lax.dynamic_slice_in_dim(values, index * size, size, axis)


def exchange(values, axis, size, bit):
    return lax.ppermute(values, axis, [(s, s ^ bit) for s in range(size)])


def gather_doubling(values, axis, size):
    place = lax.axis_index(axis)
    bit = 1
    while bit < size:
        other = exchange(values, axis, size, bit)
        low = (place & bit) == 0
        values = jnp.concatenate(
            [jnp.where(low, values, other), jnp.where(low, other, values)], axis=0
        )
        bit *= 2
    return values


def gather_relative(values, axis, size):
    bit = 1
    while bit < size:
        values = jnp.concatenate([values, exchange(values, axis, size, bit)], axis=0)
        bit *= 2
    return values


def pass_on(values, axis, size):
    up = [(s, s + 1) for s in range(size - 1)]
    down = [(s + 1, s) for s in range(size - 1)]
    rising, falling = [values], [values]
    for _ in range(1, size):
        rising.append(lax.ppermute(rising[-1], axis, up))
        falling.append(lax.ppermute(falling[-1], axis, down))
    return rising[1:], falling[1:]


def gather_patch(values, x_size):
    own = [values] + [from_x(values, x_size, k) for k in range(1, x_size)]
    return own + [swap_core(v) for v in own]


def patch_places(x_size):
    xi, ci = lax.axis_index("x"), lax.axis_index("core")
    columns = [(xi + k) % x_size for k in range(x_size)]
    return jnp.stack([x * CORES + ci for x in columns] + [x * CORES + 1 - ci for x in columns])


def halving_steps(z_size, y_size, order):
    y_steps = [("y", y_size, 1 << k) for k in range(y_size.bit_length() - 1)]
    z_steps = [("z", z_size, 1 << k) for k in range(z_size.bit_length() - 1)]
    return y_steps + z_steps if order == "y" else z_steps + y_steps


def add_low(a, b):
    return (a.astype(F32) + b.astype(F32)).astype(BF)


def reduce_scatter(keep, give, z_size, y_size, order):
    steps = halving_steps(z_size, y_size, order)
    later = []
    for k, step in enumerate(steps):
        got = exchange(give, *step)
        half = keep.shape[0] // 2
        if k < len(steps) - 1:
            keep, give = add_low(keep[:half], got[:half]), add_low(keep[half:], got[half:])
            later.append(give)
    return add_low(keep, got)[0], later


def gather_blocks(block, z_size, y_size, order):
    pieces = [block[None]]
    for step in halving_steps(z_size, y_size, order)[::-1]:
        whole_piece = pieces[0] if len(pieces) == 1 else jnp.concatenate(pieces, axis=0)
        pieces = [whole_piece, exchange(whole_piece, *step)]
    return pieces


def all_reduce(values, z_size, y_size):
    for step in halving_steps(z_size, y_size, "y"):
        values = add_low(values, exchange(values, *step))
    return values


def shards(
    z_size, y_size, x_size,
    token_ids, token_used, paired_ids, features, incoming, query_tokens, table, positions,
    emb_gain, emb_bias, qkv, out_weight, self_gain, self_bias, cross_query, key_shard,
    value_shard, cross_out, cross_gain, cross_bias, query_up, query_down, query_gain, query_bias,
    text_up, text_down, text_gain, text_bias, image_proj, text_proj, sharpness,
):
    group, slots = token_ids.shape
    queries, width = query_tokens.shape
    emb = image_proj.shape[1]
    items = group // CORES
    patch_size = x_size * CORES
    table_rows = table.shape[0]
    feat_rows = features.shape[1]
    kv_rows = key_shard.shape[0]
    dp_size = z_size * y_size
    xi, ci = lax.axis_index("x"), lax.axis_index("core")
    di = lax.axis_index("z") * y_size + lax.axis_index("y")
    member = xi * CORES + ci
    other = xi * CORES + 1 - ci
    block_rows = width // dp_size
    shared = block_rows % (8 * patch_size) == 0
    share_rows = block_rows // patch_size if shared else block_rows
    share, partner = (member, other) if shared else (jnp.int32(0), jnp.int32(0))
    info = jnp.stack([di, share, partner, ci, member, other]).astype(jnp.int32)
    places = patch_places(x_size).astype(jnp.int32)
    orders = {k: order_weights(z_size, y_size, k) for k in ("y", "z")}

    norms = jnp.stack(
        [
            emb_gain, emb_bias, self_gain, self_bias, cross_gain, cross_bias, query_gain,
            query_bias, text_gain, text_bias,
        ]
    )[:, None, :]
    names = ("emb", "self", "cross", "query", "text")
    p = {name + "_gain": Row(norms, 2 * k) for k, name in enumerate(names)}
    p |= {name + "_bias": Row(norms, 2 * k + 1) for k, name in enumerate(names)}
    p |= dict(
        positions=positions, query_tokens=query_tokens, qkv=qkv, out=out_weight,
        cross_query=cross_query, cross_out=cross_out, query_up=query_up, query_down=query_down,
        text_up=text_up, text_down=text_down, image_proj=image_proj, text_proj=text_proj,
    )

    def own_first(values):
        return jnp.concatenate(
            [part(values, ci, items, 0), part(values, 1 - ci, items, 0)], axis=0
        )

    local_ids = (own_first(token_ids) - member * table_rows).reshape(-1, 1)
    words_mine, words_give = look_up(info, local_ids, table)
    word_sum = words_mine + swap_core(words_give)
    words = [word_sum] + [from_x(word_sum, x_size, k) for k in range(1, x_size)]

    feat_mine = part(features, ci, items, 0)
    feat_got = swap_core(part(features, 1 - ci, items, 0))
    feats = [feat_mine, feat_got]
    for k in range(1, x_size):
        feats += [from_x(feat_mine, x_size, k), from_x(feat_got, x_size, k)]
    kv_shards = gather_patch(key_shard, x_size) + gather_patch(value_shard, x_size)

    ids = jnp.concatenate([token_ids, paired_ids[:, None]], axis=1)
    ids = gather_doubling(gather_doubling(ids, "y", y_size), "z", z_size)
    all_tokens = ids[:, :slots].reshape(dp_size, group * slots)
    slot_of, rows_of, most = slots_of(info, all_tokens, table_rows, patch_size)

    used = jnp.concatenate(
        [jnp.ones((items, queries), jnp.int32), part(token_used, ci, items, 0)], axis=1
    ).reshape(items // 2, 2 * (queries + slots))
    (packed, probs, normal_q, normal_t, scale_q, scale_t, cross_q, lhs_mine, lhs_give, chosen_q) = (
        self_forward(info, words, used, p, orders, share_rows)
    )
    lhs_got = swap_core(lhs_give)
    text_names = ("text_up", "text_down", "text_gain", "text_bias", "text_proj")
    query_names = ("query_up", "query_down", "query_gain", "query_bias", "image_proj")
    (t_slope, t_keep, t_give, t_normal, t_scale, text_final, text_raw) = ff_forward(
        info, normal_t, p["self_gain"], p["self_bias"], text_names, p, orders["y"], share_rows,
        items, False,
    )
    t_got = swap_core(t_give)
    keys, values = key_value(info, places, feats, kv_shards)
    cross_probs, normal_c, scale_c, mixed_mine, mixed_give = cross_forward(
        info, cross_q, keys, values, normal_q, p, orders, share_rows
    )
    mixed_got = swap_core(mixed_give)
    (q_slope, q_keep, q_give, q_normal, q_scale, query_final, image_raw) = ff_forward(
        info, normal_c, p["cross_gain"], p["cross_bias"], query_names, p, orders["y"], share_rows,
        items, True,
    )
    q_got = swap_core(q_give)

    query_other, text_other = swap_core(query_final), swap_core(text_final)
    hidden_out = hidden_assemble(
        info, query_final, text_final, query_other, text_other, items
    )

    gathered = gather_doubling(jnp.concatenate([image_raw, text_raw], axis=1), "core", CORES)
    gathered = gather_doubling(gather_doubling(gathered, "y", y_size), "z", z_size)
    loss, grad_image, grad_text, grad_sharp = contrast(
        info, gathered, ids[:, slots:], ids[:, slots:].reshape(1, -1), sharpness.reshape(1, 1),
        queries, group, emb, [hidden_out, most],
    )

    q_rhs, grad_second, q_vectors = ff_backward(
        info, incoming, 0, grad_image, (q_slope, q_normal, q_scale),
        ("query_up", "query_down", "query_gain", "image_proj"), p, True,
    )
    t_rhs, grad_text_rows, t_vectors = ff_backward(
        info, incoming, 1, grad_text, (t_slope, t_normal, t_scale),
        ("text_up", "text_down", "text_gain", "text_proj"), p, False, [q_vectors],
    )
    q_weights = ff_weights(
        info, q_keep, q_got, q_rhs, swap_core(q_rhs), share_rows, dp_size, width, [t_vectors]
    )
    t_weights = ff_weights(
        info, t_keep, t_got, t_rhs, swap_core(t_rhs), share_rows, dp_size, width, [q_weights[0]]
    )
    t_sum, t_later = reduce_scatter(*t_weights, z_size, y_size, "y")
    q_sum, q_later = reduce_scatter(*q_weights, z_size, y_size, "y")

    def spread(values):
        return gather_patch(values, x_size) if shared else [values]

    ff_parts = spread(jnp.concatenate([q_sum, t_sum], axis=0))
    spots = places if shared else jnp.zeros((1,), jnp.int32)
    query_up_grad, query_down_grad, text_up_grad, text_down_grad = ff_assemble(
        info, spots, ff_parts, share_rows
    )

    m_rhs, grad_keys, grad_values, grad_query_rows, c_vectors = cross_backward(
        info, grad_second, normal_c, scale_c, keys, values, cross_probs, cross_q, p,
        [t_weights[0]],
    )
    mid = mid_weights(
        info, (lhs_mine, lhs_got), (mixed_mine, mixed_got), (m_rhs, swap_core(m_rhs)),
        (query_final, query_other), (text_final, text_other), grad_image, grad_text, orders["y"],
        share_rows, [],
    )
    mid_sum, _ = reduce_scatter(*mid, z_size, y_size, "y")
    cuts = (2, dp_size // 2) if dp_size == 8 and kv_rows % 32 == 0 else (1, 1)
    kv_keep, kv_give = kv_weights(
        info, grad_keys, grad_values, feats, orders["y"], kv_rows, cuts,
        [mid[0]],
    )
    kv_part = add_low(kv_keep, swap_core(kv_give))
    if cuts[0] > 1:
        half = dp_size // 2
        kv_block, _ = reduce_scatter(kv_part[:half], kv_part[half:], z_size, y_size, "y")
        key_grad, value_grad = kv_assemble(
            info, gather_blocks(kv_block, z_size, y_size, "y"), orders["y"], cuts, width
        )
    else:
        kv_total = all_reduce(kv_part[0], z_size, y_size).astype(F32)
        key_grad, value_grad = kv_total[:, :width], kv_total[:, width:]
    feature_mine, feature_give = features_back(
        info, places, grad_keys, grad_values, kv_shards, feat_rows, [kv_keep]
    )
    features_grad = features_assemble(info, feature_mine, swap_core(feature_give))
    more = jnp.concatenate([c_vectors, q_vectors, t_vectors], axis=0)
    l_rhs, words_low = self_backward(
        info, grad_query_rows, grad_text_rows, (normal_q, normal_t, scale_q, scale_t), packed,
        probs, words, more, p, [feature_mine, q_later[0]],
    )
    words_other = swap_core(words_low)

    own = gather_relative(collect(info, slot_of, words_low, words_other), "y", y_size)
    rising, falling = pass_on(own, "z", z_size)

    def few(words_low, words_other):
        return table_back(info, rows_of, own, rising, falling, z_size, y_size, table_rows)

    def many(words_low, words_other):
        low_core = ci == 0
        group_words = jnp.concatenate(
            [
                jnp.where(low_core, words_low, words_other),
                jnp.where(low_core, words_other, words_low),
            ],
            axis=0,
        )
        own = lax.dynamic_index_in_dim(all_tokens, di, axis=0, keepdims=False)
        rows = lax.broadcasted_iota(jnp.int32, (1, table_rows), 1) + member * table_rows
        hot = (own[:, None] == rows).astype(BF)
        return all_reduce(tn(hot, group_words).astype(BF), z_size, y_size).astype(F32)

    table_grad = lax.cond(most[0, 0] <= SLOTS, few, many, words_low, words_other)

    last = last_weights(
        info, chosen_q, (lhs_mine, lhs_got), (l_rhs, swap_core(l_rhs)), orders["y"], share_rows,
        [own],
    )
    last_sum, _ = reduce_scatter(*last, z_size, y_size, "y")
    tail_parts = spread(jnp.concatenate([mid_sum, last_sum], axis=1))
    (
        qkv_grad, out_grad, cross_query_grad, cross_out_grad, image_proj_grad, text_proj_grad,
        tokens_grad, position_grad, vectors,
    ) = tail_assemble(info, spots, tail_parts, share_rows, width, emb, queries)

    return (
        hidden_out, loss.reshape(-1), features_grad, tokens_grad, table_grad, position_grad,
        vectors[0], vectors[1], qkv_grad, out_grad, vectors[2], vectors[3], cross_query_grad,
        key_grad, value_grad, cross_out_grad, vectors[4], vectors[5], query_up_grad,
        query_down_grad, vectors[6], vectors[7], text_up_grad, text_down_grad, vectors[8],
        vectors[9], image_proj_grad, text_proj_grad, grad_sharp.reshape(()),
    )


def solution(mesh):
    dp_size = mesh.shape["dp"]
    y_size = 1 << ((dp_size.bit_length() - 2) // 2)
    z_size = dp_size // y_size
    x_size = mesh.shape["patch"] // CORES
    split = Mesh(
        mesh.devices.reshape(z_size, y_size, x_size, CORES), ("z", "y", "x", "core")
    )
    dp, patch = ("z", "y"), ("x", "core")
    placed = (
        [P(dp, None), P(dp, None), P(dp), P(dp, patch, None), P(dp, None, None), P()]
        + [P(patch, None)]
        + [P()] * 8
        + [P(patch, None)] * 2
        + [P()] * 14
    )
    out = (
        [P(dp, None, None), P(dp), P(dp, patch, None), P(None, dp), P(patch, None)]
        + [P(None, dp), P(dp), P(dp), P(dp, None), P(dp, None), P(dp), P(dp)]
        + [P(dp, None), P(patch, None), P(patch, None), P(dp, None), P(dp), P(dp)]
        + [P(dp, None), P(dp, None), P(dp), P(dp), P(dp, None), P(dp, None)]
        + [P(dp), P(dp), P(dp, None), P(dp, None), P()]
    )

    def body(*args):
        return shards(z_size, y_size, x_size, *args)

    return jax.shard_map(
        body, mesh=split, in_specs=tuple(placed), out_specs=tuple(out), check_vma=False
    )
```

```python
import functools
import math

import jax
import jax.numpy as jnp
from jax import lax
from jax.experimental import pallas as pl
from jax.experimental.pallas import tpu as pltpu
from jax.sharding import Mesh, PartitionSpec as P

HEADS = 12
GROUP = 4
SLOTS = 128
CORES = 2
BF = jnp.bfloat16
F32 = jnp.float32
HIGHEST = lax.Precision.HIGHEST
VMEM_BYTES = 60 * 1024 * 1024
VMEM_SPARE = 10 * 1024 * 1024
SLAB = 32
DP, SHARE, PARTNER, CORE, MEMBER, OTHER = range(6)


def nn(a, b):
    return lax.dot_general(a, b, (((1,), (0,)), ((), ())), preferred_element_type=F32)


def nt(a, b):
    return lax.dot_general(a, b, (((1,), (1,)), ((), ())), preferred_element_type=F32)


def tn(a, b):
    return lax.dot_general(a, b, (((0,), (0,)), ((), ())), preferred_element_type=F32)


def exact(a, b, dims):
    return lax.dot_general(a, b, ((dims[0], dims[1]), ((), ())), precision=HIGHEST)


def normalise(values):
    centred = values - jnp.mean(values, axis=-1, keepdims=True)
    spread = jnp.mean(centred * centred, axis=-1, keepdims=True)
    scale = lax.rsqrt(spread + 1e-06)
    return centred * scale, scale


def slabs(rows):
    step = math.gcd(rows, SLAB)
    return [slice(r, r + step) for r in range(0, rows, step)]


def fold(values):
    return jnp.sum(values.reshape(-1, 8, values.shape[-1]), axis=0)


def norm_back(grad, normal, scale, gain):
    inner = grad * gain
    first = jnp.mean(inner, axis=-1, keepdims=True)
    second = jnp.mean(inner * normal, axis=-1, keepdims=True)
    return scale * (inner - first - normal * second), fold(grad * normal), fold(grad)


def norm_back_rows(grad_of, normal, scale, gain, put):
    gains = biases = None
    for at in slabs(normal.shape[0]):
        grad_in, part_gain, part_bias = norm_back(grad_of(at), normal[at], scale[at], gain[...])
        put(at, grad_in)
        gains = part_gain if gains is None else gains + part_gain
        biases = part_bias if biases is None else biases + part_bias
    return jnp.sum(gains, axis=0, keepdims=True), jnp.sum(biases, axis=0, keepdims=True)


def gelu_both(values):
    size = jnp.abs(values)
    t = 1.0 / (1.0 + (0.3275911 * math.sqrt(0.5)) * size)
    bell = jnp.exp(-0.5 * values * values)
    poly = t * (
        0.254829592
        + t * (-0.284496736 + t * (1.421413741 + t * (-1.453152027 + t * 1.061405429)))
    )
    tail = 0.5 * poly * bell
    cdf = jnp.where(values < 0, tail, 1.0 - tail)
    return values * cdf, cdf + values * bell * (1.0 / math.sqrt(2.0 * math.pi))


def order_weights(z_size, y_size, order):
    y_weights = [1 << k for k in range(y_size.bit_length() - 1)]
    z_weights = [y_size << k for k in range(z_size.bit_length() - 1)]
    return y_weights + z_weights if order == "y" else z_weights + y_weights


def relative_of(position, weights):
    last = len(weights) - 1
    return sum(w for k, w in enumerate(weights) if (position >> (last - k)) & 1)


def position_of(relative, weights):
    last = len(weights) - 1
    place = jnp.int32(0)
    for k, w in enumerate(weights):
        place = place + jnp.where((relative & w) != 0, 1 << (last - k), 0)
    return place


def choose_rows(info, share, weights, rows, size, width):
    blocks = []
    row = lax.broadcasted_iota(jnp.int32, (rows, width), 0)
    column = lax.broadcasted_iota(jnp.int32, (rows, width), 1)
    for position in range(1 << len(weights)):
        block = info[DP] ^ relative_of(position, weights)
        start = block * size + info[share] * rows
        blocks.append(jnp.where(column == row + start, 1.0, 0.0))
    return jnp.concatenate(blocks, axis=0).astype(BF)


def head_masks(lanes, head):
    lane = lax.broadcasted_iota(jnp.int32, (1, lanes), 1)
    return [(lane >= h * head) & (lane < (h + 1) * head) for h in range(lanes // head)]


def stack_heads(values, masks):
    zero = jnp.zeros_like(values)
    return jnp.concatenate([jnp.where(m, values, zero) for m in masks], axis=0)


def merge_heads(stacked, masks):
    rows = stacked.shape[0] // len(masks)
    total = None
    for h, m in enumerate(masks):
        piece = jnp.where(m, stacked[h * rows : (h + 1) * rows], 0.0)
        total = piece if total is None else total + piece
    return total


def softmax_into(out, scores, tile, scaling, closed=None):
    for r in range(0, scores.shape[0], tile):
        part = scores[r : r + tile] * scaling
        if closed is not None:
            part = part + closed
        top = jnp.max(part, axis=-1, keepdims=True)
        powers = jnp.exp(part - top)
        out[r : r + tile] = (powers / jnp.sum(powers, axis=-1, keepdims=True)).astype(BF)


def softmax_back(probs, grads, tile):
    parts = []
    for r in range(0, grads.shape[0], tile):
        p, dp = probs[r : r + tile].astype(F32), grads[r : r + tile]
        parts.append((p * (dp - jnp.sum(p * dp, axis=-1, keepdims=True))).astype(BF))
    return jnp.concatenate(parts, axis=0)


def whole(shape):
    zeros = (0,) * len(shape)
    return pl.BlockSpec(tuple(shape), lambda *_: zeros)


SCALARS = pl.BlockSpec(memory_space=pltpu.SMEM)


def call(kernel, ins, outs, *, grid=(), in_specs=None, out_specs=None, scratch=(), flops=0, name, after=(), weight=1):
    if in_specs is None:
        in_specs = [None] * len(ins)
    in_specs = [
        spec or (SCALARS if k == 0 else whole(v.shape))
        for k, (spec, v) in enumerate(zip(in_specs, ins))
    ]
    out_shape = [jax.ShapeDtypeStruct(shape, dtype) for shape, dtype in outs]
    if out_specs is None:
        out_specs = [None] * len(outs)
    out_specs = [spec or whole(o.shape) for spec, o in zip(out_specs, out_shape)]
    moved = sum(v.size * v.dtype.itemsize for v in list(ins) + out_shape)
    limit = VMEM_BYTES
    if not grid:
        held = sum(math.prod(v.shape) * jnp.dtype(v.dtype).itemsize for v in scratch)
        limit = min(VMEM_BYTES, moved + held + VMEM_SPARE)
    count = len(ins)

    def body(*refs):
        kernel(*refs[:count], *refs[count + len(after) :])

    return pl.pallas_call(
        body,
        grid=grid,
        in_specs=in_specs + [pl.BlockSpec(memory_space=pl.ANY)] * len(after),
        out_specs=out_specs,
        out_shape=out_shape,
        scratch_shapes=list(scratch),
        compiler_params=pltpu.CompilerParams(vmem_limit_bytes=limit),
        cost_estimate=pl.CostEstimate(
            flops=weight, bytes_accessed=1, transcendentals=0
        ),
        name=name,
    )(*ins, *after)


def words_kernel(info, ids, table, mine, give, total):
    step = pl.program_id(0)
    chunk = table.shape[0]

    @pl.when(step == 0)
    def _():
        total[...] = jnp.zeros_like(total)

    column = lax.broadcasted_iota(jnp.int32, (ids.shape[0], chunk), 1) + step * chunk
    hot = jnp.where(ids[...] == column, 1.0, 0.0).astype(BF)
    total[...] += nn(hot, table[...])

    @pl.when(step == pl.num_programs(0) - 1)
    def _():
        half = total.shape[0] // 2
        mine[...] = total[:half].astype(BF)
        give[...] = total[half:].astype(BF)


def look_up(info, ids, table, chunk=640):
    rows, width = table.shape
    count = ids.shape[0]
    return call(
        words_kernel,
        [info, ids, table],
        [((count // 2, width), BF)] * 2,
        grid=(rows // chunk,),
        in_specs=[None, None, pl.BlockSpec((chunk, width), lambda k: (k, 0))],
        scratch=[pltpu.VMEM((count, width), F32)],
        flops=2 * count * rows * width,
        name="words",
    )


def embed_slab(words, positions, at):
    slots, width = positions.shape
    total = words[0][at].astype(F32)
    for other in words[1:]:
        total = total + other[at].astype(F32)
    start = at.start % slots
    if start + total.shape[0] <= slots:
        return total + positions[start : start + total.shape[0]].astype(F32)
    return (total.reshape(-1, slots, width) + positions[...].astype(F32)[None]).reshape(-1, width)


def self_forward_kernel(
    x_size, weights, share_rows, info, positions, query_tokens, emb_gain, emb_bias, qkv,
    used, out_weight, gain, bias, cross_weight, *rest,
):
    words = rest[:x_size]
    (
        packed, probs, normal_q, normal_t, scale_q, scale_t, cross_q, keep, give, chosen_q, mixed,
        start_rows, query_rows, attended,
    ) = rest[x_size:]
    slots, width = positions.shape
    queries = query_tokens.shape[0]
    rows = queries + slots
    head = width // HEADS
    lanes = GROUP * head
    start_q = normalise(query_tokens[...].astype(F32))[0] * emb_gain[...] + emb_bias[...]
    count = words[0].shape[0]
    items = count // slots
    for at in slabs(count):
        normal, _ = normalise(embed_slab(words, positions, at))
        start_rows[at] = normal * emb_gain[...] + emb_bias[...]
    start_q_low, start_w_low = start_q.astype(BF), start_rows[...].astype(BF)
    both = jnp.concatenate([start_q_low, start_w_low], axis=0)
    for c in range(3):
        span = slice(c * width, (c + 1) * width)
        product = nn(both, qkv[:, span]).astype(BF)
        for i in range(items):
            packed[i * rows : i * rows + queries, span] = product[:queries]
            packed[i * rows + queries : (i + 1) * rows, span] = product[
                queries + i * slots : queries + (i + 1) * slots
            ]
    masks = head_masks(lanes, head)
    pair = 2 * rows
    row_item = lax.broadcasted_iota(jnp.int32, (pair, pair), 0) // rows
    column_item = lax.broadcasted_iota(jnp.int32, (pair, pair), 1) // rows
    for j in range(items // 2):
        closed = jnp.where((row_item == column_item) & (used[j : j + 1] > 0), 0.0, -1e30)
        at = slice(j * pair, (j + 1) * pair)
        for g in range(HEADS // GROUP):
            base = g * lanes
            q = stack_heads(packed[at, base : base + lanes], masks)
            k = packed[at, width + base : width + base + lanes]
            v = packed[at, 2 * width + base : 2 * width + base + lanes]
            p = probs.at[j * (HEADS // GROUP) + g]
            softmax_into(p, nt(q, k), pair, 1.0 / math.sqrt(head), closed)
            mixed[at, base : base + lanes] = merge_heads(nn(p[...], v), masks).astype(BF)
    attended[...] = nn(mixed[...], out_weight[...])
    for i in range(items):
        base = i * rows
        for at in slabs(queries):
            into = slice(i * queries + at.start, i * queries + at.stop)
            normal, scale = normalise(attended[base + at.start : base + at.stop] + start_q[at])
            normal_q[into] = normal
            scale_q[into] = scale
            query_rows[into] = (normal * gain[...] + bias[...]).astype(BF)
        for at in slabs(slots):
            into = slice(i * slots + at.start, i * slots + at.stop)
            start = base + queries + at.start
            normal, scale = normalise(
                attended[start : start + at.stop - at.start] + start_rows[into]
            )
            normal_t[into] = normal
            scale_t[into] = scale
    query_low = query_rows[...]
    cross_q[...] = nn(query_low, cross_weight[...]).astype(BF)
    size = width >> len(weights)
    for share, out in ((SHARE, keep), (PARTNER, give)):
        select = choose_rows(info, share, weights, share_rows, size, width)
        out[:, : items * slots] = nt(select, start_w_low).astype(BF)
        out[:, items * slots : items * (slots + rows)] = nt(select, mixed[...]).astype(BF)
        if share == SHARE:
            chosen_q[...] = nt(select, start_q_low).astype(BF)
        out[:, items * (slots + rows) :] = nt(select, query_low).astype(BF)


def self_forward(info, words, used, p, orders, share_rows):
    slots, width = p["positions"].shape
    queries = p["query_tokens"].shape[0]
    items = words[0].shape[0] // slots
    rows = queries + slots
    blocks = 1 << len(orders["y"])
    units = (items // 2) * (HEADS // GROUP)
    ins = [
        info, p["positions"], p["query_tokens"], p["emb_gain"], p["emb_bias"], p["qkv"], used,
        p["out"], p["self_gain"], p["self_bias"], p["cross_query"], *words,
    ]
    lhs = (blocks * share_rows, items * (slots + rows + queries))
    outs = [
        ((items * rows, 3 * width), BF),
        ((units, GROUP * 2 * rows, 2 * rows), BF),
        ((items * queries, width), F32),
        ((items * slots, width), F32),
        ((items * queries, 1), F32),
        ((items * slots, 1), F32),
        ((items * queries, width), BF),
        (lhs, BF),
        (lhs, BF),
        ((blocks * share_rows, queries), BF),
    ]
    return call(
        functools.partial(self_forward_kernel, len(words), orders["y"], share_rows),
        ins,
        outs,
        scratch=[
            pltpu.VMEM((items * rows, width), BF),
            pltpu.VMEM((items * slots, width), F32),
            pltpu.VMEM((items * queries, width), BF),
            pltpu.VMEM((items * rows, width), F32),
        ],
        flops=2 * items * rows * width * width * 6,
        name="self_forward",
    )


def fill_weights(places, shards, key_full, value_full):
    half = len(shards) // 2
    size = shards[0].shape[0]
    for k in range(half):
        at = pl.ds(pl.multiple_of(places[k] * size, 16), size)
        key_full[at, :] = shards[k][...]
        value_full[at, :] = shards[half + k][...]


def key_value_kernel(pieces, info, places, *rest):
    feats, shards = rest[:pieces], rest[pieces : 3 * pieces]
    keys, values, key_full, value_full = rest[3 * pieces :]
    fill_weights(places, shards, key_full, value_full)
    items, rows, width = feats[0].shape
    for k, piece in enumerate(feats):
        flat = piece[...].reshape(items * rows, width)
        at = slice(k * rows, (k + 1) * rows)
        keys[:, at] = nn(flat, key_full[...]).astype(BF).reshape(items, rows, -1)
        values[:, at] = nn(flat, value_full[...]).astype(BF).reshape(items, rows, -1)


def key_value(info, places, feats, shards, after):
    items, rows, deep = feats[0].shape
    width = shards[0].shape[1]
    pieces = len(feats)
    return call(
        functools.partial(key_value_kernel, pieces),
        [info, places, *feats, *shards],
        [((items, pieces * rows, width), BF)] * 2,
        in_specs=[SCALARS, SCALARS] + [None] * (3 * pieces),
        scratch=[pltpu.VMEM((deep, width), BF)] * 2,
        flops=4 * items * rows * pieces * deep * width,
        name="key_value",
        after=after,
    )


def cross_forward_kernel(
    weights, share_rows, info, cross_q, keys, values, normal_q, self_gain, self_bias,
    out_weight, probs, normal, scale, keep, give, mixed, added,
):
    items, _, width = keys.shape
    queries = cross_q.shape[0] // items
    head = width // HEADS
    lanes = GROUP * head
    masks = head_masks(lanes, head)
    groups = HEADS // GROUP
    for i in range(items):
        at = slice(i * queries, (i + 1) * queries)
        for g in range(groups):
            span = slice(g * lanes, (g + 1) * lanes)
            q = stack_heads(cross_q[at, span], masks)
            p = probs.at[i * groups + g]
            softmax_into(p, nt(q, keys[i, :, span]), 2 * queries, 1.0 / math.sqrt(head))
            mixed[at, span] = merge_heads(nn(p[...], values[i, :, span]), masks).astype(BF)
    added[...] = nn(mixed[...], out_weight[...])
    for at in slabs(added.shape[0]):
        n, s = normalise(added[at] + (normal_q[at] * self_gain[...] + self_bias[...]))
        normal[at] = n
        scale[at] = s
    for share, out in ((SHARE, keep), (PARTNER, give)):
        select = choose_rows(info, share, weights, share_rows, width >> len(weights), width)
        out[...] = nt(select, mixed[...]).astype(BF)


def cross_forward(info, cross_q, keys, values, normal_q, p, orders, share_rows):
    items, all_rows, width = keys.shape
    count = cross_q.shape[0]
    blocks = 1 << len(orders["z"])
    ins = [
        info, cross_q, keys, values, normal_q, p["self_gain"], p["self_bias"], p["cross_out"],
    ]
    outs = [
        ((items * HEADS // GROUP, GROUP * count // items, all_rows), BF),
        ((count, width), F32),
        ((count, 1), F32),
        ((blocks * share_rows, count), BF),
        ((blocks * share_rows, count), BF),
    ]
    return call(
        functools.partial(cross_forward_kernel, orders["y"], share_rows),
        ins,
        outs,
        scratch=[pltpu.VMEM((count, width), BF), pltpu.VMEM((count, width), F32)],
        flops=2 * count * width * width + 4 * count * all_rows * width,
        name="cross_forward",
    )


def ff_forward_kernel(
    weights, share_rows, averaged, info, normal_in, gain_in, bias_in, up, down, gain, bias, proj,
    slope, keep, give, normal, scale, final, raw, rows_low, total, inner, active_low,
):
    step = pl.program_id(0)
    blocks = 1 << len(weights)
    count, width = normal_in.shape
    chunk = up.shape[1]
    deep = 4 * share_rows
    size = 4 * width // blocks

    @pl.when(step == 0)
    def _():
        for at in slabs(count):
            rows = normal_in[at] * gain_in[...] + bias_in[...]
            rows_low[at] = rows.astype(BF)
            total[at] = rows
        for share, out in ((SHARE, keep), (PARTNER, give)):
            select = choose_rows(info, share, weights, share_rows, width // blocks, width)
            out[: blocks * share_rows] = nt(select, rows_low[...]).astype(BF)

    inner[...] = nn(rows_low[...], up[...])
    for at in slabs(count):
        for c in range(0, chunk, 256):
            value, slant = gelu_both(inner[at, c : c + 256])
            active_low[at, c : c + 256] = value.astype(BF)
            slope[at, c : c + 256] = slant.astype(BF)
    active = active_low[...]
    total[...] += nn(active, down[...])
    each = chunk // size
    row = lax.broadcasted_iota(jnp.int32, (deep, chunk), 0)
    column = lax.broadcasted_iota(jnp.int32, (deep, chunk), 1)
    for share, out in ((SHARE, keep), (PARTNER, give)):
        select = [
            jnp.where(column == row + (j * size + info[share] * deep), 1.0, 0.0)
            for j in range(each)
        ]
        picked = nt(jnp.concatenate(select, axis=0).astype(BF), active).astype(BF)
        for j in range(each):
            block = step * each + j
            place = position_of(block ^ info[DP], weights)
            at = pl.multiple_of(blocks * share_rows + place * deep, 16)
            out[pl.ds(at, deep), :] = picked[j * deep : (j + 1) * deep]

    @pl.when(step == pl.num_programs(0) - 1)
    def _():
        for at in slabs(count):
            n, s = normalise(total[at])
            normal[at] = n
            scale[at] = s
            final[at] = (n * gain[...] + bias[...]).astype(BF)
        low = final[...]
        items = raw.shape[0]
        if averaged:
            image = nn(low, proj[...]).reshape(items, count // items, -1)
            raw[...] = jnp.mean(image, axis=1)
        else:
            heads = jnp.concatenate(
                [low[i * (count // items) : i * (count // items) + 16] for i in range(items)], axis=0
            )
            text = nn(heads, proj[...]).reshape(items, 16, -1)
            raw[...] = text[:, 0]


def ff_forward(info, normal_in, gain_in, bias_in, names, p, weights, share_rows, items, averaged):
    up, down, gain, bias, proj = (p[k] for k in names)
    count, width = normal_in.shape
    inner = up.shape[1]
    chunk = width
    blocks = 1 << len(weights)
    lhs = (blocks * share_rows * 5, count)
    return call(
        functools.partial(ff_forward_kernel, weights, share_rows, averaged),
        [info, normal_in, gain_in, bias_in, up, down, gain, bias, proj],
        [
            ((count, inner), BF),
            (lhs, BF),
            (lhs, BF),
            ((count, width), F32),
            ((count, 1), F32),
            ((count, width), BF),
            ((items, proj.shape[1]), F32),
        ],
        grid=(inner // chunk,),
        in_specs=[None] * 4
        + [
            pl.BlockSpec((width, chunk), lambda k: (0, k)),
            pl.BlockSpec((chunk, width), lambda k: (k, 0)),
        ]
        + [None] * 3,
        out_specs=[pl.BlockSpec((count, chunk), lambda k: (0, k))] + [None] * 6,
        scratch=[
            pltpu.VMEM((count, width), BF),
            pltpu.VMEM((count, width), F32),
            pltpu.VMEM((count, chunk), F32),
            pltpu.VMEM((count, chunk), BF),
        ],
        flops=4 * count * width * inner,
        name="ff_forward",
    )


def ff_backward_kernel(
    averaged, info, incoming, extra, proj, normal, scale, gain, slope, up, down,
    rhs, grad_rows, vectors, added, outer, total,
):
    step = pl.program_id(0)
    count, width = normal.shape
    chunk = slope.shape[1]

    @pl.when(step == 0)
    def _():
        items = extra.shape[0] // 2
        each = count // items
        added[...] = nt(extra[...], proj[...])

        def grad_of(at):
            grad = incoming[at.start // each, at.start % each : at.start % each + SLAB].astype(F32)
            more = added[at.start // each : at.start // each + 1]
            if averaged:
                return grad + more
            row = lax.broadcasted_iota(jnp.int32, (SLAB, 1), 0) + at.start % each
            return grad + jnp.where(row == 0, more, 0.0)

        def put(at, grad_in):
            total[at] = grad_in
            outer[at] = grad_in.astype(BF)
            rhs[at, pl.num_programs(0) * chunk :] = grad_in.astype(BF)

        grads = norm_back_rows(grad_of, normal, scale, gain, put)
        vectors[...] = jnp.concatenate(grads, axis=0)

    inner = (nt(outer[...], down[...]) * slope[...].astype(F32)).astype(BF)
    rhs[:, pl.ds(pl.multiple_of(step * chunk, 128), chunk)] = inner
    total[...] += nt(inner, up[...])

    @pl.when(step == pl.num_programs(0) - 1)
    def _():
        grad_rows[...] = total[...]


def ff_backward(info, incoming, part_of, extra, state, names, p, averaged, after=()):
    up, down, gain, proj = (p[k] for k in names)
    slope, normal, scale = state
    count, width = normal.shape
    items = extra.shape[0] // 2
    inner = up.shape[1]
    chunk = width
    each = count // items
    gs = pltpu.PrefetchScalarGridSpec(
        num_scalar_prefetch=1,
        grid=(inner // chunk,),
        in_specs=[
            pl.BlockSpec((items, each, width), lambda k, info: (info[CORE], part_of, 0)),
            whole(extra.shape),
            whole(proj.shape),
            whole(normal.shape),
            whole(scale.shape),
            whole(gain.shape),
            pl.BlockSpec((count, chunk), lambda k, info: (0, k)),
            pl.BlockSpec((width, chunk), lambda k, info: (0, k)),
            pl.BlockSpec((chunk, width), lambda k, info: (k, 0)),
        ]
        + [pl.BlockSpec(memory_space=pl.ANY)] * len(after),
        out_specs=[whole((count, inner + width)), whole((count, width)), whole((2, width))],
        scratch_shapes=[
            pltpu.VMEM((2 * items, width), F32),
            pltpu.VMEM((count, width), BF),
            pltpu.VMEM((count, width), F32),
        ],
    )

    def body(*refs):
        ff_backward_kernel(averaged, *refs[:10], *refs[10 + len(after) :])

    return pl.pallas_call(
        body,
        grid_spec=gs,
        out_shape=[
            jax.ShapeDtypeStruct((count, inner + width), BF),
            jax.ShapeDtypeStruct((count, width), F32),
            jax.ShapeDtypeStruct((2, width), F32),
        ],
        compiler_params=pltpu.CompilerParams(vmem_limit_bytes=VMEM_BYTES),
        cost_estimate=pl.CostEstimate(
            flops=1, bytes_accessed=1, transcendentals=0
        ),
        name="ff_backward",
    )(info, incoming, extra, proj, normal, scale, gain, slope, up, down, *after)


def ff_weights_kernel(share_rows, blocks, info, lhs_a, lhs_b, rhs_a, rhs_b, keep, give, total):
    width = keep.shape[2]
    inner = rhs_a.shape[1] - width
    first = blocks * share_rows
    for c in range(inner // width):
        span = slice(c * width, (c + 1) * width)
        part = nn(lhs_a[:first], rhs_a[:, span]) + nn(lhs_b[:first], rhs_b[:, span])
        for b in range(blocks):
            total[b, c * share_rows : (c + 1) * share_rows] = part[
                b * share_rows : (b + 1) * share_rows
            ]
    deep = 4 * share_rows
    down = nn(lhs_a[first:], rhs_a[:, inner:]) + nn(lhs_b[first:], rhs_b[:, inner:])
    for b in range(blocks):
        out, at = (keep, b) if b < blocks // 2 else (give, b - blocks // 2)
        out[at, :deep] = total[b].astype(BF)
        out[at, deep:] = down[b * deep : (b + 1) * deep].astype(BF)


def ff_weights(info, lhs_a, lhs_b, rhs_a, rhs_b, share_rows, blocks, width, after):
    deep = 4 * share_rows
    out = ((blocks // 2, 2 * deep, width), BF)
    return call(
        functools.partial(ff_weights_kernel, share_rows, blocks),
        [info, lhs_a, lhs_b, rhs_a, rhs_b],
        [out, out],
        scratch=[pltpu.VMEM((blocks, deep, width), F32)],
        flops=4 * lhs_a.size * 4 * width,
        name="ff_weights",
        after=after,
    )


def log_sum(values, axis):
    top = jnp.max(values, axis=axis, keepdims=True)
    return top + jnp.log(jnp.sum(jnp.exp(values - top), axis=axis, keepdims=True))


def contrast_kernel(
    queries, slots, info, gathered, sharpness, loss, grad_image, grad_text, grad_sharp,
    all_loss, all_image, all_text,
):
    count = gathered.shape[0]
    emb = grad_image.shape[1]
    image_raw, text_raw = gathered[:, :emb], gathered[:, emb : 2 * emb]
    ids = gathered[:, 2 * emb :]
    pairs = ids[:, slots : slots + 1].astype(jnp.int32)
    pairs_row = ids.T[slots : slots + 1].astype(jnp.int32)
    image_scale = lax.rsqrt(jnp.sum(image_raw * image_raw, axis=1, keepdims=True) + 1e-06)
    text_scale = lax.rsqrt(jnp.sum(text_raw * text_raw, axis=1, keepdims=True) + 1e-06)
    image, text = image_raw * image_scale, text_raw * text_scale
    sharp = sharpness[...]
    factor = 1.0 / jnp.clip(sharp, 0.04, 0.5)
    inside = jnp.where((sharp >= 0.04) & (sharp <= 0.5), 1.0, 0.0)
    by_image = exact(image, text, ((1,), (1,))) * factor
    by_text = exact(text, image, ((1,), (1,))) * factor
    row, row_flat = log_sum(by_image, 1), log_sum(by_text, 0)
    column, column_flat = log_sum(by_text, 1), log_sum(by_image, 0)
    down = lax.broadcasted_iota(jnp.int32, (count, count), 0)
    across = lax.broadcasted_iota(jnp.int32, (count, count), 1)
    match = jnp.where(across == pairs, 1.0, 0.0)
    match_text = jnp.where(down == pairs_row, 1.0, 0.0)
    pull = 0.5 * (jnp.exp(by_image - row) + jnp.exp(by_image - column_flat)) - match
    pull_text = 0.5 * (jnp.exp(by_text - column) + jnp.exp(by_text - row_flat)) - match_text
    positive = jnp.sum(match * by_image, axis=1, keepdims=True)
    all_loss[...] = 0.5 * (row + column) - positive
    share = jnp.sum(jnp.sum(pull * by_image, axis=1, keepdims=True), axis=0, keepdims=True)
    grad_sharp[...] = -factor * inside * share
    toward_image = exact(pull, text, ((1,), (0,))) * factor
    toward_text = exact(pull_text, image, ((1,), (0,))) * factor
    all_image[...] = (
        image_scale
        * (toward_image - image * jnp.sum(image * toward_image, axis=1, keepdims=True))
        * (1.0 / queries)
    )
    all_text[...] = text_scale * (
        toward_text - text * jnp.sum(text * toward_text, axis=1, keepdims=True)
    )
    group = loss.shape[0]
    items = group // CORES
    base = info[DP] * group
    loss[...] = all_loss[pl.ds(pl.multiple_of(base, 8), group), :]
    mine = pl.ds(pl.multiple_of(base + info[CORE] * items, 8), items)
    theirs = pl.ds(pl.multiple_of(base + (1 - info[CORE]) * items, 8), items)
    grad_image[...] = jnp.concatenate([all_image[mine, :], all_image[theirs, :]], axis=0).astype(BF)
    grad_text[...] = jnp.concatenate([all_text[mine, :], all_text[theirs, :]], axis=0).astype(BF)


def contrast(info, gathered, sharpness, queries, slots, group, emb, after):
    count = gathered.shape[0]
    return call(
        functools.partial(contrast_kernel, queries, slots),
        [info, gathered, sharpness],
        [((group, 1), F32), ((group, emb), BF), ((group, emb), BF), ((1, 1), F32)],
        scratch=[
            pltpu.VMEM((count, 1), F32),
            pltpu.VMEM((count, emb), F32),
            pltpu.VMEM((count, emb), F32),
        ],
        flops=50 * count * count * emb,
        name="contrast",
        after=after,
    )


def cross_backward_kernel(
    info, grad_second, normal, scale, gain, out_weight, keys, values, probs, cross_q, cross_weight,
    rhs, grad_keys, grad_values, grad_query, vectors, grad_heads,
):
    items, _, width = keys.shape
    queries = cross_q.shape[0] // items
    head = width // HEADS
    lanes = GROUP * head
    scaling = 1.0 / math.sqrt(head)
    masks = head_masks(lanes, head)
    groups = HEADS // GROUP

    def put(at, grad_in):
        grad_query[at] = grad_in
        rhs[at, width:] = grad_in.astype(BF)

    grads = norm_back_rows(lambda at: grad_second[at], normal, scale, gain, put)
    vectors[...] = jnp.concatenate(grads, axis=0)
    grad_heads[...] = nt(rhs[:, width:], out_weight[...]).astype(BF)
    for i in range(items):
        at = slice(i * queries, (i + 1) * queries)
        for g in range(groups):
            span = slice(g * lanes, (g + 1) * lanes)
            dm = stack_heads(grad_heads[at, span], masks)
            q = stack_heads(cross_q[at, span], masks)
            p_low = probs[i * groups + g]
            ds = softmax_back(p_low, nt(dm, values[i, :, span]), 2 * queries)
            rhs[at, span] = (merge_heads(nn(ds, keys[i, :, span]), masks) * scaling).astype(BF)
            grad_keys[i, :, span] = (tn(ds, q) * scaling).astype(BF)
            grad_values[i, :, span] = tn(p_low, dm).astype(BF)
    grad_query[...] += nt(rhs[:, :width], cross_weight[...])


def cross_backward(info, grad_second, normal, scale, keys, values, probs, cross_q, p, after):
    items, all_rows, width = keys.shape
    count = cross_q.shape[0]
    return call(
        cross_backward_kernel,
        [
            info, grad_second, normal, scale, p["cross_gain"], p["cross_out"], keys, values, probs,
            cross_q, p["cross_query"],
        ],
        [
            ((count, 2 * width), BF),
            (keys.shape, BF),
            (keys.shape, BF),
            ((count, width), F32),
            ((2, width), F32),
        ],
        scratch=[pltpu.VMEM((count, width), BF)],
        flops=4 * count * width * width + 8 * count * all_rows * width,
        name="cross_backward",
        after=after,
    )


def features_kernel(pieces, info, places, grad_keys, grad_values, *rest):
    shards = rest[: 2 * pieces]
    mine, give, key_full, value_full = rest[2 * pieces :]
    fill_weights(places, shards, key_full, value_full)
    items, rows, deep = mine.shape
    for k, out in enumerate((mine, give)):
        at = slice(k * rows, (k + 1) * rows)
        grad = nt(grad_keys[:, at].reshape(items * rows, -1), key_full[...])
        grad = grad + nt(grad_values[:, at].reshape(items * rows, -1), value_full[...])
        out[...] = grad.reshape(items, rows, deep).astype(out.dtype)


def features_back(info, places, grad_keys, grad_values, shards, rows, after):
    items, _, width = grad_keys.shape
    pieces = len(shards) // 2
    deep = shards[0].shape[0] * pieces
    return call(
        functools.partial(features_kernel, pieces),
        [info, places, grad_keys, grad_values, *shards],
        [((items, rows, deep), F32), ((items, rows, deep), BF)],
        in_specs=[SCALARS, SCALARS] + [None] * (2 + len(shards)),
        scratch=[pltpu.VMEM((deep, width), BF)] * 2,
        flops=8 * items * rows * deep * width,
        name="features_back",
        after=after,
    )


def kv_weights_kernel(pieces, weights, cuts, info, grad_keys, grad_values, *rest):
    feats = rest[:pieces]
    keep, give, total, blocks = rest[pieces:]
    items, rows, deep = feats[0].shape
    width = grad_keys.shape[2]
    size = total.shape[0]
    row = lax.broadcasted_iota(jnp.int32, (size, deep), 0)
    column = lax.broadcasted_iota(jnp.int32, (size, deep), 1)
    for which, out in ((MEMBER, keep), (OTHER, give)):
        select = jnp.where(column == row + info[which] * size, 1.0, 0.0).astype(BF)
        for k, piece in enumerate(feats):
            at = slice(k * rows, (k + 1) * rows)
            picked = nt(select, piece[...].reshape(items * rows, deep)).astype(BF)
            part_k = nn(picked, grad_keys[:, at].reshape(items * rows, width))
            part_v = nn(picked, grad_values[:, at].reshape(items * rows, width))
            if k == 0:
                total[:, :width] = part_k
                total[:, width:] = part_v
            else:
                total[:, :width] += part_k
                total[:, width:] += part_v
        height, span = size // cuts[0], 2 * width // cuts[1]
        for a in range(cuts[0]):
            for b in range(cuts[1]):
                blocks[a * cuts[1] + b] = total[
                    a * height : (a + 1) * height, b * span : (b + 1) * span
                ].astype(BF)
        for position in range(cuts[0] * cuts[1]):
            if cuts[0] * cuts[1] == 1:
                out[0] = blocks[0]
            else:
                out[position] = blocks[info[DP] ^ relative_of(position, weights)]


def kv_weights(info, grad_keys, grad_values, feats, weights, size, cuts, after):
    width = grad_keys.shape[2]
    items, rows, deep = feats[0].shape
    blocks = (cuts[0] * cuts[1], size // cuts[0], 2 * width // cuts[1])
    return call(
        functools.partial(kv_weights_kernel, len(feats), weights, cuts),
        [info, grad_keys, grad_values, *feats],
        [(blocks, BF), (blocks, BF)],
        scratch=[pltpu.VMEM((size, 2 * width), F32), pltpu.VMEM(blocks, BF)],
        flops=4 * size * items * rows * len(feats) * (deep + 2 * width),
        name="kv_weights",
        after=after,
    )


def self_backward_kernel(
    x_size, info, grad_query, grad_text, normal_q, normal_t, scale_q, scale_t, gain, out_weight,
    packed, probs, positions, query_tokens, emb_gain, qkv, more, *rest,
):
    words = rest[:x_size]
    rhs, words_low, grad_mixed, attended, grad_packed, in_q, in_t = rest[x_size:]
    slots, width = positions.shape
    queries = query_tokens.shape[0]
    rows = queries + slots
    items = grad_text.shape[0] // slots
    count = items * slots
    head = width // HEADS
    lanes = GROUP * head
    scaling = 1.0 / math.sqrt(head)
    masks = head_masks(lanes, head)
    groups = HEADS // GROUP

    def put_rows(into, each, offset):
        def put(at, grad_in):
            into[at] = grad_in
            start = at.start // each * rows + offset + at.start % each
            attended[start : start + SLAB] = grad_in.astype(BF)

        return put

    gain_q, bias_q = norm_back_rows(
        lambda at: grad_query[at], normal_q, scale_q, gain, put_rows(in_q, queries, 0)
    )
    gain_t, bias_t = norm_back_rows(
        lambda at: grad_text[at], normal_t, scale_t, gain, put_rows(in_t, slots, queries)
    )
    half = items * rows // 2
    rhs[:half, 3 * width : 4 * width] = attended[:half]
    rhs[:half, 4 * width :] = attended[half:]
    grad_mixed[...] = nt(attended[...], out_weight[...]).astype(BF)
    pair = 2 * rows
    for j in range(items // 2):
        at = slice(j * pair, (j + 1) * pair)
        for g in range(groups):
            base = g * lanes
            q = stack_heads(packed[at, base : base + lanes], masks)
            k = packed[at, width + base : width + base + lanes]
            v = packed[at, 2 * width + base : 2 * width + base + lanes]
            dm = stack_heads(grad_mixed[at, base : base + lanes], masks)
            p_low = probs[j * groups + g]
            ds = softmax_back(p_low, nt(dm, v), pair)
            grad_packed[at, base : base + lanes] = (
                merge_heads(nn(ds, k), masks) * scaling
            ).astype(BF)
            grad_packed[at, width + base : width + base + lanes] = (tn(ds, q) * scaling).astype(BF)
            grad_packed[at, 2 * width + base : 2 * width + base + lanes] = tn(p_low, dm).astype(BF)
    total_q = None
    for i in range(items):
        piece = grad_packed[i * rows : i * rows + queries].astype(F32)
        total_q = piece if total_q is None else total_q + piece
        rhs[i * slots : (i + 1) * slots, : 3 * width] = grad_packed[
            i * rows + queries : (i + 1) * rows
        ]
    total_q = total_q.astype(BF)
    rhs[count : count + queries, : 3 * width] = total_q
    in_t[...] += nt(rhs[:count, : 3 * width], qkv[...])
    start_q = jnp.sum(in_q[...].reshape(items, queries, width), axis=0) + nt(total_q, qkv[...])
    normal_e, scale_e = normalise(query_tokens[...].astype(F32))
    grad_tokens, gain_e, bias_e = norm_back(start_q, normal_e, scale_e, emb_gain[...])
    gain_w, bias_w = gain_e, bias_e
    position_grad = None
    for at in slabs(count):
        normal_w, scale_w = normalise(embed_slab(words, positions, at))
        grad_words, part_gain, part_bias = norm_back(in_t[at], normal_w, scale_w, emb_gain[...])
        gain_w, bias_w = gain_w + part_gain, bias_w + part_bias
        words_low[at] = grad_words.astype(BF)
        position_grad = grad_words if position_grad is None else position_grad + grad_words
    rhs[count : count + queries, 3 * width : 4 * width] = grad_tokens.astype(BF)
    rhs[count : count + slots, 4 * width :] = position_grad.astype(BF)
    gain_w = jnp.sum(gain_w, axis=0, keepdims=True)
    bias_w = jnp.sum(bias_w, axis=0, keepdims=True)
    vectors = jnp.concatenate(
        [gain_w, bias_w, gain_q + gain_t, bias_q + bias_t]
        + [more[...], jnp.zeros((6, width), F32)],
        axis=0,
    )
    rhs[count + queries :, :width] = vectors.astype(BF)
    rhs[count + queries :, width:] = jnp.zeros((16, 4 * width), BF)


def self_backward(info, grad_query, grad_text, state, packed, probs, words, more, p, after):
    normal_q, normal_t, scale_q, scale_t = state
    slots, width = p["positions"].shape
    queries = p["query_tokens"].shape[0]
    items = words[0].shape[0] // slots
    rows = queries + slots
    count = items * slots
    ins = [
        info, grad_query, grad_text, normal_q, normal_t, scale_q, scale_t, p["self_gain"],
        p["out"], packed, probs, p["positions"], p["query_tokens"], p["emb_gain"], p["qkv"], more,
        *words,
    ]
    return call(
        functools.partial(self_backward_kernel, len(words)),
        ins,
        [((count + queries + 16, 5 * width), BF), ((count, width), BF)],
        scratch=[
            pltpu.VMEM((items * rows, width), BF),
            pltpu.VMEM((items * rows, width), BF),
            pltpu.VMEM((items * rows, 3 * width), BF),
            pltpu.VMEM((items * queries, width), F32),
            pltpu.VMEM((count, width), F32),
        ],
        flops=2 * items * rows * width * width * 7,
        name="self_backward",
        after=after,
    )


def spread_rows(grads, each, first_only):
    items, emb = grads.shape
    wide = jnp.broadcast_to(grads[:, None, :], (items, each, emb))
    if first_only:
        row = lax.broadcasted_iota(jnp.int32, (items, each, emb), 1)
        wide = jnp.where(row == 0, wide, 0.0)
    return wide.reshape(items * each, emb).astype(BF)


def mid_weights_kernel(
    weights, share_rows, info, query_a, query_b, mixed_a, mixed_b, rhs_a, rhs_b, final_a, final_b,
    text_a, text_b, grad_image, grad_text, out,
):
    count, width = final_a.shape
    items = grad_image.shape[0] // 2
    each = count // items
    blocks = 1 << len(weights)
    cross_q = nn(query_a[...], rhs_a[:, :width]) + nn(query_b[...], rhs_b[:, :width])
    cross_out = nn(mixed_a[...], rhs_a[:, width:]) + nn(mixed_b[...], rhs_b[:, width:])
    select = choose_rows(info, SHARE, weights, share_rows, width // blocks, width)
    image, text = grad_image[...].astype(F32), grad_text[...].astype(F32)
    proj_i = proj_t = None
    for k, (final, first) in enumerate(((final_a, text_a), (final_b, text_b))):
        at = slice(k * items, (k + 1) * items)
        part_i = nn(nt(select, final[...]).astype(BF), spread_rows(image[at], each, False))
        part_t = nn(nt(select, first[...]).astype(BF), spread_rows(text[at], each, True))
        proj_i = part_i if proj_i is None else proj_i + part_i
        proj_t = part_t if proj_t is None else proj_t + part_t
    top = jnp.concatenate([cross_q, proj_i], axis=1)
    low = jnp.concatenate([cross_out, proj_t], axis=1)
    for b in range(blocks):
        rows = slice(b * share_rows, (b + 1) * share_rows)
        out[b] = jnp.concatenate([top[rows], low[rows]], axis=0).astype(BF)


def mid_weights(
    info, query, mixed, rhs, final, text, grad_image, grad_text, weights, share_rows, after
):
    width = final[0].shape[1]
    emb = grad_image.shape[1]
    blocks = 1 << len(weights)
    out = ((blocks, 2 * share_rows, width + emb), BF)
    at = query[0].shape[1] - final[0].shape[0]
    lhs_spec = pl.BlockSpec(
        (query[0].shape[0], final[0].shape[0]), lambda *_: (0, at // final[0].shape[0])
    )
    return call(
        functools.partial(mid_weights_kernel, weights, share_rows),
        [info, *query, *mixed, *rhs, *final, *text, grad_image, grad_text],
        [out],
        grid=(1,),
        in_specs=[None, lhs_spec, lhs_spec] + [None] * 10,
        flops=4 * query[0].shape[0] * final[0].shape[0] * 4 * width,
        name="mid_weights",
        after=after,
        weight=10**11,
    )[0]


def last_weights_kernel(
    weights, share_rows, info, chosen_q, lhs_a, lhs_b, rhs_a, rhs_b, mid, keep, give
):
    width = rhs_a.shape[1] // 5
    blocks = 1 << len(weights)
    queries = chosen_q.shape[1]
    count = rhs_a.shape[0] - queries - 16
    select = choose_rows(info, SHARE, weights, share_rows, width // blocks, width)
    summed_q = (
        rhs_a[count : count + queries, : 3 * width].astype(F32)
        + rhs_b[count : count + queries, : 3 * width].astype(F32)
    ).astype(BF)
    qkv = nn(chosen_q[...], summed_q)
    out_grad = vector_grad = None
    for lhs, rhs in ((lhs_a, rhs_a), (lhs_b, rhs_b)):
        qkv = qkv + nn(lhs[:, :count], rhs[:count, : 3 * width])
        part = nn(lhs[:, count : 2 * count], rhs[:count, 3 * width : 4 * width])
        part = part + nn(lhs[:, 2 * count : 3 * count], rhs[:count, 4 * width :])
        out_grad = part if out_grad is None else out_grad + part
        rows = jnp.concatenate(
            [
                rhs[count : count + queries, 3 * width : 4 * width],
                rhs[count : count + queries, 4 * width :],
                rhs[count + queries :, :width],
                jnp.zeros((128 - 2 * queries - 16, width), BF),
            ],
            axis=0,
        )
        part = nt(select, rows)
        vector_grad = part if vector_grad is None else vector_grad + part
    split = 2 * width
    top = jnp.concatenate([qkv[:, :split], vector_grad], axis=1)
    low = jnp.concatenate([qkv[:, split:], out_grad, jnp.zeros_like(vector_grad)], axis=1)
    base = mid.shape[2]
    for b in range(blocks):
        out, at = (keep, b) if b < blocks // 2 else (give, b - blocks // 2)
        rows = slice(b * share_rows, (b + 1) * share_rows)
        out[at, :, :base] = mid[b]
        out[at, :, base:] = jnp.concatenate([top[rows], low[rows]], axis=0).astype(BF)


def last_weights(info, chosen_q, lhs, rhs, mid, weights, share_rows, after):
    width = rhs[0].shape[1] // 5
    blocks = 1 << len(weights)
    out = ((blocks // 2, 2 * share_rows, mid.shape[2] + 2 * width + 128), BF)
    return call(
        functools.partial(last_weights_kernel, weights, share_rows),
        [info, chosen_q, *lhs, *rhs, mid],
        [out, out],
        flops=4 * chosen_q.shape[0] * 256 * 6 * width,
        name="last_weights",
        after=after,
    )


def ff_assemble_kernel(pieces, share_rows, info, places, *rest):
    parts = rest[:pieces]
    outs = rest[pieces:]
    width = parts[0].shape[1]
    deep = 4 * share_rows
    for k, piece in enumerate(parts):
        for f in range(2):
            up, down = outs[2 * f : 2 * f + 2]
            base = f * 2 * deep
            grad = piece[base : base + deep].astype(F32)
            at = pl.ds(pl.multiple_of(places[k] * share_rows, 8), share_rows)
            for c in range(4):
                up[at, c * width : (c + 1) * width] = grad[c * share_rows : (c + 1) * share_rows]
            at = pl.ds(pl.multiple_of(places[k] * deep, 8), deep)
            down[at, :] = piece[base + deep : base + 2 * deep].astype(F32)


def ff_assemble(info, places, parts, share_rows):
    width = parts[0].shape[1]
    rows = share_rows * len(parts)
    shapes = [((rows, 4 * width), F32), ((4 * rows, width), F32)] * 2
    return call(
        functools.partial(ff_assemble_kernel, len(parts), share_rows),
        [info, places, *parts],
        shapes,
        in_specs=[SCALARS, SCALARS] + [None] * len(parts),
        name="ff_assemble",
    )


def tail_assemble_kernel(pieces, share_rows, queries, info, places, *rest):
    parts = rest[:pieces]
    qkv, out, cross_q, cross_out, image, text, tokens, slots, vectors, spread = rest[pieces:]
    width = out.shape[1]
    emb = image.shape[1]
    spread[...] = jnp.zeros_like(spread)
    for k, piece in enumerate(parts):
        at = pl.ds(pl.multiple_of(places[k] * share_rows, 8), share_rows)
        grad = piece[...].astype(F32)
        top, low = grad[:share_rows], grad[share_rows:]
        cross_q[at, :] = top[:, :width]
        image[at, :] = top[:, width : width + emb]
        cross_out[at, :] = low[:, :width]
        text[at, :] = low[:, width : width + emb]
        base = width + emb
        qkv[at, : 2 * width] = top[:, base : base + 2 * width]
        spread[at, :] = top[:, base + 2 * width :]
        qkv[at, 2 * width :] = low[:, base : base + width]
        out[at, :] = low[:, base + width : base + 2 * width]
    flipped = spread[...].T
    rows = out.shape[0]
    tokens[...] = flipped[:queries, :rows]
    slots[...] = flipped[queries : 2 * queries, :rows]
    vectors[...] = flipped[2 * queries : 2 * queries + 16, :rows]


def tail_assemble(info, places, parts, share_rows, width, emb, queries):
    rows = share_rows * len(parts)
    shapes = [
        ((rows, 3 * width), F32),
        ((rows, width), F32),
        ((rows, width), F32),
        ((rows, width), F32),
        ((rows, emb), F32),
        ((rows, emb), F32),
        ((queries, rows), F32),
        ((queries, rows), F32),
        ((16, rows), F32),
    ]
    return call(
        functools.partial(tail_assemble_kernel, len(parts), share_rows, queries),
        [info, places, *parts],
        shapes,
        in_specs=[SCALARS, SCALARS] + [None] * len(parts),
        scratch=[pltpu.VMEM((128, 128), F32)],
        name="tail_assemble",
    )


def kv_assemble_kernel(count, weights, cuts, info, *rest):
    parts = rest[:count]
    key, value, blocks = rest[count:]
    at = 0
    for piece in parts:
        for b in range(piece.shape[0]):
            blocks[info[DP] ^ relative_of(at, weights)] = piece[b].astype(F32)
            at += 1
    height, span = blocks.shape[1:]
    width = key.shape[1]
    for a in range(cuts[0]):
        for b in range(cuts[1]):
            out = key if b * span < width else value
            base = b * span % width
            out[a * height : (a + 1) * height, base : base + span] = blocks[a * cuts[1] + b]


def kv_assemble(info, parts, weights, cuts, width):
    height, span = parts[0].shape[1:]
    shape = ((height * cuts[0], width), F32)
    return call(
        functools.partial(kv_assemble_kernel, len(parts), weights, cuts),
        [info, *parts],
        [shape, shape],
        scratch=[pltpu.VMEM((cuts[0] * cuts[1], height, span), F32)],
        name="kv_assemble",
    )


def features_assemble_kernel(info, mine, theirs, out):
    @pl.when(pl.program_id(0) == info[CORE])
    def _():
        out[...] = mine[...]

    @pl.when(pl.program_id(0) != info[CORE])
    def _():
        out[...] = theirs[...].astype(F32)


def features_assemble(info, mine, theirs):
    items, rows, deep = mine.shape
    return call(
        features_assemble_kernel,
        [info, mine, theirs],
        [((CORES * items, rows, deep), F32)],
        grid=(CORES,),
        out_specs=[pl.BlockSpec((items, rows, deep), lambda k: (k, 0, 0))],
        name="features_assemble",
    )[0]


def hidden_assemble_kernel(info, query_a, text_a, query_b, text_b, out):
    items = out.shape[0]
    queries = query_a.shape[0] // items
    mine = pl.program_id(0) == info[CORE]

    def put(query, text):
        out[:, :queries] = query[...].reshape(items, queries, -1)
        out[:, queries:] = text[...].reshape(items, -1, out.shape[2])

    @pl.when(mine)
    def _():
        put(query_a, text_a)

    @pl.when(jnp.logical_not(mine))
    def _():
        put(query_b, text_b)


def hidden_assemble(info, query_a, text_a, query_b, text_b, items):
    width = query_a.shape[1]
    rows = (query_a.shape[0] + text_a.shape[0]) // items
    return call(
        hidden_assemble_kernel,
        [info, query_a, text_a, query_b, text_b],
        [((CORES * items, rows, width), BF)],
        grid=(CORES,),
        out_specs=[pl.BlockSpec((items, rows, width), lambda k: (k, 0, 0))],
        name="hidden_assemble",
    )[0]


def slots_kernel(
    table_rows, patch_size, info, tokens, slot_of, rows_of, most
):
    groups, count = tokens.shape
    here_from = info[MEMBER] * table_rows
    all_rows = tokens[...]
    flipped = all_rows.T
    place = lax.broadcasted_iota(jnp.int32, (groups, count), 1)
    step = math.gcd(count, 64)
    down = lax.broadcasted_iota(jnp.int32, (step, count), 0)

    def over_slabs(d, make, combine):
        total = None
        for r in range(0, count, step):
            part = make(d, r)
            total = part if total is None else combine(total, part)
        return total

    def first_of(d, r):
        same = flipped[r : r + step, d : d + 1] == all_rows[d : d + 1]
        return jnp.min(jnp.where(same, down + r, count), axis=0, keepdims=True)

    first = jnp.concatenate(
        [over_slabs(d, first_of, jnp.minimum) for d in range(groups)], axis=0
    )
    here = (all_rows >= here_from) & (all_rows < here_from + table_rows)
    lead = first == place
    leads = jnp.where(lead & here, 1, 0).T

    def ahead_of(d, r):
        ahead = jnp.where(down + r < first[d : d + 1], leads[r : r + step, d : d + 1], 0)
        return jnp.sum(ahead, axis=0, keepdims=True)

    slot = jnp.concatenate([over_slabs(d, ahead_of, jnp.add) for d in range(groups)], axis=0)
    slot = jnp.where(here, slot, -1)
    slot_of[...] = slot
    slot_down = slot.T
    slot_iota = lax.broadcasted_iota(jnp.int32, (step, SLOTS), 1)

    def row_of(d, r):
        hit = slot_down[r : r + step, d : d + 1] == slot_iota
        local = flipped[r : r + step, d : d + 1] - here_from
        return jnp.max(jnp.where(hit, local, -1), axis=0, keepdims=True)

    for d in range(groups):
        rows_of[:, d * SLOTS : (d + 1) * SLOTS] = over_slabs(d, row_of, jnp.maximum)
    top = jnp.zeros((1, 1), jnp.int32)
    for q in range(patch_size):
        within = lead & (all_rows >= q * table_rows) & (all_rows < (q + 1) * table_rows)
        each = jnp.sum(jnp.where(within, 1, 0), axis=1, keepdims=True)
        top = jnp.maximum(top, jnp.max(each, axis=0, keepdims=True))
    most[...] = top


def slots_of(info, tokens, table_rows, patch_size, after):
    groups, count = tokens.shape
    return call(
        functools.partial(slots_kernel, table_rows, patch_size),
        [info, tokens],
        [
            ((groups, count), jnp.int32),
            ((1, groups * SLOTS), jnp.int32),
            ((1, 1), jnp.int32),
        ],
        flops=groups * count * count * 8,
        name="slots",
        after=after,
        weight=10**11,
    )


def collect_kernel(info, slot_of, mine, theirs, out):
    count = mine.shape[0]
    slot = lax.broadcasted_iota(jnp.int32, (SLOTS, count), 0)
    total = None
    for rows, core in ((mine, info[CORE]), (theirs, 1 - info[CORE])):
        at = pl.ds(pl.multiple_of(core * count, 128), count)
        hot = jnp.where(slot_of[pl.ds(info[DP], 1), at] == slot, 1.0, 0.0).astype(BF)
        part = nn(hot, rows[...])
        total = part if total is None else total + part
    out[...] = total.astype(BF)


def collect(info, slot_of, mine, theirs, after):
    return call(
        collect_kernel,
        [info, slot_of, mine, theirs],
        [((SLOTS, mine.shape[1]), BF)],
        flops=4 * SLOTS * mine.size,
        name="collect",
        after=after,
    )[0]


def table_kernel(z_size, y_size, info, rows_of, own, *rest):
    rising, falling = rest[: z_size - 1], rest[z_size - 1 : 2 * (z_size - 1)]
    out, ordered = rest[2 * (z_size - 1) :]
    chunk = out.shape[0]

    @pl.when(pl.program_id(0) == 0)
    def _():
        z, y = info[DP] // y_size, info[DP] % y_size

        def put(piece, at_z):
            for j in range(y_size):
                at = pl.multiple_of((at_z * y_size + (y ^ j)) * SLOTS, SLOTS)
                ordered[pl.ds(at, SLOTS), :] = piece[j * SLOTS : (j + 1) * SLOTS]

        put(own, z)
        for k in range(1, z_size):

            @pl.when(z - k >= 0)
            def _():
                put(rising[k - 1], z - k)

            @pl.when(z + k < z_size)
            def _():
                put(falling[k - 1], z + k)

    row = lax.broadcasted_iota(jnp.int32, (chunk, rows_of.shape[1]), 0)
    row = row + pl.program_id(0) * chunk
    hot = jnp.where(row == rows_of[...], 1.0, 0.0).astype(BF)
    out[...] = nn(hot, ordered[...])


def table_back(info, rows_of, own, rising, falling, z_size, y_size, table_rows, chunk=640):
    width = own.shape[1]
    count = rows_of.shape[1]
    return call(
        functools.partial(table_kernel, z_size, y_size),
        [info, rows_of, own, *rising, *falling],
        [((table_rows, width), F32)],
        grid=(table_rows // chunk,),
        out_specs=[pl.BlockSpec((chunk, width), lambda k: (k, 0))],
        scratch=[pltpu.VMEM((count, width), BF)],
        flops=2 * table_rows * count * width,
        name="table",
    )[0]


def stage_kernel(info, *refs):
    half = len(refs) // 2
    for given, out in zip(refs[:half], refs[half:]):
        out[...] = given[...]


def stage(info, values, after):
    return call(
        stage_kernel, [info, *values], [(v.shape, v.dtype) for v in values], name="stage",
        after=after,
    )


def swap_core(values):
    return lax.ppermute(values, "core", [(0, 1), (1, 0)])


def from_x(values, size, step):
    return lax.ppermute(values, "x", [(s, (s - step) % size) for s in range(size)])


def part(values, index, size, axis):
    return lax.dynamic_slice_in_dim(values, index * size, size, axis)


def exchange(values, axis, size, bit):
    return lax.ppermute(values, axis, [(s, s ^ bit) for s in range(size)])


def gather_doubling(values, axis, size):
    place = lax.axis_index(axis)
    bit = 1
    while bit < size:
        other = exchange(values, axis, size, bit)
        low = (place & bit) == 0
        values = jnp.concatenate(
            [jnp.where(low, values, other), jnp.where(low, other, values)], axis=0
        )
        bit *= 2
    return values


def gather_relative(values, axis, size):
    bit = 1
    while bit < size:
        values = jnp.concatenate([values, exchange(values, axis, size, bit)], axis=0)
        bit *= 2
    return values


def pass_on(values, axis, size):
    up = [(s, s + 1) for s in range(size - 1)]
    down = [(s + 1, s) for s in range(size - 1)]
    rising, falling = [values], [values]
    for _ in range(1, size):
        rising.append(lax.ppermute(rising[-1], axis, up))
        falling.append(lax.ppermute(falling[-1], axis, down))
    return rising[1:], falling[1:]


def gather_patch(values, x_size):
    own = [values] + [from_x(values, x_size, k) for k in range(1, x_size)]
    return own + [swap_core(v) for v in own]


def patch_places(x_size):
    xi, ci = lax.axis_index("x"), lax.axis_index("core")
    columns = [(xi + k) % x_size for k in range(x_size)]
    return jnp.stack([x * CORES + ci for x in columns] + [x * CORES + 1 - ci for x in columns])


def halving_steps(z_size, y_size, order):
    y_steps = [("y", y_size, 1 << k) for k in range(y_size.bit_length() - 1)]
    z_steps = [("z", z_size, 1 << k) for k in range(z_size.bit_length() - 1)]
    return y_steps + z_steps if order == "y" else z_steps + y_steps


def add_low(a, b):
    return (a.astype(F32) + b.astype(F32)).astype(BF)


def halve_kernel(info, keep, got, stays, goes):
    half = stays.shape[0]
    for b in range(keep.shape[0]):
        total = keep[b].astype(F32) + got[b].astype(F32)
        if b < half:
            stays[b] = total.astype(BF)
        else:
            goes[b - half] = total.astype(BF)


def halve(info, keep, got, after):
    shape = ((keep.shape[0] // 2,) + keep.shape[1:], BF)
    return call(halve_kernel, [info, keep, got], [shape, shape], name="halve", after=after)


def add_kernel(info, a, b, out):
    for k in range(out.shape[0]):
        out[k] = (a[k].astype(F32) + b[k].astype(F32)).astype(BF)


def add(info, a, b, after):
    return call(add_kernel, [info, a, b], [(a.shape, BF)], name="add", after=after)[0]


def reduce_scatter(info, keep, give, z_size, y_size, order, gates=None, steps=None):
    steps = steps or halving_steps(z_size, y_size, order)
    later = []
    for k, step in enumerate(steps):
        got = exchange(give, *step)
        if k < len(steps) - 1:
            keep, give = halve(info, keep, got, gates[k] if gates else ())
            later.append(give)
    return add_low(keep, got)[0], later


def gather_blocks(block, z_size, y_size, order):
    pieces = [block[None]]
    for step in halving_steps(z_size, y_size, order)[::-1]:
        whole_piece = pieces[0] if len(pieces) == 1 else jnp.concatenate(pieces, axis=0)
        pieces = [whole_piece, exchange(whole_piece, *step)]
    return pieces


def all_reduce(values, z_size, y_size):
    for step in halving_steps(z_size, y_size, "y"):
        values = add_low(values, exchange(values, *step))
    return values


def shards(
    z_size, y_size, x_size,
    token_ids, token_used, paired_ids, features, incoming, query_tokens, table, positions,
    emb_gain, emb_bias, qkv, out_weight, self_gain, self_bias, cross_query, key_shard,
    value_shard, cross_out, cross_gain, cross_bias, query_up, query_down, query_gain, query_bias,
    text_up, text_down, text_gain, text_bias, image_proj, text_proj, sharpness,
):
    group, slots = token_ids.shape
    queries, width = query_tokens.shape
    emb = image_proj.shape[1]
    items = group // CORES
    patch_size = x_size * CORES
    table_rows = table.shape[0]
    feat_rows = features.shape[1]
    kv_rows = key_shard.shape[0]
    dp_size = z_size * y_size
    xi, ci = lax.axis_index("x"), lax.axis_index("core")
    di = lax.axis_index("z") * y_size + lax.axis_index("y")
    member = xi * CORES + ci
    other = xi * CORES + 1 - ci
    block_rows = width // dp_size
    shared = block_rows % (8 * patch_size) == 0
    share_rows = block_rows // patch_size if shared else block_rows
    share, partner = (member, other) if shared else (jnp.int32(0), jnp.int32(0))
    info = jnp.stack([di, share, partner, ci, member, other]).astype(jnp.int32)
    places = patch_places(x_size).astype(jnp.int32)
    orders = {k: order_weights(z_size, y_size, k) for k in ("y", "z")}

    p = dict(
        emb_gain=emb_gain, emb_bias=emb_bias, self_gain=self_gain, self_bias=self_bias,
        cross_gain=cross_gain, cross_bias=cross_bias, query_gain=query_gain,
        query_bias=query_bias, text_gain=text_gain, text_bias=text_bias, positions=positions, query_tokens=query_tokens, qkv=qkv, out=out_weight,
        cross_query=cross_query, cross_out=cross_out, query_up=query_up, query_down=query_down,
        text_up=text_up, text_down=text_down, image_proj=image_proj, text_proj=text_proj,
    )

    def own_first(values):
        return jnp.concatenate(
            [part(values, ci, items, 0), part(values, 1 - ci, items, 0)], axis=0
        )

    local_ids = (own_first(token_ids) - member * table_rows).reshape(-1, 1)
    words_mine, words_give = look_up(info, local_ids, table)
    word_sum = words_mine + swap_core(words_give)
    words = [word_sum] + [from_x(word_sum, x_size, k) for k in range(1, x_size)]

    feat_mine = part(features, ci, items, 0)
    feat_got = swap_core(part(features, 1 - ci, items, 0))
    feats_x = [from_x(feat_mine, x_size, k) for k in range(1, x_size)]
    feat_late, key_late, value_late = stage(
        info, [feat_got, key_shard, value_shard], [word_sum]
    )
    feats = [feat_mine, feat_got]
    for k in range(1, x_size):
        feats += [feats_x[k - 1], from_x(feat_late, x_size, k)]
    key_x = [from_x(key_late, x_size, k) for k in range(1, x_size)]
    value_x = [from_x(value_late, x_size, k) for k in range(1, x_size)]

    used = jnp.concatenate(
        [jnp.ones((items, queries), jnp.int32), part(token_used, ci, items, 0)], axis=1
    ).reshape(items // 2, 2 * (queries + slots))
    (packed, probs, normal_q, normal_t, scale_q, scale_t, cross_q, lhs_mine, lhs_give, chosen_q) = (
        self_forward(info, words, used, p, orders, share_rows)
    )
    lhs_got = swap_core(lhs_give)
    held = list(stage(info, key_x + value_x, [packed]))
    own_keys, own_values = [key_shard] + held[: x_size - 1], [value_shard] + held[x_size - 1 :]
    kv_shards = own_keys + [swap_core(v) for v in own_keys]
    kv_shards += own_values + [swap_core(v) for v in own_values]
    text_names = ("text_up", "text_down", "text_gain", "text_bias", "text_proj")
    query_names = ("query_up", "query_down", "query_gain", "query_bias", "image_proj")
    (t_slope, t_keep, t_give, t_normal, t_scale, text_final, text_raw) = ff_forward(
        info, normal_t, p["self_gain"], p["self_bias"], text_names, p, orders["y"], share_rows,
        items, False,
    )
    t_got = swap_core(t_give)
    keys, values = key_value(info, places, feats, kv_shards, [t_normal])
    cross_probs, normal_c, scale_c, mixed_mine, mixed_give = cross_forward(
        info, cross_q, keys, values, normal_q, p, orders, share_rows
    )
    mixed_got = swap_core(mixed_give)
    (q_slope, q_keep, q_give, q_normal, q_scale, query_final, image_raw) = ff_forward(
        info, normal_c, p["cross_gain"], p["cross_bias"], query_names, p, orders["z"], share_rows,
        items, True,
    )
    q_got = swap_core(q_give)

    query_other, text_other = swap_core(query_final), swap_core(text_final)
    hidden_out = hidden_assemble(
        info, query_final, text_final, query_other, text_other, items
    )

    own_ids = jnp.concatenate(
        [part(token_ids, ci, items, 0), part(paired_ids, ci, items, 0)[:, None]], axis=1
    ).astype(F32)
    own_ids = jnp.pad(own_ids, ((0, 0), (0, 128 - own_ids.shape[1])))
    gathered = gather_doubling(
        jnp.concatenate([image_raw, text_raw, own_ids], axis=1), "core", CORES
    )
    gathered = gather_doubling(gather_doubling(gathered, "y", y_size), "z", z_size)
    loss, grad_image, grad_text, grad_sharp = contrast(
        info, gathered, sharpness.reshape(1, 1), queries, slots, group, emb, [hidden_out]
    )
    ids = gathered[:, 2 * emb : 2 * emb + slots].astype(jnp.int32)
    all_tokens = ids.reshape(dp_size, group * slots)

    q_rhs, grad_second, q_vectors = ff_backward(
        info, incoming, 0, grad_image, (q_slope, q_normal, q_scale),
        ("query_up", "query_down", "query_gain", "image_proj"), p, True,
    )
    t_rhs, grad_text_rows, t_vectors = ff_backward(
        info, incoming, 1, grad_text, (t_slope, t_normal, t_scale),
        ("text_up", "text_down", "text_gain", "text_proj"), p, False,
        [q_vectors, q_got, t_got, lhs_got, mixed_got],
    )
    q_weights = ff_weights(
        info, q_keep, q_got, q_rhs, swap_core(q_rhs), share_rows, dp_size, width, [t_vectors]
    )
    t_weights = ff_weights(
        info, t_keep, t_got, t_rhs, swap_core(t_rhs), share_rows, dp_size, width, [q_weights[0]]
    )

    y_first, z_first = (halving_steps(z_size, y_size, k) for k in ("y", "z"))

    m_rhs, grad_keys, grad_values, grad_query_rows, c_vectors = cross_backward(
        info, grad_second, normal_c, scale_c, keys, values, cross_probs, cross_q, p,
        [t_weights[0]],
    )
    m_got = swap_core(m_rhs)

    more = jnp.concatenate([c_vectors, q_vectors, t_vectors], axis=0)
    l_rhs, words_low = self_backward(
        info, grad_query_rows, grad_text_rows, (normal_q, normal_t, scale_q, scale_t), packed,
        probs, words, more, p, [],
    )
    t_more = halve(info, t_weights[0], exchange(t_weights[1], *y_first[0]), [words_low])
    q_more = halve(info, q_weights[0], exchange(q_weights[1], *z_first[0]), [t_more[1]])
    (words_low,) = stage(info, [words_low], [q_more[1]])
    words_other = swap_core(words_low)
    slot_of, rows_of, most = slots_of(info, all_tokens, table_rows, patch_size, [words_low])

    own = collect(info, slot_of, words_low, words_other, [q_more[1]])
    table_start = [own]
    own = gather_relative(own, "y", y_size)
    rising, falling = pass_on(own, "z", z_size)

    def few(words_low, words_other):
        return table_back(info, rows_of, own, rising, falling, z_size, y_size, table_rows)

    def many(words_low, words_other):
        low_core = ci == 0
        group_words = jnp.concatenate(
            [
                jnp.where(low_core, words_low, words_other),
                jnp.where(low_core, words_other, words_low),
            ],
            axis=0,
        )
        own = lax.dynamic_index_in_dim(all_tokens, di, axis=0, keepdims=False)
        rows = lax.broadcasted_iota(jnp.int32, (1, table_rows), 1) + member * table_rows
        hot = (own[:, None] == rows).astype(BF)
        return all_reduce(tn(hot, group_words).astype(BF), z_size, y_size).astype(F32)

    table_grad = lax.cond(most[0, 0] <= SLOTS, few, many, words_low, words_other)

    cuts = (2, dp_size // 2) if dp_size == 8 and kv_rows % 32 == 0 else (1, 1)
    kv_keep, kv_give = kv_weights(
        info, grad_keys, grad_values, feats, orders["y"], kv_rows, cuts,
        table_start,
    )

    mid = mid_weights(
        info, (lhs_mine, lhs_got), (mixed_mine, mixed_got), (m_rhs, m_got),
        (query_final, query_other), (text_final, text_other), grad_image, grad_text, orders["y"],
        share_rows, [kv_keep],
    )
    last = last_weights(
        info, chosen_q, (lhs_mine, lhs_got), (l_rhs, swap_core(l_rhs)), mid, orders["y"],
        share_rows, [],
    )
    tail_sum, _ = reduce_scatter(
        info, *last, z_size, y_size, "y"
    )
    kv_part = add(info, kv_keep, swap_core(kv_give), [rising[0]])
    if cuts[0] > 1:
        half = dp_size // 2
        kv_block, _ = reduce_scatter(
            info, kv_part[:half], kv_part[half:], z_size, y_size, "y"
        )
        key_grad, value_grad = kv_assemble(
            info, gather_blocks(kv_block, z_size, y_size, "y"), orders["y"], cuts, width
        )
    else:
        kv_total = all_reduce(kv_part[0], z_size, y_size).astype(F32)
        key_grad, value_grad = kv_total[:, :width], kv_total[:, width:]
    feature_mine, feature_give = features_back(
        info, places, grad_keys, grad_values, kv_shards, feat_rows, [kv_keep]
    )
    features_grad = features_assemble(info, feature_mine, swap_core(feature_give))

    def spread(values):
        return gather_patch(values, x_size) if shared else [values]

    q_sum, _ = reduce_scatter(
        info, *q_more, z_size, y_size, "z", [[last[0]]] * len(z_first), z_first[1:]
    )
    t_sum, _ = reduce_scatter(
        info, *t_more, z_size, y_size, "y", [[last[0]]] * len(y_first), y_first[1:]
    )
    ff_parts = spread(jnp.concatenate([q_sum, t_sum], axis=0))
    spots = places if shared else jnp.zeros((1,), jnp.int32)
    query_up_grad, query_down_grad, text_up_grad, text_down_grad = ff_assemble(
        info, spots, ff_parts, share_rows
    )

    tail_parts = spread(tail_sum)
    (
        qkv_grad, out_grad, cross_query_grad, cross_out_grad, image_proj_grad, text_proj_grad,
        tokens_grad, position_grad, vectors,
    ) = tail_assemble(info, spots, tail_parts, share_rows, width, emb, queries)

    return (
        hidden_out, loss.reshape(-1), features_grad, tokens_grad, table_grad, position_grad,
        vectors[0], vectors[1], qkv_grad, out_grad, vectors[2], vectors[3], cross_query_grad,
        key_grad, value_grad, cross_out_grad, vectors[4], vectors[5], query_up_grad,
        query_down_grad, vectors[6], vectors[7], text_up_grad, text_down_grad, vectors[8],
        vectors[9], image_proj_grad, text_proj_grad, grad_sharp.reshape(()),
    )


def solution(mesh):
    dp_size = mesh.shape["dp"]
    y_size = 1 << ((dp_size.bit_length() - 2) // 2)
    z_size = dp_size // y_size
    x_size = mesh.shape["patch"] // CORES
    split = Mesh(
        mesh.devices.reshape(z_size, y_size, x_size, CORES), ("z", "y", "x", "core")
    )
    dp, patch = ("z", "y"), ("x", "core")
    placed = (
        [P(dp, None), P(dp, None), P(dp), P(dp, patch, None), P(dp, None, None), P()]
        + [P(patch, None)]
        + [P()] * 8
        + [P(patch, None)] * 2
        + [P()] * 14
    )
    out = (
        [P(dp, None, None), P(dp), P(dp, patch, None), P(None, dp), P(patch, None)]
        + [P(None, dp), P(dp), P(dp), P(dp, None), P(dp, None), P(dp), P(dp)]
        + [P(dp, None), P(patch, None), P(patch, None), P(dp, None), P(dp), P(dp)]
        + [P(dp, None), P(dp, None), P(dp), P(dp), P(dp, None), P(dp, None)]
        + [P(dp), P(dp), P(dp, None), P(dp, None), P()]
    )

    def body(*args):
        return shards(z_size, y_size, x_size, *args)

    return jax.shard_map(
        body, mesh=split, in_specs=tuple(placed), out_specs=tuple(out), check_vma=False
    )
```

```python
import functools
import math

import jax
import jax.numpy as jnp
from jax import lax
from jax.experimental import pallas as pl
from jax.experimental.pallas import tpu as pltpu
from jax.sharding import Mesh, PartitionSpec as P

HEADS = 12
GROUP = 4
SLOTS = 128
CORES = 2
BF = jnp.bfloat16
F32 = jnp.float32
HIGHEST = lax.Precision.HIGHEST
VMEM_BYTES = 60 * 1024 * 1024
VMEM_SPARE = 10 * 1024 * 1024
SLAB = 32
DP, SHARE, PARTNER, CORE, MEMBER, OTHER = range(6)


def nn(a, b):
    return lax.dot_general(a, b, (((1,), (0,)), ((), ())), preferred_element_type=F32)


def nt(a, b):
    return lax.dot_general(a, b, (((1,), (1,)), ((), ())), preferred_element_type=F32)


def tn(a, b):
    return lax.dot_general(a, b, (((0,), (0,)), ((), ())), preferred_element_type=F32)


def exact(a, b, dims):
    return lax.dot_general(a, b, ((dims[0], dims[1]), ((), ())), precision=HIGHEST)


def normalise(values):
    centred = values - jnp.mean(values, axis=-1, keepdims=True)
    spread = jnp.mean(centred * centred, axis=-1, keepdims=True)
    scale = lax.rsqrt(spread + 1e-06)
    return centred * scale, scale


def slabs(rows):
    step = math.gcd(rows, SLAB)
    return [slice(r, r + step) for r in range(0, rows, step)]


def fold(values):
    return jnp.sum(values.reshape(-1, 8, values.shape[-1]), axis=0)


def norm_back(grad, normal, scale, gain):
    inner = grad * gain
    first = jnp.mean(inner, axis=-1, keepdims=True)
    second = jnp.mean(inner * normal, axis=-1, keepdims=True)
    return scale * (inner - first - normal * second), fold(grad * normal), fold(grad)


def norm_back_rows(grad_of, normal, scale, gain, put):
    gains = biases = None
    for at in slabs(normal.shape[0]):
        grad_in, part_gain, part_bias = norm_back(grad_of(at), normal[at], scale[at], gain[...])
        put(at, grad_in)
        gains = part_gain if gains is None else gains + part_gain
        biases = part_bias if biases is None else biases + part_bias
    return jnp.sum(gains, axis=0, keepdims=True), jnp.sum(biases, axis=0, keepdims=True)


def gelu_both(values):
    size = jnp.abs(values)
    t = 1.0 / (1.0 + (0.3275911 * math.sqrt(0.5)) * size)
    bell = jnp.exp(-0.5 * values * values)
    poly = t * (
        0.254829592
        + t * (-0.284496736 + t * (1.421413741 + t * (-1.453152027 + t * 1.061405429)))
    )
    tail = 0.5 * poly * bell
    cdf = jnp.where(values < 0, tail, 1.0 - tail)
    return values * cdf, cdf + values * bell * (1.0 / math.sqrt(2.0 * math.pi))


def order_weights(z_size, y_size, order):
    y_weights = [1 << k for k in range(y_size.bit_length() - 1)]
    z_weights = [y_size << k for k in range(z_size.bit_length() - 1)]
    return y_weights + z_weights if order == "y" else z_weights + y_weights


def relative_of(position, weights):
    last = len(weights) - 1
    return sum(w for k, w in enumerate(weights) if (position >> (last - k)) & 1)


def position_of(relative, weights):
    last = len(weights) - 1
    place = jnp.int32(0)
    for k, w in enumerate(weights):
        place = place + jnp.where((relative & w) != 0, 1 << (last - k), 0)
    return place


def choose_rows(info, share, weights, rows, size, width):
    blocks = []
    row = lax.broadcasted_iota(jnp.int32, (rows, width), 0)
    column = lax.broadcasted_iota(jnp.int32, (rows, width), 1)
    for position in range(1 << len(weights)):
        block = info[DP] ^ relative_of(position, weights)
        start = block * size + info[share] * rows
        blocks.append(jnp.where(column == row + start, 1.0, 0.0))
    return jnp.concatenate(blocks, axis=0).astype(BF)


def head_masks(lanes, head):
    lane = lax.broadcasted_iota(jnp.int32, (1, lanes), 1)
    return [(lane >= h * head) & (lane < (h + 1) * head) for h in range(lanes // head)]


def stack_heads(values, masks):
    zero = jnp.zeros_like(values)
    return jnp.concatenate([jnp.where(m, values, zero) for m in masks], axis=0)


def merge_heads(stacked, masks):
    rows = stacked.shape[0] // len(masks)
    total = None
    for h, m in enumerate(masks):
        piece = jnp.where(m, stacked[h * rows : (h + 1) * rows], 0.0)
        total = piece if total is None else total + piece
    return total


def softmax_into(out, scores, tile, scaling, closed=None):
    for r in range(0, scores.shape[0], tile):
        part = scores[r : r + tile] * scaling
        if closed is not None:
            part = part + closed
        top = jnp.max(part, axis=-1, keepdims=True)
        powers = jnp.exp(part - top)
        out[r : r + tile] = (powers / jnp.sum(powers, axis=-1, keepdims=True)).astype(BF)


def softmax_back(probs, grads, tile):
    parts = []
    for r in range(0, grads.shape[0], tile):
        p, dp = probs[r : r + tile].astype(F32), grads[r : r + tile]
        parts.append((p * (dp - jnp.sum(p * dp, axis=-1, keepdims=True))).astype(BF))
    return jnp.concatenate(parts, axis=0)


def whole(shape):
    zeros = (0,) * len(shape)
    return pl.BlockSpec(tuple(shape), lambda *_: zeros)


SCALARS = pl.BlockSpec(memory_space=pltpu.SMEM)


def call(kernel, ins, outs, *, grid=(), in_specs=None, out_specs=None, scratch=(), flops=0, name, after=(), weight=1):
    if in_specs is None:
        in_specs = [None] * len(ins)
    in_specs = [
        spec or (SCALARS if k == 0 else whole(v.shape))
        for k, (spec, v) in enumerate(zip(in_specs, ins))
    ]
    out_shape = [jax.ShapeDtypeStruct(shape, dtype) for shape, dtype in outs]
    if out_specs is None:
        out_specs = [None] * len(outs)
    out_specs = [spec or whole(o.shape) for spec, o in zip(out_specs, out_shape)]
    moved = sum(v.size * v.dtype.itemsize for v in list(ins) + out_shape)
    limit = VMEM_BYTES
    if not grid:
        held = sum(math.prod(v.shape) * jnp.dtype(v.dtype).itemsize for v in scratch)
        limit = min(VMEM_BYTES, moved + held + VMEM_SPARE)
    elif grid == (1,):
        held = sum(math.prod(v.shape) * jnp.dtype(v.dtype).itemsize for v in scratch)
        limit = min(VMEM_BYTES, 2 * moved + held + VMEM_SPARE)
    count = len(ins)

    def body(*refs):
        kernel(*refs[:count], *refs[count + len(after) :])

    return pl.pallas_call(
        body,
        grid=grid,
        in_specs=in_specs + [pl.BlockSpec(memory_space=pl.ANY)] * len(after),
        out_specs=out_specs,
        out_shape=out_shape,
        scratch_shapes=list(scratch),
        compiler_params=pltpu.CompilerParams(vmem_limit_bytes=limit),
        cost_estimate=pl.CostEstimate(
            flops=weight, bytes_accessed=1, transcendentals=0
        ),
        name=name,
    )(*ins, *after)


def words_kernel(info, ids, table, mine, give, total):
    step = pl.program_id(0)
    chunk = table.shape[0]

    @pl.when(step == 0)
    def _():
        total[...] = jnp.zeros_like(total)

    column = lax.broadcasted_iota(jnp.int32, (ids.shape[0], chunk), 1) + step * chunk
    hot = jnp.where(ids[...] == column, 1.0, 0.0).astype(BF)
    total[...] += nn(hot, table[...])

    @pl.when(step == pl.num_programs(0) - 1)
    def _():
        half = total.shape[0] // 2
        mine[...] = total[:half].astype(BF)
        give[...] = total[half:].astype(BF)


def look_up(info, ids, table, chunk=640):
    rows, width = table.shape
    count = ids.shape[0]
    return call(
        words_kernel,
        [info, ids, table],
        [((count // 2, width), BF)] * 2,
        grid=(rows // chunk,),
        in_specs=[None, None, pl.BlockSpec((chunk, width), lambda k: (k, 0))],
        scratch=[pltpu.VMEM((count, width), F32)],
        flops=2 * count * rows * width,
        name="words",
    )


def embed_slab(words, positions, at):
    slots, width = positions.shape
    total = words[0][at].astype(F32)
    for other in words[1:]:
        total = total + other[at].astype(F32)
    start = at.start % slots
    if start + total.shape[0] <= slots:
        return total + positions[start : start + total.shape[0]].astype(F32)
    return (total.reshape(-1, slots, width) + positions[...].astype(F32)[None]).reshape(-1, width)


def self_forward_kernel(
    x_size, weights, share_rows, info, positions, query_tokens, emb_gain, emb_bias, qkv,
    used, out_weight, gain, bias, cross_weight, *rest,
):
    words = rest[:x_size]
    (
        packed, probs, normal_q, normal_t, scale_q, scale_t, cross_q, keep, give, chosen_q, mixed,
        start_rows, query_rows, attended,
    ) = rest[x_size:]
    slots, width = positions.shape
    queries = query_tokens.shape[0]
    rows = queries + slots
    head = width // HEADS
    lanes = GROUP * head
    start_q = normalise(query_tokens[...].astype(F32))[0] * emb_gain[...] + emb_bias[...]
    count = words[0].shape[0]
    items = count // slots
    for at in slabs(count):
        normal, _ = normalise(embed_slab(words, positions, at))
        start_rows[at] = normal * emb_gain[...] + emb_bias[...]
    start_q_low, start_w_low = start_q.astype(BF), start_rows[...].astype(BF)
    both = jnp.concatenate([start_q_low, start_w_low], axis=0)
    for c in range(3):
        span = slice(c * width, (c + 1) * width)
        product = nn(both, qkv[:, span]).astype(BF)
        for i in range(items):
            packed[i * rows : i * rows + queries, span] = product[:queries]
            packed[i * rows + queries : (i + 1) * rows, span] = product[
                queries + i * slots : queries + (i + 1) * slots
            ]
    masks = head_masks(lanes, head)
    pair = 2 * rows
    row_item = lax.broadcasted_iota(jnp.int32, (pair, pair), 0) // rows
    column_item = lax.broadcasted_iota(jnp.int32, (pair, pair), 1) // rows
    for j in range(items // 2):
        closed = jnp.where((row_item == column_item) & (used[j : j + 1] > 0), 0.0, -1e30)
        at = slice(j * pair, (j + 1) * pair)
        for g in range(HEADS // GROUP):
            base = g * lanes
            q = stack_heads(packed[at, base : base + lanes], masks)
            k = packed[at, width + base : width + base + lanes]
            v = packed[at, 2 * width + base : 2 * width + base + lanes]
            p = probs.at[j * (HEADS // GROUP) + g]
            softmax_into(p, nt(q, k), pair, 1.0 / math.sqrt(head), closed)
            mixed[at, base : base + lanes] = merge_heads(nn(p[...], v), masks).astype(BF)
    attended[...] = nn(mixed[...], out_weight[...])
    for i in range(items):
        base = i * rows
        for at in slabs(queries):
            into = slice(i * queries + at.start, i * queries + at.stop)
            normal, scale = normalise(attended[base + at.start : base + at.stop] + start_q[at])
            normal_q[into] = normal
            scale_q[into] = scale
            query_rows[into] = (normal * gain[...] + bias[...]).astype(BF)
        for at in slabs(slots):
            into = slice(i * slots + at.start, i * slots + at.stop)
            start = base + queries + at.start
            normal, scale = normalise(
                attended[start : start + at.stop - at.start] + start_rows[into]
            )
            normal_t[into] = normal
            scale_t[into] = scale
    query_low = query_rows[...]
    cross_q[...] = nn(query_low, cross_weight[...]).astype(BF)
    size = width >> len(weights)
    for share, out in ((SHARE, keep), (PARTNER, give)):
        select = choose_rows(info, share, weights, share_rows, size, width)
        out[:, : items * slots] = nt(select, start_w_low).astype(BF)
        out[:, items * slots : items * (slots + rows)] = nt(select, mixed[...]).astype(BF)
        if share == SHARE:
            chosen_q[...] = nt(select, start_q_low).astype(BF)
        out[:, items * (slots + rows) :] = nt(select, query_low).astype(BF)


def self_forward(info, words, used, p, orders, share_rows):
    slots, width = p["positions"].shape
    queries = p["query_tokens"].shape[0]
    items = words[0].shape[0] // slots
    rows = queries + slots
    blocks = 1 << len(orders["y"])
    units = (items // 2) * (HEADS // GROUP)
    ins = [
        info, p["positions"], p["query_tokens"], p["emb_gain"], p["emb_bias"], p["qkv"], used,
        p["out"], p["self_gain"], p["self_bias"], p["cross_query"], *words,
    ]
    lhs = (blocks * share_rows, items * (slots + rows + queries))
    outs = [
        ((items * rows, 3 * width), BF),
        ((units, GROUP * 2 * rows, 2 * rows), BF),
        ((items * queries, width), F32),
        ((items * slots, width), F32),
        ((items * queries, 1), F32),
        ((items * slots, 1), F32),
        ((items * queries, width), BF),
        (lhs, BF),
        (lhs, BF),
        ((blocks * share_rows, queries), BF),
    ]
    return call(
        functools.partial(self_forward_kernel, len(words), orders["y"], share_rows),
        ins,
        outs,
        scratch=[
            pltpu.VMEM((items * rows, width), BF),
            pltpu.VMEM((items * slots, width), F32),
            pltpu.VMEM((items * queries, width), BF),
            pltpu.VMEM((items * rows, width), F32),
        ],
        flops=2 * items * rows * width * width * 6,
        name="self_forward",
        grid=(1,),
    )


def fill_weights(places, shards, key_full, value_full):
    half = len(shards) // 2
    size = shards[0].shape[0]
    for k in range(half):
        at = pl.ds(pl.multiple_of(places[k] * size, 16), size)
        key_full[at, :] = shards[k][...]
        value_full[at, :] = shards[half + k][...]


def key_value_kernel(pieces, info, places, *rest):
    feats, shards = rest[:pieces], rest[pieces : 3 * pieces]
    keys, values, key_full, value_full = rest[3 * pieces :]
    fill_weights(places, shards, key_full, value_full)
    items, rows, width = feats[0].shape
    for k, piece in enumerate(feats):
        flat = piece[...].reshape(items * rows, width)
        at = slice(k * rows, (k + 1) * rows)
        keys[:, at] = nn(flat, key_full[...]).astype(BF).reshape(items, rows, -1)
        values[:, at] = nn(flat, value_full[...]).astype(BF).reshape(items, rows, -1)


def key_value(info, places, feats, shards, after):
    items, rows, deep = feats[0].shape
    width = shards[0].shape[1]
    pieces = len(feats)
    return call(
        functools.partial(key_value_kernel, pieces),
        [info, places, *feats, *shards],
        [((items, pieces * rows, width), BF)] * 2,
        in_specs=[SCALARS, SCALARS] + [None] * (3 * pieces),
        scratch=[pltpu.VMEM((deep, width), BF)] * 2,
        flops=4 * items * rows * pieces * deep * width,
        name="key_value",
        after=after,
    )


def cross_forward_kernel(
    weights, share_rows, info, cross_q, keys, values, normal_q, self_gain, self_bias,
    out_weight, probs, normal, scale, keep, give, mixed, added,
):
    items, _, width = keys.shape
    queries = cross_q.shape[0] // items
    head = width // HEADS
    lanes = GROUP * head
    masks = head_masks(lanes, head)
    groups = HEADS // GROUP
    for i in range(items):
        at = slice(i * queries, (i + 1) * queries)
        for g in range(groups):
            span = slice(g * lanes, (g + 1) * lanes)
            q = stack_heads(cross_q[at, span], masks)
            p = probs.at[i * groups + g]
            softmax_into(p, nt(q, keys[i, :, span]), 2 * queries, 1.0 / math.sqrt(head))
            mixed[at, span] = merge_heads(nn(p[...], values[i, :, span]), masks).astype(BF)
    added[...] = nn(mixed[...], out_weight[...])
    for at in slabs(added.shape[0]):
        n, s = normalise(added[at] + (normal_q[at] * self_gain[...] + self_bias[...]))
        normal[at] = n
        scale[at] = s
    for share, out in ((SHARE, keep), (PARTNER, give)):
        select = choose_rows(info, share, weights, share_rows, width >> len(weights), width)
        out[...] = nt(select, mixed[...]).astype(BF)


def cross_forward(info, cross_q, keys, values, normal_q, p, orders, share_rows):
    items, all_rows, width = keys.shape
    count = cross_q.shape[0]
    blocks = 1 << len(orders["z"])
    ins = [
        info, cross_q, keys, values, normal_q, p["self_gain"], p["self_bias"], p["cross_out"],
    ]
    outs = [
        ((items * HEADS // GROUP, GROUP * count // items, all_rows), BF),
        ((count, width), F32),
        ((count, 1), F32),
        ((blocks * share_rows, count), BF),
        ((blocks * share_rows, count), BF),
    ]
    return call(
        functools.partial(cross_forward_kernel, orders["y"], share_rows),
        ins,
        outs,
        scratch=[pltpu.VMEM((count, width), BF), pltpu.VMEM((count, width), F32)],
        flops=2 * count * width * width + 4 * count * all_rows * width,
        name="cross_forward",
    )


def ff_forward_kernel(
    weights, share_rows, averaged, info, normal_in, gain_in, bias_in, up, down, gain, bias, proj,
    slope, keep, give, normal, scale, final, raw, rows_low, total, inner, active_low,
):
    step = pl.program_id(0)
    blocks = 1 << len(weights)
    count, width = normal_in.shape
    chunk = up.shape[1]
    deep = 4 * share_rows
    size = 4 * width // blocks

    @pl.when(step == 0)
    def _():
        for at in slabs(count):
            rows = normal_in[at] * gain_in[...] + bias_in[...]
            rows_low[at] = rows.astype(BF)
            total[at] = rows
        for share, out in ((SHARE, keep), (PARTNER, give)):
            select = choose_rows(info, share, weights, share_rows, width // blocks, width)
            out[: blocks * share_rows] = nt(select, rows_low[...]).astype(BF)

    inner[...] = nn(rows_low[...], up[...])
    for at in slabs(count):
        for c in range(0, chunk, 256):
            value, slant = gelu_both(inner[at, c : c + 256])
            active_low[at, c : c + 256] = value.astype(BF)
            slope[at, c : c + 256] = slant.astype(BF)
    active = active_low[...]
    total[...] += nn(active, down[...])
    each = chunk // size
    row = lax.broadcasted_iota(jnp.int32, (deep, chunk), 0)
    column = lax.broadcasted_iota(jnp.int32, (deep, chunk), 1)
    for share, out in ((SHARE, keep), (PARTNER, give)):
        select = [
            jnp.where(column == row + (j * size + info[share] * deep), 1.0, 0.0)
            for j in range(each)
        ]
        picked = nt(jnp.concatenate(select, axis=0).astype(BF), active).astype(BF)
        for j in range(each):
            block = step * each + j
            place = position_of(block ^ info[DP], weights)
            at = pl.multiple_of(blocks * share_rows + place * deep, 16)
            out[pl.ds(at, deep), :] = picked[j * deep : (j + 1) * deep]

    @pl.when(step == pl.num_programs(0) - 1)
    def _():
        for at in slabs(count):
            n, s = normalise(total[at])
            normal[at] = n
            scale[at] = s
            final[at] = (n * gain[...] + bias[...]).astype(BF)
        low = final[...]
        items = raw.shape[0]
        if averaged:
            image = nn(low, proj[...]).reshape(items, count // items, -1)
            raw[...] = jnp.mean(image, axis=1)
        else:
            heads = jnp.concatenate(
                [low[i * (count // items) : i * (count // items) + 16] for i in range(items)], axis=0
            )
            text = nn(heads, proj[...]).reshape(items, 16, -1)
            raw[...] = text[:, 0]


def ff_forward(info, normal_in, gain_in, bias_in, names, p, weights, share_rows, items, averaged):
    up, down, gain, bias, proj = (p[k] for k in names)
    count, width = normal_in.shape
    inner = up.shape[1]
    chunk = width
    blocks = 1 << len(weights)
    lhs = (blocks * share_rows * 5, count)
    return call(
        functools.partial(ff_forward_kernel, weights, share_rows, averaged),
        [info, normal_in, gain_in, bias_in, up, down, gain, bias, proj],
        [
            ((count, inner), BF),
            (lhs, BF),
            (lhs, BF),
            ((count, width), F32),
            ((count, 1), F32),
            ((count, width), BF),
            ((items, proj.shape[1]), F32),
        ],
        grid=(inner // chunk,),
        in_specs=[None] * 4
        + [
            pl.BlockSpec((width, chunk), lambda k: (0, k)),
            pl.BlockSpec((chunk, width), lambda k: (k, 0)),
        ]
        + [None] * 3,
        out_specs=[pl.BlockSpec((count, chunk), lambda k: (0, k))] + [None] * 6,
        scratch=[
            pltpu.VMEM((count, width), BF),
            pltpu.VMEM((count, width), F32),
            pltpu.VMEM((count, chunk), F32),
            pltpu.VMEM((count, chunk), BF),
        ],
        flops=4 * count * width * inner,
        name="ff_forward",
    )


def ff_backward_kernel(
    averaged, info, incoming, extra, proj, normal, scale, gain, slope, up, down,
    rhs, grad_rows, vectors, added, outer, total,
):
    step = pl.program_id(0)
    count, width = normal.shape
    chunk = slope.shape[1]

    @pl.when(step == 0)
    def _():
        items = extra.shape[0] // 2
        each = count // items
        added[...] = nt(extra[...], proj[...])

        def grad_of(at):
            grad = incoming[at.start // each, at.start % each : at.start % each + SLAB].astype(F32)
            more = added[at.start // each : at.start // each + 1]
            if averaged:
                return grad + more
            row = lax.broadcasted_iota(jnp.int32, (SLAB, 1), 0) + at.start % each
            return grad + jnp.where(row == 0, more, 0.0)

        def put(at, grad_in):
            total[at] = grad_in
            outer[at] = grad_in.astype(BF)
            rhs[at, pl.num_programs(0) * chunk :] = grad_in.astype(BF)

        grads = norm_back_rows(grad_of, normal, scale, gain, put)
        vectors[...] = jnp.concatenate(grads, axis=0)

    inner = (nt(outer[...], down[...]) * slope[...].astype(F32)).astype(BF)
    rhs[:, pl.ds(pl.multiple_of(step * chunk, 128), chunk)] = inner
    total[...] += nt(inner, up[...])

    @pl.when(step == pl.num_programs(0) - 1)
    def _():
        grad_rows[...] = total[...]


def ff_backward(info, incoming, part_of, extra, state, names, p, averaged, after=()):
    up, down, gain, proj = (p[k] for k in names)
    slope, normal, scale = state
    count, width = normal.shape
    items = extra.shape[0] // 2
    inner = up.shape[1]
    chunk = width
    each = count // items
    gs = pltpu.PrefetchScalarGridSpec(
        num_scalar_prefetch=1,
        grid=(inner // chunk,),
        in_specs=[
            pl.BlockSpec((items, each, width), lambda k, info: (info[CORE], part_of, 0)),
            whole(extra.shape),
            whole(proj.shape),
            whole(normal.shape),
            whole(scale.shape),
            whole(gain.shape),
            pl.BlockSpec((count, chunk), lambda k, info: (0, k)),
            pl.BlockSpec((width, chunk), lambda k, info: (0, k)),
            pl.BlockSpec((chunk, width), lambda k, info: (k, 0)),
        ]
        + [pl.BlockSpec(memory_space=pl.ANY)] * len(after),
        out_specs=[whole((count, inner + width)), whole((count, width)), whole((2, width))],
        scratch_shapes=[
            pltpu.VMEM((2 * items, width), F32),
            pltpu.VMEM((count, width), BF),
            pltpu.VMEM((count, width), F32),
        ],
    )

    def body(*refs):
        ff_backward_kernel(averaged, *refs[:10], *refs[10 + len(after) :])

    return pl.pallas_call(
        body,
        grid_spec=gs,
        out_shape=[
            jax.ShapeDtypeStruct((count, inner + width), BF),
            jax.ShapeDtypeStruct((count, width), F32),
            jax.ShapeDtypeStruct((2, width), F32),
        ],
        compiler_params=pltpu.CompilerParams(vmem_limit_bytes=VMEM_BYTES),
        cost_estimate=pl.CostEstimate(
            flops=1, bytes_accessed=1, transcendentals=0
        ),
        name="ff_backward",
    )(info, incoming, extra, proj, normal, scale, gain, slope, up, down, *after)


def ff_weights_kernel(share_rows, blocks, info, lhs_a, lhs_b, rhs_a, rhs_b, keep, give, total):
    width = keep.shape[2]
    inner = rhs_a.shape[1] - width
    first = blocks * share_rows
    for c in range(inner // width):
        span = slice(c * width, (c + 1) * width)
        part = nn(lhs_a[:first], rhs_a[:, span]) + nn(lhs_b[:first], rhs_b[:, span])
        for b in range(blocks):
            total[b, c * share_rows : (c + 1) * share_rows] = part[
                b * share_rows : (b + 1) * share_rows
            ]
    deep = 4 * share_rows
    down = nn(lhs_a[first:], rhs_a[:, inner:]) + nn(lhs_b[first:], rhs_b[:, inner:])
    for b in range(blocks):
        out, at = (keep, b) if b < blocks // 2 else (give, b - blocks // 2)
        out[at, :deep] = total[b].astype(BF)
        out[at, deep:] = down[b * deep : (b + 1) * deep].astype(BF)


def ff_weights(info, lhs_a, lhs_b, rhs_a, rhs_b, share_rows, blocks, width, after):
    deep = 4 * share_rows
    out = ((blocks // 2, 2 * deep, width), BF)
    return call(
        functools.partial(ff_weights_kernel, share_rows, blocks),
        [info, lhs_a, lhs_b, rhs_a, rhs_b],
        [out, out],
        scratch=[pltpu.VMEM((blocks, deep, width), F32)],
        flops=4 * lhs_a.size * 4 * width,
        name="ff_weights",
        after=after,
    )


def log_sum(values, axis):
    top = jnp.max(values, axis=axis, keepdims=True)
    return top + jnp.log(jnp.sum(jnp.exp(values - top), axis=axis, keepdims=True))


def contrast_kernel(
    queries, slots, y_size, z_size, info, sharpness, *rest
):
    pieces = rest[:z_size]
    (
        loss, grad_image, grad_text, grad_sharp, all_ids, gathered, all_loss, all_image, all_text
    ) = rest[z_size:]
    each = pieces[0].shape[0] // y_size
    for k, piece in enumerate(pieces):
        for j in range(y_size):
            at = pl.multiple_of((info[DP] ^ (k * y_size + j)) * each, 8)
            gathered[pl.ds(at, each), :] = piece[j * each : (j + 1) * each]
    count = gathered.shape[0]
    emb = grad_image.shape[1]
    image_raw, text_raw = gathered[:, :emb], gathered[:, emb : 2 * emb]
    ids = gathered[:, 2 * emb :]
    all_ids[...] = ids.astype(jnp.int32)
    pairs = ids[:, slots : slots + 1].astype(jnp.int32)
    pairs_row = ids.T[slots : slots + 1].astype(jnp.int32)
    image_scale = lax.rsqrt(jnp.sum(image_raw * image_raw, axis=1, keepdims=True) + 1e-06)
    text_scale = lax.rsqrt(jnp.sum(text_raw * text_raw, axis=1, keepdims=True) + 1e-06)
    image, text = image_raw * image_scale, text_raw * text_scale
    sharp = sharpness[...]
    factor = 1.0 / jnp.clip(sharp, 0.04, 0.5)
    inside = jnp.where((sharp >= 0.04) & (sharp <= 0.5), 1.0, 0.0)
    by_image = exact(image, text, ((1,), (1,))) * factor
    by_text = exact(text, image, ((1,), (1,))) * factor
    row, row_flat = log_sum(by_image, 1), log_sum(by_text, 0)
    column, column_flat = log_sum(by_text, 1), log_sum(by_image, 0)
    down = lax.broadcasted_iota(jnp.int32, (count, count), 0)
    across = lax.broadcasted_iota(jnp.int32, (count, count), 1)
    match = jnp.where(across == pairs, 1.0, 0.0)
    match_text = jnp.where(down == pairs_row, 1.0, 0.0)
    pull = 0.5 * (jnp.exp(by_image - row) + jnp.exp(by_image - column_flat)) - match
    pull_text = 0.5 * (jnp.exp(by_text - column) + jnp.exp(by_text - row_flat)) - match_text
    positive = jnp.sum(match * by_image, axis=1, keepdims=True)
    all_loss[...] = 0.5 * (row + column) - positive
    share = jnp.sum(jnp.sum(pull * by_image, axis=1, keepdims=True), axis=0, keepdims=True)
    grad_sharp[...] = -factor * inside * share
    toward_image = exact(pull, text, ((1,), (0,))) * factor
    toward_text = exact(pull_text, image, ((1,), (0,))) * factor
    all_image[...] = (
        image_scale
        * (toward_image - image * jnp.sum(image * toward_image, axis=1, keepdims=True))
        * (1.0 / queries)
    )
    all_text[...] = text_scale * (
        toward_text - text * jnp.sum(text * toward_text, axis=1, keepdims=True)
    )
    group = loss.shape[0]
    items = group // CORES
    base = info[DP] * group
    loss[...] = all_loss[pl.ds(pl.multiple_of(base, 8), group), :]
    mine = pl.ds(pl.multiple_of(base + info[CORE] * items, 8), items)
    theirs = pl.ds(pl.multiple_of(base + (1 - info[CORE]) * items, 8), items)
    grad_image[...] = jnp.concatenate([all_image[mine, :], all_image[theirs, :]], axis=0).astype(BF)
    grad_text[...] = jnp.concatenate([all_text[mine, :], all_text[theirs, :]], axis=0).astype(BF)


def contrast(info, pieces, sharpness, queries, slots, group, emb, y_size, after):
    count = pieces[0].shape[0] * len(pieces)
    spare = pieces[0].shape[1] - 2 * emb
    return call(
        functools.partial(contrast_kernel, queries, slots, y_size, len(pieces)),
        [info, sharpness, *pieces],
        [
            ((group, 1), F32),
            ((group, emb), BF),
            ((group, emb), BF),
            ((1, 1), F32),
            ((count, spare), jnp.int32),
        ],
        scratch=[
            pltpu.VMEM((count, pieces[0].shape[1]), F32),
            pltpu.VMEM((count, 1), F32),
            pltpu.VMEM((count, emb), F32),
            pltpu.VMEM((count, emb), F32),
        ],
        flops=50 * count * count * emb,
        name="contrast",
        after=after,
    )


def cross_backward_kernel(
    info, grad_second, normal, scale, gain, out_weight, keys, values, probs, cross_q, cross_weight,
    rhs, grad_keys, grad_values, grad_query, vectors, grad_heads,
):
    items, _, width = keys.shape
    queries = cross_q.shape[0] // items
    head = width // HEADS
    lanes = GROUP * head
    scaling = 1.0 / math.sqrt(head)
    masks = head_masks(lanes, head)
    groups = HEADS // GROUP

    def put(at, grad_in):
        grad_query[at] = grad_in
        rhs[at, width:] = grad_in.astype(BF)

    grads = norm_back_rows(lambda at: grad_second[at], normal, scale, gain, put)
    vectors[...] = jnp.concatenate(grads, axis=0)
    grad_heads[...] = nt(rhs[:, width:], out_weight[...]).astype(BF)
    for i in range(items):
        at = slice(i * queries, (i + 1) * queries)
        for g in range(groups):
            span = slice(g * lanes, (g + 1) * lanes)
            dm = stack_heads(grad_heads[at, span], masks)
            q = stack_heads(cross_q[at, span], masks)
            p_low = probs[i * groups + g]
            ds = softmax_back(p_low, nt(dm, values[i, :, span]), 2 * queries)
            rhs[at, span] = (merge_heads(nn(ds, keys[i, :, span]), masks) * scaling).astype(BF)
            grad_keys[i, :, span] = (tn(ds, q) * scaling).astype(BF)
            grad_values[i, :, span] = tn(p_low, dm).astype(BF)
    grad_query[...] += nt(rhs[:, :width], cross_weight[...])


def cross_backward(info, grad_second, normal, scale, keys, values, probs, cross_q, p, after):
    items, all_rows, width = keys.shape
    count = cross_q.shape[0]
    return call(
        cross_backward_kernel,
        [
            info, grad_second, normal, scale, p["cross_gain"], p["cross_out"], keys, values, probs,
            cross_q, p["cross_query"],
        ],
        [
            ((count, 2 * width), BF),
            (keys.shape, BF),
            (keys.shape, BF),
            ((count, width), F32),
            ((2, width), F32),
        ],
        scratch=[pltpu.VMEM((count, width), BF)],
        flops=4 * count * width * width + 8 * count * all_rows * width,
        name="cross_backward",
        grid=(1,),
        after=after,
    )


def features_kernel(pieces, info, places, grad_keys, grad_values, *rest):
    shards = rest[: 2 * pieces]
    mine, give, key_full, value_full = rest[2 * pieces :]
    fill_weights(places, shards, key_full, value_full)
    items, rows, deep = mine.shape
    for k, out in enumerate((mine, give)):
        at = slice(k * rows, (k + 1) * rows)
        grad = nt(grad_keys[:, at].reshape(items * rows, -1), key_full[...])
        grad = grad + nt(grad_values[:, at].reshape(items * rows, -1), value_full[...])
        out[...] = grad.reshape(items, rows, deep).astype(out.dtype)


def features_back(info, places, grad_keys, grad_values, shards, rows, after):
    items, _, width = grad_keys.shape
    pieces = len(shards) // 2
    deep = shards[0].shape[0] * pieces
    return call(
        functools.partial(features_kernel, pieces),
        [info, places, grad_keys, grad_values, *shards],
        [((items, rows, deep), F32), ((items, rows, deep), BF)],
        in_specs=[SCALARS, SCALARS] + [None] * (2 + len(shards)),
        scratch=[pltpu.VMEM((deep, width), BF)] * 2,
        flops=8 * items * rows * deep * width,
        name="features_back",
        after=after,
    )


def kv_weights_kernel(pieces, weights, cuts, info, grad_keys, grad_values, *rest):
    feats = rest[:pieces]
    keep, give, total, blocks = rest[pieces:]
    items, rows, deep = feats[0].shape
    width = grad_keys.shape[2]
    size = total.shape[0]
    row = lax.broadcasted_iota(jnp.int32, (size, deep), 0)
    column = lax.broadcasted_iota(jnp.int32, (size, deep), 1)
    for which, out in ((MEMBER, keep), (OTHER, give)):
        select = jnp.where(column == row + info[which] * size, 1.0, 0.0).astype(BF)
        for k, piece in enumerate(feats):
            at = slice(k * rows, (k + 1) * rows)
            picked = nt(select, piece[...].reshape(items * rows, deep)).astype(BF)
            part_k = nn(picked, grad_keys[:, at].reshape(items * rows, width))
            part_v = nn(picked, grad_values[:, at].reshape(items * rows, width))
            if k == 0:
                total[:, :width] = part_k
                total[:, width:] = part_v
            else:
                total[:, :width] += part_k
                total[:, width:] += part_v
        height, span = size // cuts[0], 2 * width // cuts[1]
        for a in range(cuts[0]):
            for b in range(cuts[1]):
                blocks[a * cuts[1] + b] = total[
                    a * height : (a + 1) * height, b * span : (b + 1) * span
                ].astype(BF)
        for position in range(cuts[0] * cuts[1]):
            if cuts[0] * cuts[1] == 1:
                out[0] = blocks[0]
            else:
                out[position] = blocks[info[DP] ^ relative_of(position, weights)]


def kv_weights(info, grad_keys, grad_values, feats, weights, size, cuts, after):
    width = grad_keys.shape[2]
    items, rows, deep = feats[0].shape
    blocks = (cuts[0] * cuts[1], size // cuts[0], 2 * width // cuts[1])
    return call(
        functools.partial(kv_weights_kernel, len(feats), weights, cuts),
        [info, grad_keys, grad_values, *feats],
        [(blocks, BF), (blocks, BF)],
        scratch=[pltpu.VMEM((size, 2 * width), F32), pltpu.VMEM(blocks, BF)],
        flops=4 * size * items * rows * len(feats) * (deep + 2 * width),
        name="kv_weights",
        after=after,
    )


def self_backward_kernel(
    x_size, info, grad_query, grad_text, normal_q, normal_t, scale_q, scale_t, gain, out_weight,
    packed, probs, positions, query_tokens, emb_gain, qkv, more, *rest,
):
    words = rest[:x_size]
    rhs, words_low, grad_mixed, attended, grad_packed, in_q, in_t = rest[x_size:]
    slots, width = positions.shape
    queries = query_tokens.shape[0]
    rows = queries + slots
    items = grad_text.shape[0] // slots
    count = items * slots
    head = width // HEADS
    lanes = GROUP * head
    scaling = 1.0 / math.sqrt(head)
    masks = head_masks(lanes, head)
    groups = HEADS // GROUP

    def put_rows(into, each, offset):
        def put(at, grad_in):
            into[at] = grad_in
            start = at.start // each * rows + offset + at.start % each
            attended[start : start + SLAB] = grad_in.astype(BF)

        return put

    gain_q, bias_q = norm_back_rows(
        lambda at: grad_query[at], normal_q, scale_q, gain, put_rows(in_q, queries, 0)
    )
    gain_t, bias_t = norm_back_rows(
        lambda at: grad_text[at], normal_t, scale_t, gain, put_rows(in_t, slots, queries)
    )
    half = items * rows // 2
    rhs[:half, 3 * width : 4 * width] = attended[:half]
    rhs[:half, 4 * width :] = attended[half:]
    grad_mixed[...] = nt(attended[...], out_weight[...]).astype(BF)
    pair = 2 * rows
    for j in range(items // 2):
        at = slice(j * pair, (j + 1) * pair)
        for g in range(groups):
            base = g * lanes
            q = stack_heads(packed[at, base : base + lanes], masks)
            k = packed[at, width + base : width + base + lanes]
            v = packed[at, 2 * width + base : 2 * width + base + lanes]
            dm = stack_heads(grad_mixed[at, base : base + lanes], masks)
            p_low = probs[j * groups + g]
            ds = softmax_back(p_low, nt(dm, v), pair)
            grad_packed[at, base : base + lanes] = (
                merge_heads(nn(ds, k), masks) * scaling
            ).astype(BF)
            grad_packed[at, width + base : width + base + lanes] = (tn(ds, q) * scaling).astype(BF)
            grad_packed[at, 2 * width + base : 2 * width + base + lanes] = tn(p_low, dm).astype(BF)
    total_q = None
    for i in range(items):
        piece = grad_packed[i * rows : i * rows + queries].astype(F32)
        total_q = piece if total_q is None else total_q + piece
        rhs[i * slots : (i + 1) * slots, : 3 * width] = grad_packed[
            i * rows + queries : (i + 1) * rows
        ]
    total_q = total_q.astype(BF)
    rhs[count : count + queries, : 3 * width] = total_q
    in_t[...] += nt(rhs[:count, : 3 * width], qkv[...])
    start_q = jnp.sum(in_q[...].reshape(items, queries, width), axis=0) + nt(total_q, qkv[...])
    normal_e, scale_e = normalise(query_tokens[...].astype(F32))
    grad_tokens, gain_e, bias_e = norm_back(start_q, normal_e, scale_e, emb_gain[...])
    gain_w, bias_w = gain_e, bias_e
    position_grad = None
    for at in slabs(count):
        normal_w, scale_w = normalise(embed_slab(words, positions, at))
        grad_words, part_gain, part_bias = norm_back(in_t[at], normal_w, scale_w, emb_gain[...])
        gain_w, bias_w = gain_w + part_gain, bias_w + part_bias
        words_low[at] = grad_words.astype(BF)
        position_grad = grad_words if position_grad is None else position_grad + grad_words
    rhs[count : count + queries, 3 * width : 4 * width] = grad_tokens.astype(BF)
    rhs[count : count + slots, 4 * width :] = position_grad.astype(BF)
    gain_w = jnp.sum(gain_w, axis=0, keepdims=True)
    bias_w = jnp.sum(bias_w, axis=0, keepdims=True)
    vectors = jnp.concatenate(
        [gain_w, bias_w, gain_q + gain_t, bias_q + bias_t]
        + [more[...], jnp.zeros((6, width), F32)],
        axis=0,
    )
    rhs[count + queries :, :width] = vectors.astype(BF)
    rhs[count + queries :, width:] = jnp.zeros((16, 4 * width), BF)


def self_backward(info, grad_query, grad_text, state, packed, probs, words, more, p, after):
    normal_q, normal_t, scale_q, scale_t = state
    slots, width = p["positions"].shape
    queries = p["query_tokens"].shape[0]
    items = words[0].shape[0] // slots
    rows = queries + slots
    count = items * slots
    ins = [
        info, grad_query, grad_text, normal_q, normal_t, scale_q, scale_t, p["self_gain"],
        p["out"], packed, probs, p["positions"], p["query_tokens"], p["emb_gain"], p["qkv"], more,
        *words,
    ]
    return call(
        functools.partial(self_backward_kernel, len(words)),
        ins,
        [((count + queries + 16, 5 * width), BF), ((count, width), BF)],
        scratch=[
            pltpu.VMEM((items * rows, width), BF),
            pltpu.VMEM((items * rows, width), BF),
            pltpu.VMEM((items * rows, 3 * width), BF),
            pltpu.VMEM((items * queries, width), F32),
            pltpu.VMEM((count, width), F32),
        ],
        flops=2 * items * rows * width * width * 7,
        name="self_backward",
        after=after,
    )


def spread_rows(grads, each, first_only):
    items, emb = grads.shape
    wide = jnp.broadcast_to(grads[:, None, :], (items, each, emb))
    if first_only:
        row = lax.broadcasted_iota(jnp.int32, (items, each, emb), 1)
        wide = jnp.where(row == 0, wide, 0.0)
    return wide.reshape(items * each, emb).astype(BF)


def mid_weights_kernel(
    weights, share_rows, info, query_a, query_b, mixed_a, mixed_b, rhs_a, rhs_b, final_a, final_b,
    text_a, text_b, grad_image, grad_text, out,
):
    count, width = final_a.shape
    items = grad_image.shape[0] // 2
    each = count // items
    blocks = 1 << len(weights)
    cross_q = nn(query_a[...], rhs_a[:, :width]) + nn(query_b[...], rhs_b[:, :width])
    cross_out = nn(mixed_a[...], rhs_a[:, width:]) + nn(mixed_b[...], rhs_b[:, width:])
    select = choose_rows(info, SHARE, weights, share_rows, width // blocks, width)
    image, text = grad_image[...].astype(F32), grad_text[...].astype(F32)
    proj_i = proj_t = None
    for k, (final, first) in enumerate(((final_a, text_a), (final_b, text_b))):
        at = slice(k * items, (k + 1) * items)
        part_i = nn(nt(select, final[...]).astype(BF), spread_rows(image[at], each, False))
        part_t = nn(nt(select, first[...]).astype(BF), spread_rows(text[at], each, True))
        proj_i = part_i if proj_i is None else proj_i + part_i
        proj_t = part_t if proj_t is None else proj_t + part_t
    top = jnp.concatenate([cross_q, proj_i], axis=1)
    low = jnp.concatenate([cross_out, proj_t], axis=1)
    for b in range(blocks):
        rows = slice(b * share_rows, (b + 1) * share_rows)
        out[b] = jnp.concatenate([top[rows], low[rows]], axis=0).astype(BF)


def mid_weights(
    info, query, mixed, rhs, final, text, grad_image, grad_text, weights, share_rows, after
):
    width = final[0].shape[1]
    emb = grad_image.shape[1]
    blocks = 1 << len(weights)
    out = ((blocks, 2 * share_rows, width + emb), BF)
    at = query[0].shape[1] - final[0].shape[0]
    lhs_spec = pl.BlockSpec(
        (query[0].shape[0], final[0].shape[0]), lambda *_: (0, at // final[0].shape[0])
    )
    return call(
        functools.partial(mid_weights_kernel, weights, share_rows),
        [info, *query, *mixed, *rhs, *final, *text, grad_image, grad_text],
        [out],
        grid=(1,),
        in_specs=[None, lhs_spec, lhs_spec] + [None] * 10,
        flops=4 * query[0].shape[0] * final[0].shape[0] * 4 * width,
        name="mid_weights",
        after=after,
        weight=10**11,
    )[0]


def last_weights_kernel(
    weights, share_rows, info, chosen_q, lhs_a, lhs_b, rhs_a, rhs_b, mid, keep, give
):
    width = rhs_a.shape[1] // 5
    blocks = 1 << len(weights)
    queries = chosen_q.shape[1]
    count = rhs_a.shape[0] - queries - 16
    select = choose_rows(info, SHARE, weights, share_rows, width // blocks, width)
    summed_q = (
        rhs_a[count : count + queries, : 3 * width].astype(F32)
        + rhs_b[count : count + queries, : 3 * width].astype(F32)
    ).astype(BF)
    qkv = nn(chosen_q[...], summed_q)
    out_grad = vector_grad = None
    for lhs, rhs in ((lhs_a, rhs_a), (lhs_b, rhs_b)):
        qkv = qkv + nn(lhs[:, :count], rhs[:count, : 3 * width])
        part = nn(lhs[:, count : 2 * count], rhs[:count, 3 * width : 4 * width])
        part = part + nn(lhs[:, 2 * count : 3 * count], rhs[:count, 4 * width :])
        out_grad = part if out_grad is None else out_grad + part
        rows = jnp.concatenate(
            [
                rhs[count : count + queries, 3 * width : 4 * width],
                rhs[count : count + queries, 4 * width :],
                rhs[count + queries :, :width],
                jnp.zeros((128 - 2 * queries - 16, width), BF),
            ],
            axis=0,
        )
        part = nt(select, rows)
        vector_grad = part if vector_grad is None else vector_grad + part
    split = 2 * width
    top = jnp.concatenate([qkv[:, :split], vector_grad], axis=1)
    low = jnp.concatenate([qkv[:, split:], out_grad, jnp.zeros_like(vector_grad)], axis=1)
    base = mid.shape[2]
    for b in range(blocks):
        out, at = (keep, b) if b < blocks // 2 else (give, b - blocks // 2)
        rows = slice(b * share_rows, (b + 1) * share_rows)
        out[at, :, :base] = mid[b]
        out[at, :, base:] = jnp.concatenate([top[rows], low[rows]], axis=0).astype(BF)


def last_weights(info, chosen_q, lhs, rhs, mid, weights, share_rows, after):
    width = rhs[0].shape[1] // 5
    blocks = 1 << len(weights)
    out = ((blocks // 2, 2 * share_rows, mid.shape[2] + 2 * width + 128), BF)
    return call(
        functools.partial(last_weights_kernel, weights, share_rows),
        [info, chosen_q, *lhs, *rhs, mid],
        [out, out],
        flops=4 * chosen_q.shape[0] * 256 * 6 * width,
        name="last_weights",
        after=after,
    )


def ff_assemble_kernel(pieces, share_rows, info, places, *rest):
    parts = rest[:pieces]
    outs = rest[pieces:]
    width = parts[0].shape[1]
    deep = 4 * share_rows
    for k, piece in enumerate(parts):
        for f in range(2):
            up, down = outs[2 * f : 2 * f + 2]
            base = f * 2 * deep
            grad = piece[base : base + deep].astype(F32)
            at = pl.ds(pl.multiple_of(places[k] * share_rows, 8), share_rows)
            for c in range(4):
                up[at, c * width : (c + 1) * width] = grad[c * share_rows : (c + 1) * share_rows]
            at = pl.ds(pl.multiple_of(places[k] * deep, 8), deep)
            down[at, :] = piece[base + deep : base + 2 * deep].astype(F32)


def ff_assemble(info, places, parts, share_rows):
    width = parts[0].shape[1]
    rows = share_rows * len(parts)
    shapes = [((rows, 4 * width), F32), ((4 * rows, width), F32)] * 2
    return call(
        functools.partial(ff_assemble_kernel, len(parts), share_rows),
        [info, places, *parts],
        shapes,
        in_specs=[SCALARS, SCALARS] + [None] * len(parts),
        name="ff_assemble",
    )


def tail_assemble_kernel(pieces, share_rows, queries, info, places, *rest):
    parts = rest[:pieces]
    qkv, out, cross_q, cross_out, image, text, tokens, slots, vectors, spread = rest[pieces:]
    width = out.shape[1]
    emb = image.shape[1]
    spread[...] = jnp.zeros_like(spread)
    for k, piece in enumerate(parts):
        at = pl.ds(pl.multiple_of(places[k] * share_rows, 8), share_rows)
        grad = piece[...].astype(F32)
        top, low = grad[:share_rows], grad[share_rows:]
        cross_q[at, :] = top[:, :width]
        image[at, :] = top[:, width : width + emb]
        cross_out[at, :] = low[:, :width]
        text[at, :] = low[:, width : width + emb]
        base = width + emb
        qkv[at, : 2 * width] = top[:, base : base + 2 * width]
        spread[at, :] = top[:, base + 2 * width :]
        qkv[at, 2 * width :] = low[:, base : base + width]
        out[at, :] = low[:, base + width : base + 2 * width]
    flipped = spread[...].T
    rows = out.shape[0]
    tokens[...] = flipped[:queries, :rows]
    slots[...] = flipped[queries : 2 * queries, :rows]
    vectors[...] = flipped[2 * queries : 2 * queries + 16, :rows]


def tail_assemble(info, places, parts, share_rows, width, emb, queries):
    rows = share_rows * len(parts)
    shapes = [
        ((rows, 3 * width), F32),
        ((rows, width), F32),
        ((rows, width), F32),
        ((rows, width), F32),
        ((rows, emb), F32),
        ((rows, emb), F32),
        ((queries, rows), F32),
        ((queries, rows), F32),
        ((16, rows), F32),
    ]
    return call(
        functools.partial(tail_assemble_kernel, len(parts), share_rows, queries),
        [info, places, *parts],
        shapes,
        in_specs=[SCALARS, SCALARS] + [None] * len(parts),
        scratch=[pltpu.VMEM((128, 128), F32)],
        name="tail_assemble",
    )


def kv_assemble_kernel(count, weights, cuts, info, *rest):
    parts = rest[:count]
    key, value, blocks = rest[count:]
    at = 0
    for piece in parts:
        for b in range(piece.shape[0]):
            blocks[info[DP] ^ relative_of(at, weights)] = piece[b].astype(F32)
            at += 1
    height, span = blocks.shape[1:]
    width = key.shape[1]
    for a in range(cuts[0]):
        for b in range(cuts[1]):
            out = key if b * span < width else value
            base = b * span % width
            out[a * height : (a + 1) * height, base : base + span] = blocks[a * cuts[1] + b]


def kv_assemble(info, parts, weights, cuts, width):
    height, span = parts[0].shape[1:]
    shape = ((height * cuts[0], width), F32)
    return call(
        functools.partial(kv_assemble_kernel, len(parts), weights, cuts),
        [info, *parts],
        [shape, shape],
        scratch=[pltpu.VMEM((cuts[0] * cuts[1], height, span), F32)],
        name="kv_assemble",
    )


def features_assemble_kernel(info, mine, theirs, out):
    @pl.when(pl.program_id(0) == info[CORE])
    def _():
        out[...] = mine[...]

    @pl.when(pl.program_id(0) != info[CORE])
    def _():
        out[...] = theirs[...].astype(F32)


def features_assemble(info, mine, theirs):
    items, rows, deep = mine.shape
    return call(
        features_assemble_kernel,
        [info, mine, theirs],
        [((CORES * items, rows, deep), F32)],
        grid=(CORES,),
        out_specs=[pl.BlockSpec((items, rows, deep), lambda k: (k, 0, 0))],
        name="features_assemble",
    )[0]


def hidden_assemble_kernel(info, query_a, text_a, query_b, text_b, out):
    items = out.shape[0]
    queries = query_a.shape[0] // items
    mine = pl.program_id(0) == info[CORE]

    def put(query, text):
        out[:, :queries] = query[...].reshape(items, queries, -1)
        out[:, queries:] = text[...].reshape(items, -1, out.shape[2])

    @pl.when(mine)
    def _():
        put(query_a, text_a)

    @pl.when(jnp.logical_not(mine))
    def _():
        put(query_b, text_b)


def hidden_assemble(info, query_a, text_a, query_b, text_b, items):
    width = query_a.shape[1]
    rows = (query_a.shape[0] + text_a.shape[0]) // items
    return call(
        hidden_assemble_kernel,
        [info, query_a, text_a, query_b, text_b],
        [((CORES * items, rows, width), BF)],
        grid=(CORES,),
        out_specs=[pl.BlockSpec((items, rows, width), lambda k: (k, 0, 0))],
        name="hidden_assemble",
    )[0]


def slots_kernel(
    table_rows, patch_size, info, tokens, slot_of, rows_of, most
):
    groups, count = tokens.shape
    here_from = info[MEMBER] * table_rows
    all_rows = tokens[...]
    flipped = all_rows.T
    place = lax.broadcasted_iota(jnp.int32, (groups, count), 1)
    step = math.gcd(count, 64)
    down = lax.broadcasted_iota(jnp.int32, (step, count), 0)

    def over_slabs(d, make, combine):
        total = None
        for r in range(0, count, step):
            part = make(d, r)
            total = part if total is None else combine(total, part)
        return total

    def first_of(d, r):
        same = flipped[r : r + step, d : d + 1] == all_rows[d : d + 1]
        return jnp.min(jnp.where(same, down + r, count), axis=0, keepdims=True)

    first = jnp.concatenate(
        [over_slabs(d, first_of, jnp.minimum) for d in range(groups)], axis=0
    )
    here = (all_rows >= here_from) & (all_rows < here_from + table_rows)
    lead = first == place
    leads = jnp.where(lead & here, 1, 0).T

    def ahead_of(d, r):
        ahead = jnp.where(down + r < first[d : d + 1], leads[r : r + step, d : d + 1], 0)
        return jnp.sum(ahead, axis=0, keepdims=True)

    slot = jnp.concatenate([over_slabs(d, ahead_of, jnp.add) for d in range(groups)], axis=0)
    slot = jnp.where(here, slot, -1)
    slot_of[...] = slot
    slot_down = slot.T
    slot_iota = lax.broadcasted_iota(jnp.int32, (step, SLOTS), 1)

    def row_of(d, r):
        hit = slot_down[r : r + step, d : d + 1] == slot_iota
        local = flipped[r : r + step, d : d + 1] - here_from
        return jnp.max(jnp.where(hit, local, -1), axis=0, keepdims=True)

    for d in range(groups):
        rows_of[:, d * SLOTS : (d + 1) * SLOTS] = over_slabs(d, row_of, jnp.maximum)
    top = jnp.zeros((1, 1), jnp.int32)
    for q in range(patch_size):
        within = lead & (all_rows >= q * table_rows) & (all_rows < (q + 1) * table_rows)
        each = jnp.sum(jnp.where(within, 1, 0), axis=1, keepdims=True)
        top = jnp.maximum(top, jnp.max(each, axis=0, keepdims=True))
    most[...] = top


def slots_of(info, tokens, table_rows, patch_size, after):
    groups, count = tokens.shape
    return call(
        functools.partial(slots_kernel, table_rows, patch_size),
        [info, tokens],
        [
            ((groups, count), jnp.int32),
            ((1, groups * SLOTS), jnp.int32),
            ((1, 1), jnp.int32),
        ],
        flops=groups * count * count * 8,
        name="slots",
        after=after,
        weight=10**11,
    )


def collect_kernel(info, slot_of, mine, theirs, out):
    count = mine.shape[0]
    slot = lax.broadcasted_iota(jnp.int32, (SLOTS, count), 0)
    total = None
    for rows, core in ((mine, info[CORE]), (theirs, 1 - info[CORE])):
        at = pl.ds(pl.multiple_of(core * count, 128), count)
        hot = jnp.where(slot_of[pl.ds(info[DP], 1), at] == slot, 1.0, 0.0).astype(BF)
        part = nn(hot, rows[...])
        total = part if total is None else total + part
    out[...] = total.astype(BF)


def collect(info, slot_of, mine, theirs, after):
    return call(
        collect_kernel,
        [info, slot_of, mine, theirs],
        [((SLOTS, mine.shape[1]), BF)],
        flops=4 * SLOTS * mine.size,
        name="collect",
        after=after,
    )[0]


def table_kernel(z_size, y_size, info, rows_of, own, *rest):
    rising, falling = rest[: z_size - 1], rest[z_size - 1 : 2 * (z_size - 1)]
    out, ordered = rest[2 * (z_size - 1) :]
    chunk = out.shape[0]

    @pl.when(pl.program_id(0) == 0)
    def _():
        z, y = info[DP] // y_size, info[DP] % y_size

        def put(piece, at_z):
            for j in range(y_size):
                at = pl.multiple_of((at_z * y_size + (y ^ j)) * SLOTS, SLOTS)
                ordered[pl.ds(at, SLOTS), :] = piece[j * SLOTS : (j + 1) * SLOTS]

        put(own, z)
        for k in range(1, z_size):

            @pl.when(z - k >= 0)
            def _():
                put(rising[k - 1], z - k)

            @pl.when(z + k < z_size)
            def _():
                put(falling[k - 1], z + k)

    row = lax.broadcasted_iota(jnp.int32, (chunk, rows_of.shape[1]), 0)
    row = row + pl.program_id(0) * chunk
    hot = jnp.where(row == rows_of[...], 1.0, 0.0).astype(BF)
    out[...] = nn(hot, ordered[...])


def table_back(info, rows_of, own, rising, falling, z_size, y_size, table_rows, chunk=640):
    width = own.shape[1]
    count = rows_of.shape[1]
    return call(
        functools.partial(table_kernel, z_size, y_size),
        [info, rows_of, own, *rising, *falling],
        [((table_rows, width), F32)],
        grid=(table_rows // chunk,),
        out_specs=[pl.BlockSpec((chunk, width), lambda k: (k, 0))],
        scratch=[pltpu.VMEM((count, width), BF)],
        flops=2 * table_rows * count * width,
        name="table",
    )[0]


def stage_kernel(info, *refs):
    half = len(refs) // 2
    for given, out in zip(refs[:half], refs[half:]):
        out[...] = given[...]


def stage(info, values, after):
    return call(
        stage_kernel, [info, *values], [(v.shape, v.dtype) for v in values], name="stage",
        after=after,
    )


def swap_core(values):
    return lax.ppermute(values, "core", [(0, 1), (1, 0)])


def from_x(values, size, step):
    return lax.ppermute(values, "x", [(s, (s - step) % size) for s in range(size)])


def part(values, index, size, axis):
    return lax.dynamic_slice_in_dim(values, index * size, size, axis)


def exchange(values, axis, size, bit):
    return lax.ppermute(values, axis, [(s, s ^ bit) for s in range(size)])


def gather_doubling(values, axis, size):
    place = lax.axis_index(axis)
    bit = 1
    while bit < size:
        other = exchange(values, axis, size, bit)
        low = (place & bit) == 0
        values = jnp.concatenate(
            [jnp.where(low, values, other), jnp.where(low, other, values)], axis=0
        )
        bit *= 2
    return values


def gather_relative(values, axis, size):
    bit = 1
    while bit < size:
        values = jnp.concatenate([values, exchange(values, axis, size, bit)], axis=0)
        bit *= 2
    return values


def pass_on(values, axis, size):
    up = [(s, s + 1) for s in range(size - 1)]
    down = [(s + 1, s) for s in range(size - 1)]
    rising, falling = [values], [values]
    for _ in range(1, size):
        rising.append(lax.ppermute(rising[-1], axis, up))
        falling.append(lax.ppermute(falling[-1], axis, down))
    return rising[1:], falling[1:]


def gather_patch(values, x_size):
    own = [values] + [from_x(values, x_size, k) for k in range(1, x_size)]
    return own + [swap_core(v) for v in own]


def patch_places(x_size):
    xi, ci = lax.axis_index("x"), lax.axis_index("core")
    columns = [(xi + k) % x_size for k in range(x_size)]
    return jnp.stack([x * CORES + ci for x in columns] + [x * CORES + 1 - ci for x in columns])


def halving_steps(z_size, y_size, order):
    y_steps = [("y", y_size, 1 << k) for k in range(y_size.bit_length() - 1)]
    z_steps = [("z", z_size, 1 << k) for k in range(z_size.bit_length() - 1)]
    return y_steps + z_steps if order == "y" else z_steps + y_steps


def add_low(a, b):
    return (a.astype(F32) + b.astype(F32)).astype(BF)


def halve_kernel(info, keep, got, stays, goes):
    half = stays.shape[0]
    for b in range(keep.shape[0]):
        total = keep[b].astype(F32) + got[b].astype(F32)
        if b < half:
            stays[b] = total.astype(BF)
        else:
            goes[b - half] = total.astype(BF)


def halve(info, keep, got, after):
    shape = ((keep.shape[0] // 2,) + keep.shape[1:], BF)
    return call(halve_kernel, [info, keep, got], [shape, shape], name="halve", after=after)


def add_kernel(info, a, b, out):
    for k in range(out.shape[0]):
        out[k] = (a[k].astype(F32) + b[k].astype(F32)).astype(BF)


def add(info, a, b, after):
    return call(add_kernel, [info, a, b], [(a.shape, BF)], name="add", after=after)[0]


def reduce_scatter(info, keep, give, z_size, y_size, order, gates=None, steps=None):
    steps = steps or halving_steps(z_size, y_size, order)
    later = []
    for k, step in enumerate(steps):
        got = exchange(give, *step)
        if k < len(steps) - 1:
            keep, give = halve(info, keep, got, gates[k] if gates else ())
            later.append(give)
    return add_low(keep, got)[0], later


def gather_blocks(block, z_size, y_size, order):
    pieces = [block[None]]
    for step in halving_steps(z_size, y_size, order)[::-1]:
        whole_piece = pieces[0] if len(pieces) == 1 else jnp.concatenate(pieces, axis=0)
        pieces = [whole_piece, exchange(whole_piece, *step)]
    return pieces


def all_reduce(values, z_size, y_size):
    for step in halving_steps(z_size, y_size, "y"):
        values = add_low(values, exchange(values, *step))
    return values


def shards(
    z_size, y_size, x_size,
    token_ids, token_used, paired_ids, features, incoming, query_tokens, table, positions,
    emb_gain, emb_bias, qkv, out_weight, self_gain, self_bias, cross_query, key_shard,
    value_shard, cross_out, cross_gain, cross_bias, query_up, query_down, query_gain, query_bias,
    text_up, text_down, text_gain, text_bias, image_proj, text_proj, sharpness,
):
    group, slots = token_ids.shape
    queries, width = query_tokens.shape
    emb = image_proj.shape[1]
    items = group // CORES
    patch_size = x_size * CORES
    table_rows = table.shape[0]
    feat_rows = features.shape[1]
    kv_rows = key_shard.shape[0]
    dp_size = z_size * y_size
    xi, ci = lax.axis_index("x"), lax.axis_index("core")
    di = lax.axis_index("z") * y_size + lax.axis_index("y")
    member = xi * CORES + ci
    other = xi * CORES + 1 - ci
    block_rows = width // dp_size
    shared = block_rows % (8 * patch_size) == 0
    share_rows = block_rows // patch_size if shared else block_rows
    share, partner = (member, other) if shared else (jnp.int32(0), jnp.int32(0))
    info = jnp.stack([di, share, partner, ci, member, other]).astype(jnp.int32)
    places = patch_places(x_size).astype(jnp.int32)
    orders = {k: order_weights(z_size, y_size, k) for k in ("y", "z")}

    p = dict(
        emb_gain=emb_gain, emb_bias=emb_bias, self_gain=self_gain, self_bias=self_bias,
        cross_gain=cross_gain, cross_bias=cross_bias, query_gain=query_gain,
        query_bias=query_bias, text_gain=text_gain, text_bias=text_bias, positions=positions, query_tokens=query_tokens, qkv=qkv, out=out_weight,
        cross_query=cross_query, cross_out=cross_out, query_up=query_up, query_down=query_down,
        text_up=text_up, text_down=text_down, image_proj=image_proj, text_proj=text_proj,
    )

    def own_first(values):
        return jnp.concatenate(
            [part(values, ci, items, 0), part(values, 1 - ci, items, 0)], axis=0
        )

    local_ids = (own_first(token_ids) - member * table_rows).reshape(-1, 1)
    words_mine, words_give = look_up(info, local_ids, table)
    word_sum = words_mine + swap_core(words_give)
    words = [word_sum] + [from_x(word_sum, x_size, k) for k in range(1, x_size)]

    feat_mine = part(features, ci, items, 0)
    feat_got = swap_core(part(features, 1 - ci, items, 0))
    feats_x = [from_x(feat_mine, x_size, k) for k in range(1, x_size)]
    feat_late, key_late, value_late = stage(
        info, [feat_got, key_shard, value_shard], [word_sum]
    )
    feats = [feat_mine, feat_got]
    for k in range(1, x_size):
        feats += [feats_x[k - 1], from_x(feat_late, x_size, k)]
    key_x = [from_x(key_late, x_size, k) for k in range(1, x_size)]
    value_x = [from_x(value_late, x_size, k) for k in range(1, x_size)]

    used = jnp.concatenate(
        [jnp.ones((items, queries), jnp.int32), part(token_used, ci, items, 0)], axis=1
    ).reshape(items // 2, 2 * (queries + slots))
    (packed, probs, normal_q, normal_t, scale_q, scale_t, cross_q, lhs_mine, lhs_give, chosen_q) = (
        self_forward(info, words, used, p, orders, share_rows)
    )
    lhs_got = swap_core(lhs_give)
    held = list(stage(info, key_x + value_x, [packed]))
    own_keys, own_values = [key_shard] + held[: x_size - 1], [value_shard] + held[x_size - 1 :]
    kv_shards = own_keys + [swap_core(v) for v in own_keys]
    kv_shards += own_values + [swap_core(v) for v in own_values]
    text_names = ("text_up", "text_down", "text_gain", "text_bias", "text_proj")
    query_names = ("query_up", "query_down", "query_gain", "query_bias", "image_proj")
    (t_slope, t_keep, t_give, t_normal, t_scale, text_final, text_raw) = ff_forward(
        info, normal_t, p["self_gain"], p["self_bias"], text_names, p, orders["y"], share_rows,
        items, False,
    )
    t_got = swap_core(t_give)
    keys, values = key_value(info, places, feats, kv_shards, [t_normal])
    cross_probs, normal_c, scale_c, mixed_mine, mixed_give = cross_forward(
        info, cross_q, keys, values, normal_q, p, orders, share_rows
    )
    mixed_got = swap_core(mixed_give)
    (q_slope, q_keep, q_give, q_normal, q_scale, query_final, image_raw) = ff_forward(
        info, normal_c, p["cross_gain"], p["cross_bias"], query_names, p, orders["z"], share_rows,
        items, True,
    )
    q_got = swap_core(q_give)

    query_other, text_other = swap_core(query_final), swap_core(text_final)
    hidden_out = hidden_assemble(
        info, query_final, text_final, query_other, text_other, items
    )

    own_ids = jnp.concatenate(
        [part(token_ids, ci, items, 0), part(paired_ids, ci, items, 0)[:, None]], axis=1
    ).astype(F32)
    own_ids = jnp.pad(own_ids, ((0, 0), (0, 128 - own_ids.shape[1])))
    gathered = gather_doubling(
        jnp.concatenate([image_raw, text_raw, own_ids], axis=1), "core", CORES
    )
    gathered = jnp.concatenate(
        [gathered] + [exchange(gathered, "y", y_size, j) for j in range(1, y_size)], axis=0
    )
    pieces = [gathered] + [exchange(gathered, "z", z_size, k) for k in range(1, z_size)]
    loss, grad_image, grad_text, grad_sharp, ids = contrast(
        info, pieces, sharpness.reshape(1, 1), queries, slots, group, emb, y_size, [hidden_out]
    )
    all_tokens = ids[:, :slots].reshape(dp_size, group * slots)

    q_rhs, grad_second, q_vectors = ff_backward(
        info, incoming, 0, grad_image, (q_slope, q_normal, q_scale),
        ("query_up", "query_down", "query_gain", "image_proj"), p, True,
    )
    t_rhs, grad_text_rows, t_vectors = ff_backward(
        info, incoming, 1, grad_text, (t_slope, t_normal, t_scale),
        ("text_up", "text_down", "text_gain", "text_proj"), p, False,
        [q_vectors, q_got, t_got, lhs_got, mixed_got],
    )
    q_weights = ff_weights(
        info, q_keep, q_got, q_rhs, swap_core(q_rhs), share_rows, dp_size, width, [t_vectors]
    )
    t_weights = ff_weights(
        info, t_keep, t_got, t_rhs, swap_core(t_rhs), share_rows, dp_size, width, [q_weights[0]]
    )

    y_first, z_first = (halving_steps(z_size, y_size, k) for k in ("y", "z"))

    m_rhs, grad_keys, grad_values, grad_query_rows, c_vectors = cross_backward(
        info, grad_second, normal_c, scale_c, keys, values, cross_probs, cross_q, p,
        [t_weights[0]],
    )
    m_got = swap_core(m_rhs)

    more = jnp.concatenate([c_vectors, q_vectors, t_vectors], axis=0)
    l_rhs, words_low = self_backward(
        info, grad_query_rows, grad_text_rows, (normal_q, normal_t, scale_q, scale_t), packed,
        probs, words, more, p, [],
    )
    t_more = halve(info, t_weights[0], exchange(t_weights[1], *y_first[0]), [words_low])
    q_more = halve(info, q_weights[0], exchange(q_weights[1], *z_first[0]), [t_more[1]])
    (words_low,) = stage(info, [words_low], [q_more[1]])
    words_other = swap_core(words_low)
    slot_of, rows_of, most = slots_of(info, all_tokens, table_rows, patch_size, [words_low])

    own = collect(info, slot_of, words_low, words_other, [q_more[1]])
    table_start = [own]
    own = gather_relative(own, "y", y_size)
    rising, falling = pass_on(own, "z", z_size)

    def few(words_low, words_other):
        return table_back(info, rows_of, own, rising, falling, z_size, y_size, table_rows)

    def many(words_low, words_other):
        low_core = ci == 0
        group_words = jnp.concatenate(
            [
                jnp.where(low_core, words_low, words_other),
                jnp.where(low_core, words_other, words_low),
            ],
            axis=0,
        )
        own = lax.dynamic_index_in_dim(all_tokens, di, axis=0, keepdims=False)
        rows = lax.broadcasted_iota(jnp.int32, (1, table_rows), 1) + member * table_rows
        hot = (own[:, None] == rows).astype(BF)
        return all_reduce(tn(hot, group_words).astype(BF), z_size, y_size).astype(F32)

    table_grad = lax.cond(most[0, 0] <= SLOTS, few, many, words_low, words_other)

    cuts = (2, dp_size // 2) if dp_size == 8 and kv_rows % 32 == 0 else (1, 1)
    kv_keep, kv_give = kv_weights(
        info, grad_keys, grad_values, feats, orders["y"], kv_rows, cuts,
        table_start,
    )

    mid = mid_weights(
        info, (lhs_mine, lhs_got), (mixed_mine, mixed_got), (m_rhs, m_got),
        (query_final, query_other), (text_final, text_other), grad_image, grad_text, orders["y"],
        share_rows, [kv_keep],
    )
    last = last_weights(
        info, chosen_q, (lhs_mine, lhs_got), (l_rhs, swap_core(l_rhs)), mid, orders["y"],
        share_rows, [],
    )
    tail_sum, _ = reduce_scatter(
        info, *last, z_size, y_size, "y"
    )
    kv_part = add(info, kv_keep, swap_core(kv_give), [rising[0]])
    if cuts[0] > 1:
        half = dp_size // 2
        kv_block, _ = reduce_scatter(
            info, kv_part[:half], kv_part[half:], z_size, y_size, "y"
        )
        key_grad, value_grad = kv_assemble(
            info, gather_blocks(kv_block, z_size, y_size, "y"), orders["y"], cuts, width
        )
    else:
        kv_total = all_reduce(kv_part[0], z_size, y_size).astype(F32)
        key_grad, value_grad = kv_total[:, :width], kv_total[:, width:]
    feature_mine, feature_give = features_back(
        info, places, grad_keys, grad_values, kv_shards, feat_rows, [kv_keep]
    )
    features_grad = features_assemble(info, feature_mine, swap_core(feature_give))

    def spread(values):
        return gather_patch(values, x_size) if shared else [values]

    q_sum, _ = reduce_scatter(
        info, *q_more, z_size, y_size, "z", [[last[0]]] * len(z_first), z_first[1:]
    )
    t_sum, _ = reduce_scatter(
        info, *t_more, z_size, y_size, "y", [[last[0]]] * len(y_first), y_first[1:]
    )
    ff_parts = spread(jnp.concatenate([q_sum, t_sum], axis=0))
    spots = places if shared else jnp.zeros((1,), jnp.int32)
    query_up_grad, query_down_grad, text_up_grad, text_down_grad = ff_assemble(
        info, spots, ff_parts, share_rows
    )

    tail_parts = spread(tail_sum)
    (
        qkv_grad, out_grad, cross_query_grad, cross_out_grad, image_proj_grad, text_proj_grad,
        tokens_grad, position_grad, vectors,
    ) = tail_assemble(info, spots, tail_parts, share_rows, width, emb, queries)

    return (
        hidden_out, loss.reshape(-1), features_grad, tokens_grad, table_grad, position_grad,
        vectors[0], vectors[1], qkv_grad, out_grad, vectors[2], vectors[3], cross_query_grad,
        key_grad, value_grad, cross_out_grad, vectors[4], vectors[5], query_up_grad,
        query_down_grad, vectors[6], vectors[7], text_up_grad, text_down_grad, vectors[8],
        vectors[9], image_proj_grad, text_proj_grad, grad_sharp.reshape(()),
    )


def solution(mesh):
    dp_size = mesh.shape["dp"]
    y_size = 1 << ((dp_size.bit_length() - 2) // 2)
    z_size = dp_size // y_size
    x_size = mesh.shape["patch"] // CORES
    split = Mesh(
        mesh.devices.reshape(z_size, y_size, x_size, CORES), ("z", "y", "x", "core")
    )
    dp, patch = ("z", "y"), ("x", "core")
    placed = (
        [P(dp, None), P(dp, None), P(dp), P(dp, patch, None), P(dp, None, None), P()]
        + [P(patch, None)]
        + [P()] * 8
        + [P(patch, None)] * 2
        + [P()] * 14
    )
    out = (
        [P(dp, None, None), P(dp), P(dp, patch, None), P(None, dp), P(patch, None)]
        + [P(None, dp), P(dp), P(dp), P(dp, None), P(dp, None), P(dp), P(dp)]
        + [P(dp, None), P(patch, None), P(patch, None), P(dp, None), P(dp), P(dp)]
        + [P(dp, None), P(dp, None), P(dp), P(dp), P(dp, None), P(dp, None)]
        + [P(dp), P(dp), P(dp, None), P(dp, None), P()]
    )

    def body(*args):
        return shards(z_size, y_size, x_size, *args)

    return jax.shard_map(
        body, mesh=split, in_specs=tuple(placed), out_specs=tuple(out), check_vma=False
    )
```
